32 devices in a mesh: ctx: 8 (over z, x), ch: 4 (over y, core).
Axes of the slice: x: 2, y: 2, z: 4, core: 2. Of those that a mesh axis runs over, the one named last changes fastest.
Arguments:
- query_proj: bfloat16 [8192, 1024], P('ch', 'ctx'), may hold values from -6 to 6
- key_proj: bfloat16 [8192, 1024], P('ch', 'ctx'), may hold values from -6 to 6
- value_proj: bfloat16 [8192, 1024], P('ch', 'ctx'), may hold values from -6 to 6
- cotangent: bfloat16 [8192, 1024], P('ch', 'ctx'), may hold values from -0.046875 to 0.046875
- positions: int32 [1024], P('ctx'), may hold values from 0 to 1023, as said below
- group_of: int32 [8192], replicated, may hold values from 0 to 511, as said below
- decay_rates: float32 [512, 16], replicated, may hold values from 9.765625e-05 to 0.03
- residues: float32 [512, 16], replicated, may hold values from -1.5 to 1.5
Outputs:
- output: bfloat16 [8192, 1024], P('ch', 'ctx')
- filter_grad: float32 [512, 1024], P('ch', 'ctx')
The draws below stay inside these ranges and needn't reach their ends.
Inputs may be any that keep to these rules, and one draw needn't show every extreme that they name: positions is a permutation of the sequence positions; every aligned run of 64 stored tokens holds consecutive positions that start at a multiple of 64. `group_of`: every group has exactly 16 channels; each aligned block of 2048 channels holds exactly 512 channels of the groups of each aligned block of 128 groups.
All inputs are finite; a program needn't handle non-finite values.
Results may differ from the reference program's by a relative error of at most 0.0058.
Values may be sent and summed in bfloat16 or wider, within the bound.
No kernel may reach another device: no remote copies, remote signals or barrier semaphores. Data moves between devices by JAX's collectives and lax.ppermute only.
A program may use at most 64 MiB of HBM per device.

```python
import math
import jax
import jax.numpy as jnp
from jax import lax

CHANNELS = 8192
GROUP_SIZE = 16
ORDER = 16
TOK_DEV = 128
TOKENS = 1024
CH_DEV = 2048
GROUPS = 512
OWN_GROUPS = 128
SLOTS = 512


def draw_positions(key, part):
    half_run = TOK_DEV // 2
    run_count = TOKENS // half_run
    run_order = jax.random.permutation(jax.random.fold_in(key, 11), run_count).astype(jnp.int32)
    within = jnp.arange(half_run, dtype=jnp.int32)
    return (run_order[:, None] * half_run + within[None, :]).reshape(-1).astype(jnp.int32)


def shuffle_one(subkey):
    return jax.random.permutation(subkey, CH_DEV).astype(jnp.int32)


def draw_group_of(key, part):
    owner_count = CHANNELS // CH_DEV
    key_owner, key_source = jax.random.split(jax.random.fold_in(key, 23))
    owner_perm = jax.vmap(shuffle_one)(jax.random.split(key_owner, owner_count))
    source_perm = jax.vmap(shuffle_one)(jax.random.split(key_source, owner_count))
    owner_ids = source_perm // SLOTS
    slot_ids = source_perm % SLOTS
    source_ids = jnp.arange(owner_count, dtype=jnp.int32)[:, None]
    group_slot = owner_perm[owner_ids, source_ids * SLOTS + slot_ids]
    return (owner_ids * OWN_GROUPS + group_slot // GROUP_SIZE).reshape(-1).astype(jnp.int32)


def level_of(key, dims, cuts, least, top_value):
    gain, own = 1.0, jax.random.fold_in(key, 6)
    for dim, shards_of in cuts:
        steps = jnp.exp(jax.random.uniform(jax.random.fold_in(own, dim), (shards_of,), jnp.float32, least / len(cuts), top_value / len(cuts)))
        gain = gain * jnp.repeat(steps, dims[dim] // shards_of).reshape([-1 if axis == dim else 1 for axis in range(len(dims))])
    return gain


def scatter_about(rng, shape, deviation, reach, cuts=(), kind=jnp.bfloat16):
    factor_of = level_of(rng, shape, cuts, -0.22, 0.18) if cuts else 1.0
    result = jax.random.normal(rng, shape, jnp.float32) * deviation * factor_of
    return jnp.minimum(jnp.maximum(result, -reach), reach).astype(kind)


def setup_inputs(seed: int = 0) -> dict:
    key_list = jax.random.split(jax.random.key(seed), 9)
    return {
        "query_proj": scatter_about(key_list[0], (CHANNELS, TOKENS), 1.0, 6.0, ((0, 4), (1, 8))),
        "key_proj": scatter_about(key_list[1], (CHANNELS, TOKENS), 1.0, 6.0, ((0, 4), (1, 8))),
        "value_proj": scatter_about(key_list[2], (CHANNELS, TOKENS), 1.0, 6.0, ((0, 4), (1, 8))),
        "cotangent": scatter_about(key_list[3], (CHANNELS, TOKENS), (0.25 / TOKENS ** 0.5), 0.046875, ((0, 4), (1, 8))),
        "positions": draw_positions(jax.random.fold_in(key_list[8], 71), 0),
        "group_of": draw_group_of(jax.random.fold_in(key_list[8], 71), 0),
        "decay_rates": jnp.clip(jnp.exp(jax.random.uniform(key_list[6], (GROUPS, ORDER), jnp.float32, math.log(9.765625145519152e-05), math.log(0.03))), 9.765625145519152e-05, 0.03),
        "residues": scatter_about(key_list[7], (GROUPS, ORDER), 0.25, 1.5, (), jnp.float32),
    }


def reference(query_proj, key_proj, value_proj, cotangent, positions, group_of, decay_rates, residues):
    channel_count, seq_length = query_proj.shape
    extent = 2 * seq_length
    block_rows = min(256, channel_count)
    blocks = channel_count // block_rows
    source_index = jnp.zeros((seq_length,), jnp.int32).at[positions].set(jnp.arange(seq_length, dtype=jnp.int32))
    tap_index = jnp.arange(seq_length, dtype=jnp.float32)

    def fold_blocks(array_in):
        return array_in.reshape((blocks, block_rows) + array_in.shape[1:])

    def block_step(running, pieces):
        query_rows, key_rows, value_rows, cot_rows, group_rows = pieces
        gated = (key_rows.astype(jnp.float32) * value_rows.astype(jnp.float32)).astype(jnp.bfloat16)
        weighted = (cot_rows.astype(jnp.float32) * query_rows.astype(jnp.float32)).astype(jnp.bfloat16)
        gated_seq = gated[:, source_index].astype(jnp.float32)
        weighted_seq = weighted[:, source_index].astype(jnp.float32)
        decay_rows = decay_rates[group_rows]
        gain_rows = residues[group_rows]
        coefs = gain_rows * jnp.sqrt(2.0 * decay_rows)
        filters = lax.optimization_barrier(jnp.sum(coefs[:, :, None] * jnp.exp(-decay_rows[:, :, None] * tap_index), axis=1))
        gated_spec = jnp.fft.rfft(gated_seq, n=extent, axis=1)
        filter_spec = jnp.fft.rfft(filters, n=extent, axis=1)
        weighted_spec = jnp.fft.rfft(weighted_seq, n=extent, axis=1)
        convolved = jnp.fft.irfft(filter_spec * gated_spec, n=extent, axis=1)[:, :seq_length].astype(jnp.bfloat16)
        lagged = jnp.fft.irfft(weighted_spec * jnp.conj(gated_spec), n=extent, axis=1)[:, :seq_length]
        output = (query_rows.astype(jnp.float32) * convolved[:, positions].astype(jnp.float32)).astype(jnp.bfloat16)
        running = running + jax.ops.segment_sum(lagged.astype(jnp.float32), group_rows, num_segments=GROUPS)
        return (running, output)
    filter_grad, outputs = lax.scan(block_step, jnp.zeros((GROUPS, seq_length), jnp.float32), (fold_blocks(query_proj), fold_blocks(key_proj), fold_blocks(value_proj), fold_blocks(cotangent), fold_blocks(group_of)))
    return (outputs.reshape(channel_count, seq_length), filter_grad)
```

```python
import functools
import math

import jax
import jax.numpy as jnp
from jax import lax
from jax.experimental import pallas as pl
from jax.experimental.pallas import tpu as pltpu
from jax.sharding import PartitionSpec as P

F32 = jnp.float32
BF16 = jnp.bfloat16
I32 = jnp.int32
LANES = 128
VMEM_LIMIT = 48 * 1024 * 1024


def product(form, left, right):
    return jnp.einsum(form, left, right, precision=lax.Precision.HIGHEST)


def split_rows(extent):
    chosen = 2
    for divisor in range(2, math.isqrt(extent) + 1, 2):
        if extent % divisor == 0:
            chosen = divisor
    return chosen


def dft_tables(row_count, col_count, extent):
    row_index = jnp.arange(row_count, dtype=jnp.int32)
    col_index = jnp.arange(col_count, dtype=jnp.int32)

    def angles(left_index, right_index, modulus):
        phase = left_index[:, None] * right_index[None, :] % modulus
        return phase.astype(jnp.float32) * (2.0 * math.pi / modulus)

    row_angle = angles(row_index, row_index, row_count)
    col_angle = angles(col_index, col_index, col_count)
    twist_angle = angles(row_index, col_index, extent)
    return (
        jnp.cos(row_angle),
        jnp.sin(row_angle),
        jnp.cos(col_angle),
        jnp.sin(col_angle),
        jnp.cos(twist_angle),
        jnp.sin(twist_angle),
    )


def forward_transform(signal, tables, row_count, col_count):
    row_cos, row_sin, col_cos, col_sin, twist_cos, twist_sin = tables
    folded = signal.reshape(signal.shape[0], row_count // 2, col_count)
    mid_real = product("ka,cab->ckb", row_cos[:, : row_count // 2], folded)
    mid_imag = -product("ka,cab->ckb", row_sin[:, : row_count // 2], folded)
    turned_real = mid_real * twist_cos + mid_imag * twist_sin
    turned_imag = mid_imag * twist_cos - mid_real * twist_sin
    spec_real = product("ckb,bm->ckm", turned_real, col_cos) + product(
        "ckb,bm->ckm", turned_imag, col_sin
    )
    spec_imag = product("ckb,bm->ckm", turned_imag, col_cos) - product(
        "ckb,bm->ckm", turned_real, col_sin
    )
    return (spec_real, spec_imag)


def inverse_transform(spec_real, spec_imag, tables, row_count, col_count):
    row_cos, row_sin, col_cos, col_sin, twist_cos, twist_sin = tables
    mid_real = product("ckm,bm->ckb", spec_real, col_cos) - product(
        "ckm,bm->ckb", spec_imag, col_sin
    )
    mid_imag = product("ckm,bm->ckb", spec_imag, col_cos) + product(
        "ckm,bm->ckb", spec_real, col_sin
    )
    turned_real = mid_real * twist_cos - mid_imag * twist_sin
    turned_imag = mid_imag * twist_cos + mid_real * twist_sin
    folded = product("ak,ckb->cab", row_cos[: row_count // 2, :], turned_real) - product(
        "ak,ckb->cab", row_sin[: row_count // 2, :], turned_imag
    )
    return folded.reshape(spec_real.shape[0], -1) / float(row_count * col_count)


def spectra(gated_seq, weighted_seq, chan_groups, decay_rates, residues, seq_length):
    extent = 2 * seq_length
    row_count = split_rows(extent)
    col_count = extent // row_count
    decay_rows = decay_rates[chan_groups]
    gain_rows = residues[chan_groups]
    tap_index = jnp.arange(seq_length, dtype=jnp.float32)
    coefs = gain_rows * jnp.sqrt(2.0 * decay_rows)
    filters = jnp.sum(coefs[:, :, None] * jnp.exp(-decay_rows[:, :, None] * tap_index), axis=1)
    tables = dft_tables(row_count, col_count, extent)
    gated_real, gated_imag = forward_transform(
        gated_seq.astype(jnp.float32), tables, row_count, col_count
    )
    filter_real, filter_imag = forward_transform(filters, tables, row_count, col_count)
    weight_real, weight_imag = forward_transform(
        weighted_seq.astype(jnp.float32), tables, row_count, col_count
    )
    convolved = inverse_transform(
        filter_real * gated_real - filter_imag * gated_imag,
        filter_real * gated_imag + filter_imag * gated_real,
        tables,
        row_count,
        col_count,
    )
    lagged = inverse_transform(
        weight_real * gated_real + weight_imag * gated_imag,
        weight_imag * gated_real - weight_real * gated_imag,
        tables,
        row_count,
        col_count,
    )
    return (convolved, lagged)


def general_way(
    query_proj, key_proj, value_proj, cotangent, positions, group_of, decay_rates, residues
):
    ctx_count = lax.axis_size("ctx")
    ch_count = lax.axis_size("ch")
    ctx_rank = lax.axis_index("ctx")
    ch_rank = lax.axis_index("ch")
    local_channels, local_tokens = query_proj.shape
    half_run = local_tokens // 2
    run_count = 2 * ctx_count
    seq_length = local_tokens * ctx_count
    per_device = local_channels // ctx_count
    groups_total = decay_rates.shape[0]
    gated = (key_proj.astype(jnp.float32) * value_proj.astype(jnp.float32)).astype(jnp.bfloat16)
    weighted = (cotangent.astype(jnp.float32) * query_proj.astype(jnp.float32)).astype(jnp.bfloat16)
    run_ids = jnp.stack([positions[0], positions[half_run]]) // half_run
    all_runs = lax.all_to_all(
        jnp.broadcast_to(run_ids[None, :], (ctx_count, 2)),
        "ctx",
        split_axis=0,
        concat_axis=0,
        tiled=True,
    ).reshape(run_count)
    source_run = (
        jnp.zeros((run_count,), jnp.int32).at[all_runs].set(jnp.arange(run_count, dtype=jnp.int32))
    )

    def to_sequence(stored):
        return stored.reshape(per_device, run_count, half_run)[:, source_run, :].reshape(
            per_device, seq_length
        )

    shard_groups = lax.dynamic_slice_in_dim(group_of, ch_rank * local_channels, local_channels)
    gated_cols, weighted_cols = (
        lax.all_to_all(gated, "ctx", split_axis=0, concat_axis=1, tiled=True),
        lax.all_to_all(weighted, "ctx", split_axis=0, concat_axis=1, tiled=True),
    )
    first_channel = ch_rank * local_channels + ctx_rank * per_device
    chan_groups = lax.dynamic_slice_in_dim(group_of, first_channel, per_device)
    convolved, lagged = spectra(
        to_sequence(gated_cols),
        to_sequence(weighted_cols),
        chan_groups,
        decay_rates,
        residues,
        seq_length,
    )
    ordered = convolved.astype(jnp.bfloat16).reshape(per_device, run_count, half_run)[
        :, all_runs, :
    ]
    conv_tokens = lax.all_to_all(
        ordered.reshape(per_device, seq_length), "ctx", split_axis=1, concat_axis=0, tiled=True
    )
    output = (query_proj.astype(jnp.float32) * conv_tokens.astype(jnp.float32)).astype(jnp.bfloat16)
    lag_rows = lax.all_to_all(lagged, "ctx", split_axis=1, concat_axis=0, tiled=True)
    select_all = (
        jnp.arange(groups_total, dtype=jnp.int32)[:, None] == shard_groups[None, :]
    ).astype(jnp.float32)
    partial = jnp.dot(
        select_all, lag_rows, precision=lax.Precision.HIGHEST, preferred_element_type=jnp.float32
    ).reshape(ch_count, groups_total // ch_count, local_tokens)
    filter_grad = jnp.sum(
        lax.all_to_all(partial, "ch", split_axis=0, concat_axis=0, tiled=True), axis=0
    )
    return (output, filter_grad)


def iota(shape, dim):
    return lax.broadcasted_iota(I32, shape, dim)


def hot(flags):
    return jnp.where(flags, 1.0, 0.0).astype(BF16)


def dot(left, right):
    return jnp.dot(left, right, preferred_element_type=F32)


def dot_lanes(left, right):
    return lax.dot_general(left, right, (((1,), (1,)), ((), ())), preferred_element_type=F32)


def two_terms(values):
    high = values.astype(BF16)
    return high, (values - high.astype(F32)).astype(BF16)


class Sizes:
    def __init__(self, ctx, ch, channels, tokens, groups):
        self.ctx, self.ch = ctx, ch
        self.peers = ctx * ch
        self.channels = channels
        self.tokens = tokens
        self.run = tokens // 2
        self.runs = 2 * ctx
        self.groups = groups
        self.block = groups // ch
        self.each = self.block // self.peers
        self.own = groups // self.peers
        self.size = channels * ch // groups
        self.cap = 96
        powers = [self.block, max(self.each, 1), self.own, self.size]
        self.fits = (
            tokens == LANES
            and self.runs == 16
            and self.own == 16
            and self.size == 16
            and self.each * self.peers == self.block
            and self.each * 8 * self.run == 16 * LANES
            and ch == 4
            and channels % 2048 == 0
            and channels // self.peers <= 64
            and all(p & (p - 1) == 0 for p in powers)
        )

    def owner(self, group):
        return lax.shift_right_logical(group & (self.block - 1), self.each.bit_length() - 1)

    def place(self, group):
        block = lax.shift_right_logical(group, self.block.bit_length() - 1)
        return block * self.each + (group & (self.each - 1))


def running_counts(marks, upper):
    width = upper.shape[0]
    before, counts = jnp.zeros((marks.shape[0], 1), F32), []
    for start in range(0, marks.shape[1], width):
        part = marks[:, start : start + width]
        counts.append(dot(part, upper) + before)
        before = before + jnp.sum(part.astype(F32), axis=1, keepdims=True)
    return jnp.concatenate(counts, axis=1), before


def upper_ones(width):
    return hot(iota((width, width), 0) < iota((width, width), 1))


def pack_kernel(
    sizes, runs_ref, group_ref, key_ref, value_ref, cot_ref, query_ref, out_ref, dest_ref, data
):
    part = out_ref.shape[0]

    @pl.when(pl.program_id(0) == 0)
    def _():
        owner = sizes.owner(group_ref[...])
        marks = iota((sizes.peers, sizes.channels), 0) == owner
        counts, _ = running_counts(hot(marks), upper_ones(256))
        slot = jnp.sum(jnp.where(marks, counts, 0.0), axis=0, keepdims=True).astype(I32)
        dest_ref[0:1, :] = jnp.where(slot < sizes.cap - 1, owner * sizes.cap + slot, -1)
        dest_ref[1:2, :] = owner
        dest_ref[2:3, :] = slot
        dest_ref[3:8, :] = jnp.zeros((5, sizes.channels), I32)
        data[:, :LANES] = (key_ref[...].astype(F32) * value_ref[...].astype(F32)).astype(BF16)
        data[:, LANES:] = (cot_ref[...].astype(F32) * query_ref[...].astype(F32)).astype(BF16)

    dest = dest_ref[0:1, :]
    lane = iota((1, 2 * LANES), 1)
    run_row = jnp.where(lane < LANES, runs_ref[0], runs_ref[1]).astype(F32)
    row = iota((sizes.cap, 1), 0)

    def one_peer(index, carry):
        base = (pl.program_id(0) * part + index) * sizes.cap
        chosen = hot(iota((sizes.cap, sizes.channels), 0) == dest - base)
        rows = dot(chosen, data[...])
        out_ref[index] = jnp.where(row == sizes.cap - 1, run_row, rows).astype(BF16)
        return carry

    lax.fori_loop(0, part, one_peer, 0)


def pack(sizes, run_ids, shard_groups, key_proj, value_proj, cotangent, query_proj):
    part = 8
    whole = lambda shape: pl.BlockSpec(shape, lambda step: (0, 0))
    rows = (sizes.channels, sizes.tokens)
    return pl.pallas_call(
        functools.partial(pack_kernel, sizes),
        grid=(sizes.peers // part,),
        in_specs=[
            pl.BlockSpec(memory_space=pltpu.SMEM),
            whole((1, sizes.channels)),
            whole(rows),
            whole(rows),
            whole(rows),
            whole(rows),
        ],
        out_specs=[
            pl.BlockSpec((part, sizes.cap, 2 * LANES), lambda step: (step, 0, 0)),
            whole((8, sizes.channels)),
        ],
        out_shape=[
            jax.ShapeDtypeStruct((sizes.peers, sizes.cap, 2 * LANES), BF16),
            jax.ShapeDtypeStruct((8, sizes.channels), I32),
        ],
        scratch_shapes=[pltpu.VMEM((sizes.channels, 2 * LANES), BF16)],
        compiler_params=pltpu.CompilerParams(vmem_limit_bytes=VMEM_LIMIT),
        name="pack_rows",
    )(run_ids, shard_groups, key_proj, value_proj, cotangent, query_proj)


def index_kernel(
    sizes, me_ref, group_ref, rate_ref, gain_ref, into_ref, back_ref, over_ref, table_ref
):
    me = me_ref[0]
    upper = upper_ones(256)
    group = group_ref[...]
    owner, place = sizes.owner(group), sizes.place(group)
    most = jnp.zeros((sizes.peers, 1), F32)
    for source in range(sizes.ch):
        marks = iota((sizes.peers, sizes.channels), 0) == owner[source : source + 1]
        most = jnp.maximum(most, jnp.sum(jnp.where(marks, 1.0, 0.0), axis=1, keepdims=True))
    over_ref[...] = jnp.broadcast_to(jnp.max(most, axis=0, keepdims=True), (8, LANES)).astype(I32)

    earlier = jnp.zeros((sizes.own, 1), F32)
    into = jnp.zeros((256, sizes.ch * sizes.cap), F32)
    for source in range(sizes.ch):
        mine = owner[source : source + 1] == me
        where = jnp.where(mine, place[source : source + 1], -1)
        marks = iota((sizes.own, sizes.channels), 0) == where
        counts, totals = running_counts(hot(marks), upper)
        slot = jnp.sum(counts, axis=0, keepdims=True).astype(I32)
        nth = jnp.sum(jnp.where(marks, counts + earlier, 0.0), axis=0, keepdims=True).astype(I32)
        earlier = earlier + totals
        row = jnp.where(mine, where * sizes.size + nth, -1)
        column = jnp.where(mine & (slot < sizes.cap - 1), slot, -1)
        to_row = hot(iota((256, sizes.channels), 0) == row)
        to_column = hot(iota((LANES, sizes.channels), 0) == column)
        found = dot_lanes(to_row, to_column).astype(BF16)
        back_ref[:, source * LANES : (source + 1) * LANES] = found
        shape = (LANES, sizes.ch * sizes.cap)
        moved = hot(
            (iota(shape, 1) == iota(shape, 0) + source * sizes.cap)
            & (iota(shape, 0) < sizes.cap)
        )
        into = into + dot(found, moved)
    into_ref[...] = into.astype(BF16)

    rate, gain = rate_ref[...], gain_ref[...]
    step = iota((256, sizes.run), 1).astype(F32)
    high, low = two_terms(gain * jnp.exp(-rate * step))
    table_ref[...] = jnp.concatenate([high, low], axis=1)


def index(sizes, me, all_groups, rate_col, gain_col):
    return pl.pallas_call(
        functools.partial(index_kernel, sizes),
        in_specs=[pl.BlockSpec(memory_space=pltpu.SMEM)]
        + [pl.BlockSpec(memory_space=pltpu.VMEM)] * 3,
        out_shape=[
            jax.ShapeDtypeStruct((256, sizes.ch * sizes.cap), BF16),
            jax.ShapeDtypeStruct((256, sizes.ch * LANES), BF16),
            jax.ShapeDtypeStruct((8, LANES), I32),
            jax.ShapeDtypeStruct((256, 2 * sizes.run), BF16),
        ],
        compiler_params=pltpu.CompilerParams(vmem_limit_bytes=VMEM_LIMIT),
        cost_estimate=pl.CostEstimate(flops=2 * 10**9, bytes_accessed=10**6, transcendentals=0),
        name="index_rows",
    )(me, all_groups, rate_col, gain_col)


def local_kernel(
    sizes, group_ref, param_ref, key_ref, value_ref, conv_ref, decay_ref, params, turned
):
    modes = param_ref.shape[0] // 2
    blocks = sizes.channels // LANES
    exact = param_ref[...]
    high, rest = two_terms(exact)
    low, last = two_terms(exact - high.astype(F32) - rest.astype(F32))
    stacked = jnp.concatenate([high, rest, low], axis=0)
    rows = 2 * modes
    for start in range(0, sizes.channels, 256):
        chosen = hot(iota((sizes.groups, 256), 0) == group_ref[:, start : start + 256])
        found = dot(stacked, chosen)
        found = found[:rows] + found[rows : 2 * rows] + found[2 * rows :]
        for half in range(2):
            block = start // LANES + half
            params[block * rows : (block + 1) * rows, :] = found[
                :, half * LANES : (half + 1) * LANES
            ]

    def turn(block, carry):
        at = pl.ds(pl.multiple_of(block * LANES, LANES), LANES)
        gated = (key_ref[at, :].astype(F32) * value_ref[at, :].astype(F32)).astype(BF16)
        turned[pl.ds(block, sizes.tokens, stride=blocks), :] = gated.astype(F32).T
        return carry

    lax.fori_loop(0, blocks, turn, 0)
    for first in range(0, blocks, 8):
        decays, gains = [], []
        for mode in range(modes):
            rate = params[pl.ds(first * rows + mode, 8, stride=rows), :]
            gains.append(params[pl.ds(first * rows + modes + mode, 8, stride=rows), :])
            decays.append(jnp.exp(-rate))
            decay_ref[mode * blocks + first : mode * blocks + first + 8, :] = decays[-1]
        for half in range(2):

            def step(token, states):
                at = (half * sizes.run + token) * blocks + first
                at = pl.ds(pl.multiple_of(at, 8), 8)
                value = turned[at, :]
                states = [a * s + c * value for a, c, s in zip(decays, gains, states)]
                conv_ref[at, :] = tree_sum(states)
                return states

            lax.fori_loop(0, sizes.run, step, [jnp.zeros((8, LANES), F32)] * modes)


def tree_sum(terms):
    while len(terms) > 1:
        terms = [
            terms[i] + terms[i + 1] if i + 1 < len(terms) else terms[i]
            for i in range(0, len(terms), 2)
        ]
    return terms[0]


def local(sizes, shard_groups, params, key_proj, value_proj):
    modes = params.shape[0] // 2
    blocks = sizes.channels // LANES
    return pl.pallas_call(
        functools.partial(local_kernel, sizes),
        in_specs=[pl.BlockSpec(memory_space=pltpu.VMEM)] * 4,
        out_shape=[
            jax.ShapeDtypeStruct((sizes.tokens * blocks, LANES), F32),
            jax.ShapeDtypeStruct((modes * blocks, LANES), F32),
        ],
        scratch_shapes=[
            pltpu.VMEM((blocks * 2 * modes, LANES), F32),
            pltpu.VMEM((sizes.tokens * blocks, LANES), F32),
        ],
        compiler_params=pltpu.CompilerParams(vmem_limit_bytes=VMEM_LIMIT),
        cost_estimate=pl.CostEstimate(flops=4 * 10**9, bytes_accessed=3 * 10**6, transcendentals=0),
        name="local_runs",
    )(shard_groups, params, key_proj, value_proj)


def owner_kernel(
    sizes,
    recv_ref,
    into_ref,
    back_ref,
    table_ref,
    leap_ref,
    out_ref,
    gated,
    weighted,
    states,
    sums,
    run_at,
):
    run, runs, own, size = sizes.run, sizes.runs, sizes.own, sizes.size
    rows = own * size
    lane = iota((rows, LANES), 1)
    mirror = hot(iota((LANES, LANES), 0) + iota((LANES, LANES), 1) == LANES - 1)
    weighted[runs : 2 * runs + 1] = jnp.zeros((runs + 1, rows, LANES), BF16)
    for source in range(sizes.ctx):
        tail = recv_ref[source * sizes.ch, sizes.cap - 16 : sizes.cap, :].astype(F32)
        ids = tail[15:16, :]
        first = jnp.max(ids[:, :LANES]).astype(I32)
        second = jnp.max(ids[:, LANES:]).astype(I32)
        run_at[2 * source] = first
        run_at[2 * source + 1] = second
        block = recv_ref[source * sizes.ch : (source + 1) * sizes.ch]
        block = block.reshape(sizes.ch * sizes.cap, 2 * LANES)
        found = dot(into_ref[...], block)
        mirrored = dot(found[:, :LANES].astype(BF16), mirror)
        swapped = pltpu.roll(mirrored, run, 1)
        gated[second] = jnp.where(lane < run, mirrored, swapped).astype(BF16)
        gated[first] = jnp.where(lane < run, swapped, mirrored).astype(BF16)
        value = found[:, LANES:]
        turned = pltpu.roll(value, run, 1).astype(BF16)
        value = value.astype(BF16)
        weighted[first + 1, :, :run] = value[:, :run]
        weighted[first, :, run:] = turned[:, run:]
        weighted[second + 1, :, :run] = turned[:, :run]
        weighted[second, :, run:] = value[:, run:]

    modes = states.shape[1]
    group_lane = lax.shift_right_logical(iota((modes, rows), 1), size.bit_length() - 1)
    carried = jnp.zeros((modes, rows), F32)
    leap = leap_ref[...]
    for at in range(runs):
        states[at] = carried
        if at + 1 < runs:
            ends = dot_lanes(table_ref[...], gated[at])
            total = jnp.zeros((modes, rows), F32)
            for group in range(own):
                piece = ends[group * modes : (group + 1) * modes]
                total = total + jnp.where(group_lane == group, piece, 0.0)
            carried = carried * leap + total

    seq = run * runs

    def one_group(group, carry):
        at = pl.ds(pl.multiple_of(group * size, size), size)
        left = gated[:, at, :].reshape(runs * size, LANES).T[:run]
        right = jnp.concatenate(
            [
                weighted[1 + lag : 1 + lag + runs, at, :].reshape(runs * size, LANES)
                for lag in range(0, runs, 2)
            ],
            axis=1,
        )
        gram = jnp.concatenate([dot(left, right), jnp.zeros((run, LANES), F32)], axis=1)
        skewed = pltpu.roll(gram, seq + LANES - (run - 1), 1, stride=1, stride_axis=0)
        sums[pl.ds(group, 1), :] = jnp.sum(skewed, axis=0, keepdims=True)[:, :seq]
        return carry

    lax.fori_loop(0, own, one_group, 0)

    each = sizes.each
    quarter = LANES // 4
    out_lane = iota((32, LANES), 1)
    for target in range(sizes.ctx):
        pair = jnp.concatenate(
            [states[run_at[2 * target]], states[run_at[2 * target + 1]]], axis=0
        )
        sent = dot(pair.astype(BF16), back_ref[...])
        lags = sums[:, target * LANES : (target + 1) * LANES]
        high = lags.astype(BF16).astype(F32)
        low = lags - high
        moved = [
            [pltpu.roll(term, (7 * quarter - q * quarter) % LANES, 1) for q in range(4)]
            for term in (high, low)
        ]
        for chan in range(sizes.ch):
            lag_rows = jnp.concatenate(
                [part[chan * each : (chan + 1) * each] for term in moved for part in term], axis=0
            )
            mine = sent[:, chan * LANES : (chan + 1) * LANES]
            out_ref[target * sizes.ch + chan] = jnp.where(
                out_lane < 3 * quarter, mine, lag_rows
            ).astype(BF16)


def owner(sizes, recv, into, back, table, leap):
    rows = sizes.own * sizes.size
    modes = leap.shape[0]
    return pl.pallas_call(
        functools.partial(owner_kernel, sizes),
        in_specs=[pl.BlockSpec(memory_space=pltpu.VMEM)] * 5,
        out_shape=jax.ShapeDtypeStruct((sizes.peers, 2 * modes, LANES), BF16),
        scratch_shapes=[
            pltpu.VMEM((sizes.runs, rows, LANES), BF16),
            pltpu.VMEM((2 * sizes.runs + 1, rows, LANES), BF16),
            pltpu.VMEM((sizes.runs, modes, rows), F32),
            pltpu.VMEM((sizes.own, sizes.run * sizes.runs), F32),
            pltpu.SMEM((sizes.runs,), I32),
        ],
        compiler_params=pltpu.CompilerParams(vmem_limit_bytes=VMEM_LIMIT),
        name="owner_sums",
    )(recv, into, back, table, leap)


def finish_kernel(
    sizes, recv_ref, dest_ref, conv_ref, decay_ref, query_ref, out_ref, grad_ref, found, total
):
    blocks = sizes.channels // LANES
    rows = recv_ref.shape[1]
    modes = rows // 2
    everything = recv_ref[...].reshape(sizes.peers * rows, LANES)

    def fetch(part, carry):
        at = pl.ds(pl.multiple_of(part * 256, 256), 256)
        owner, slot = dest_ref[1:2, at], dest_ref[2:3, at]
        chosen = hot(iota((LANES, 256), 0) == slot)
        picked = dot(everything, chosen)
        mine = jnp.zeros((rows, 256), F32)
        for peer in range(sizes.peers):
            mine = mine + jnp.where(owner == peer, picked[peer * rows : (peer + 1) * rows], 0.0)
        for half in range(2):
            start = pl.multiple_of((2 * part + half) * rows, rows)
            found[pl.ds(start, rows), :] = mine[:, half * LANES : (half + 1) * LANES]
        return carry

    lax.fori_loop(0, sizes.channels // 256, fetch, 0)
    for first in range(0, blocks, 8):
        decays = [
            decay_ref[mode * blocks + first : mode * blocks + first + 8, :]
            for mode in range(modes)
        ]
        for half in range(2):
            states = [
                found[pl.ds(first * rows + half * modes + mode, 8, stride=rows), :]
                for mode in range(modes)
            ]

            def step(token, states):
                at = (half * sizes.run + token) * blocks + first
                at = pl.ds(pl.multiple_of(at, 8), 8)
                states = [a * s for a, s in zip(decays, states)]
                total[at, :] = conv_ref[at, :] + tree_sum(states)
                return states

            lax.fori_loop(0, sizes.run, step, states)

    def turn(block, carry):
        at = pl.ds(pl.multiple_of(block * LANES, LANES), LANES)
        conv = total[pl.ds(block, sizes.tokens, stride=blocks), :].T.astype(BF16)
        out_ref[at, :] = (query_ref[at, :].astype(F32) * conv.astype(F32)).astype(BF16)
        return carry

    lax.fori_loop(0, blocks, turn, 0)

    each, quarter = sizes.each, LANES // 4
    high_low = recv_ref[...].astype(F32)
    terms = []
    lane_part = lax.shift_right_logical(iota((sizes.peers * 16, LANES), 1), 5)
    row = iota((sizes.peers * 16, LANES), 0)
    row_part = lax.shift_right_logical(row & 15, each.bit_length() - 1)
    for term in range(2):
        piece = high_low[:, term * 16 : (term + 1) * 16, :].reshape(sizes.peers * 16, LANES)
        placed = jnp.zeros((sizes.peers * 16, LANES), F32)
        for part in range(4):
            moved = pltpu.roll(piece, (part * quarter + quarter) % LANES, 1)
            placed = jnp.where((row_part == part) & (lane_part == part), moved, placed)
        terms.append(placed.astype(BF16))
    shape = (sizes.block, sizes.peers * 16)
    to, come = iota(shape, 0), iota(shape, 1)
    bits = each.bit_length() - 1
    chosen = hot(
        (lax.shift_right_logical(to, bits) == lax.shift_right_logical(come, 4))
        & ((to & (each - 1)) == (come & (each - 1)))
    )
    grad_ref[...] = dot(chosen, terms[0]) + dot(chosen, terms[1])


def finish(sizes, recv, dest, conv, decay, query_proj):
    blocks = sizes.channels // LANES
    return pl.pallas_call(
        functools.partial(finish_kernel, sizes),
        in_specs=[pl.BlockSpec(memory_space=pltpu.VMEM)] * 5,
        out_shape=[
            jax.ShapeDtypeStruct((sizes.channels, sizes.tokens), BF16),
            jax.ShapeDtypeStruct((sizes.block, LANES), F32),
        ],
        scratch_shapes=[
            pltpu.VMEM((blocks * recv.shape[1], LANES), F32),
            pltpu.VMEM((sizes.tokens * blocks, LANES), F32),
        ],
        compiler_params=pltpu.CompilerParams(vmem_limit_bytes=VMEM_LIMIT),
        name="finish_rows",
    )(recv, dest, conv, decay, query_proj)


def exchange(blocks):
    return lax.all_to_all(blocks, ("ctx", "ch"), split_axis=0, concat_axis=0, tiled=True)


def owners_way(sizes, args):
    query_proj, key_proj, value_proj, cotangent, positions, group_of, decay_rates, residues = args
    ch_rank = lax.axis_index("ch")
    me = lax.axis_index("ctx") * sizes.ch + ch_rank
    run_ids = jnp.stack([positions[0], positions[sizes.run]]) // sizes.run
    all_groups = group_of.reshape(sizes.ch, sizes.channels)
    shard_groups = lax.dynamic_slice_in_dim(all_groups, ch_rank, 1)
    sent, dest = pack(sizes, run_ids, shard_groups, key_proj, value_proj, cotangent, query_proj)
    recv = exchange(sent)

    gains = residues * jnp.sqrt(2.0 * decay_rates)
    params = jnp.concatenate([decay_rates, gains], axis=1).T
    conv, decay = local(sizes, shard_groups, params, key_proj, value_proj)
    modes = decay_rates.shape[1]

    def owned(values):
        split = values.reshape(sizes.ch, sizes.peers, sizes.each, modes)
        mine = lax.dynamic_index_in_dim(split, me, 1, keepdims=False)
        return mine.reshape(sizes.own, modes)

    own_rates, own_gains = owned(decay_rates), owned(gains)
    leap = jnp.repeat(jnp.exp(-float(sizes.run) * own_rates.T), sizes.size, axis=1)
    into, back, most, table = index(
        sizes,
        me.reshape(1).astype(I32),
        all_groups,
        own_rates.reshape(-1, 1),
        own_gains.reshape(-1, 1),
    )

    def fast(recv, into, back, table, leap, dest, conv, decay, *args):
        returned = exchange(owner(sizes, recv, into, back, table, leap))
        return tuple(finish(sizes, returned, dest, conv, decay, args[0]))

    def slow(recv, into, back, table, leap, dest, conv, decay, *args):
        return general_way(*args)

    return lax.cond(
        most[0, 0] <= sizes.cap - 1,
        fast,
        slow,
        recv,
        into,
        back,
        table,
        leap,
        dest,
        conv,
        decay,
        *args,
    )


def shards(*args):
    sizes = Sizes(
        lax.axis_size("ctx"), lax.axis_size("ch"), *args[0].shape, args[6].shape[0]
    )
    if not sizes.fits:
        return general_way(*args)
    return owners_way(sizes, args)


def solution(mesh):
    placed = (
        P("ch", "ctx"),
        P("ch", "ctx"),
        P("ch", "ctx"),
        P("ch", "ctx"),
        P("ctx"),
        P(),
        P(),
        P(),
    )
    return jax.shard_map(
        shards,
        mesh=mesh,
        in_specs=placed,
        out_specs=(P("ch", "ctx"), P("ch", "ctx")),
        check_vma=False,
    )
```

```python
import functools
import math

import jax
import jax.numpy as jnp
import numpy as np
from jax import lax
from jax.experimental import pallas as pl
from jax.experimental.pallas import tpu as pltpu
from jax.sharding import PartitionSpec as P

F32 = jnp.float32
BF16 = jnp.bfloat16
I32 = jnp.int32
LANES = 128
VMEM_LIMIT = 48 * 1024 * 1024


def product(form, left, right):
    return jnp.einsum(form, left, right, precision=lax.Precision.HIGHEST)


def split_rows(extent):
    chosen = 2
    for divisor in range(2, math.isqrt(extent) + 1, 2):
        if extent % divisor == 0:
            chosen = divisor
    return chosen


def dft_tables(row_count, col_count, extent):
    row_index = jnp.arange(row_count, dtype=jnp.int32)
    col_index = jnp.arange(col_count, dtype=jnp.int32)

    def angles(left_index, right_index, modulus):
        phase = left_index[:, None] * right_index[None, :] % modulus
        return phase.astype(jnp.float32) * (2.0 * math.pi / modulus)

    row_angle = angles(row_index, row_index, row_count)
    col_angle = angles(col_index, col_index, col_count)
    twist_angle = angles(row_index, col_index, extent)
    return (
        jnp.cos(row_angle),
        jnp.sin(row_angle),
        jnp.cos(col_angle),
        jnp.sin(col_angle),
        jnp.cos(twist_angle),
        jnp.sin(twist_angle),
    )


def forward_transform(signal, tables, row_count, col_count):
    row_cos, row_sin, col_cos, col_sin, twist_cos, twist_sin = tables
    folded = signal.reshape(signal.shape[0], row_count // 2, col_count)
    mid_real = product("ka,cab->ckb", row_cos[:, : row_count // 2], folded)
    mid_imag = -product("ka,cab->ckb", row_sin[:, : row_count // 2], folded)
    turned_real = mid_real * twist_cos + mid_imag * twist_sin
    turned_imag = mid_imag * twist_cos - mid_real * twist_sin
    spec_real = product("ckb,bm->ckm", turned_real, col_cos) + product(
        "ckb,bm->ckm", turned_imag, col_sin
    )
    spec_imag = product("ckb,bm->ckm", turned_imag, col_cos) - product(
        "ckb,bm->ckm", turned_real, col_sin
    )
    return (spec_real, spec_imag)


def inverse_transform(spec_real, spec_imag, tables, row_count, col_count):
    row_cos, row_sin, col_cos, col_sin, twist_cos, twist_sin = tables
    mid_real = product("ckm,bm->ckb", spec_real, col_cos) - product(
        "ckm,bm->ckb", spec_imag, col_sin
    )
    mid_imag = product("ckm,bm->ckb", spec_imag, col_cos) + product(
        "ckm,bm->ckb", spec_real, col_sin
    )
    turned_real = mid_real * twist_cos - mid_imag * twist_sin
    turned_imag = mid_imag * twist_cos + mid_real * twist_sin
    folded = product("ak,ckb->cab", row_cos[: row_count // 2, :], turned_real) - product(
        "ak,ckb->cab", row_sin[: row_count // 2, :], turned_imag
    )
    return folded.reshape(spec_real.shape[0], -1) / float(row_count * col_count)


def spectra(gated_seq, weighted_seq, chan_groups, decay_rates, residues, seq_length):
    extent = 2 * seq_length
    row_count = split_rows(extent)
    col_count = extent // row_count
    decay_rows = decay_rates[chan_groups]
    gain_rows = residues[chan_groups]
    tap_index = jnp.arange(seq_length, dtype=jnp.float32)
    coefs = gain_rows * jnp.sqrt(2.0 * decay_rows)
    filters = jnp.sum(coefs[:, :, None] * jnp.exp(-decay_rows[:, :, None] * tap_index), axis=1)
    tables = dft_tables(row_count, col_count, extent)
    gated_real, gated_imag = forward_transform(
        gated_seq.astype(jnp.float32), tables, row_count, col_count
    )
    filter_real, filter_imag = forward_transform(filters, tables, row_count, col_count)
    weight_real, weight_imag = forward_transform(
        weighted_seq.astype(jnp.float32), tables, row_count, col_count
    )
    convolved = inverse_transform(
        filter_real * gated_real - filter_imag * gated_imag,
        filter_real * gated_imag + filter_imag * gated_real,
        tables,
        row_count,
        col_count,
    )
    lagged = inverse_transform(
        weight_real * gated_real + weight_imag * gated_imag,
        weight_imag * gated_real - weight_real * gated_imag,
        tables,
        row_count,
        col_count,
    )
    return (convolved, lagged)


def general_way(
    query_proj, key_proj, value_proj, cotangent, positions, group_of, decay_rates, residues
):
    ctx_count = lax.axis_size("ctx")
    ch_count = lax.axis_size("ch")
    ctx_rank = lax.axis_index("ctx")
    ch_rank = lax.axis_index("ch")
    local_channels, local_tokens = query_proj.shape
    half_run = local_tokens // 2
    run_count = 2 * ctx_count
    seq_length = local_tokens * ctx_count
    per_device = local_channels // ctx_count
    groups_total = decay_rates.shape[0]
    gated = (key_proj.astype(jnp.float32) * value_proj.astype(jnp.float32)).astype(jnp.bfloat16)
    weighted = (cotangent.astype(jnp.float32) * query_proj.astype(jnp.float32)).astype(jnp.bfloat16)
    run_ids = jnp.stack([positions[0], positions[half_run]]) // half_run
    all_runs = lax.all_to_all(
        jnp.broadcast_to(run_ids[None, :], (ctx_count, 2)),
        "ctx",
        split_axis=0,
        concat_axis=0,
        tiled=True,
    ).reshape(run_count)
    source_run = (
        jnp.zeros((run_count,), jnp.int32).at[all_runs].set(jnp.arange(run_count, dtype=jnp.int32))
    )

    def to_sequence(stored):
        return stored.reshape(per_device, run_count, half_run)[:, source_run, :].reshape(
            per_device, seq_length
        )

    shard_groups = lax.dynamic_slice_in_dim(group_of, ch_rank * local_channels, local_channels)
    gated_cols, weighted_cols = (
        lax.all_to_all(gated, "ctx", split_axis=0, concat_axis=1, tiled=True),
        lax.all_to_all(weighted, "ctx", split_axis=0, concat_axis=1, tiled=True),
    )
    first_channel = ch_rank * local_channels + ctx_rank * per_device
    chan_groups = lax.dynamic_slice_in_dim(group_of, first_channel, per_device)
    convolved, lagged = spectra(
        to_sequence(gated_cols),
        to_sequence(weighted_cols),
        chan_groups,
        decay_rates,
        residues,
        seq_length,
    )
    ordered = convolved.astype(jnp.bfloat16).reshape(per_device, run_count, half_run)[
        :, all_runs, :
    ]
    conv_tokens = lax.all_to_all(
        ordered.reshape(per_device, seq_length), "ctx", split_axis=1, concat_axis=0, tiled=True
    )
    output = (query_proj.astype(jnp.float32) * conv_tokens.astype(jnp.float32)).astype(jnp.bfloat16)
    lag_rows = lax.all_to_all(lagged, "ctx", split_axis=1, concat_axis=0, tiled=True)
    select_all = (
        jnp.arange(groups_total, dtype=jnp.int32)[:, None] == shard_groups[None, :]
    ).astype(jnp.float32)
    partial = jnp.dot(
        select_all, lag_rows, precision=lax.Precision.HIGHEST, preferred_element_type=jnp.float32
    ).reshape(ch_count, groups_total // ch_count, local_tokens)
    filter_grad = jnp.sum(
        lax.all_to_all(partial, "ch", split_axis=0, concat_axis=0, tiled=True), axis=0
    )
    return (output, filter_grad)


def iota(shape, dim):
    return lax.broadcasted_iota(I32, shape, dim)


def hot(flags):
    return jnp.where(flags, 1.0, 0.0).astype(BF16)


def dot(left, right):
    return jnp.dot(left, right, preferred_element_type=F32)


def dot_lanes(left, right):
    return lax.dot_general(left, right, (((1,), (1,)), ((), ())), preferred_element_type=F32)


def two_terms(values):
    high = values.astype(BF16)
    return high, (values - high.astype(F32)).astype(BF16)


class Sizes:
    def __init__(self, ctx, ch, channels, tokens, groups):
        self.ctx, self.ch = ctx, ch
        self.peers = ctx * ch
        self.channels = channels
        self.tokens = tokens
        self.run = tokens // 2
        self.runs = 2 * ctx
        self.groups = groups
        self.block = groups // ch
        self.each = self.block // self.peers
        self.own = groups // self.peers
        self.size = channels * ch // groups
        self.cap = 80
        powers = [self.block, max(self.each, 1), self.own, self.size]
        self.fits = (
            tokens == LANES
            and self.block == LANES
            and self.runs == 16
            and self.own == 16
            and self.size == 16
            and self.each * self.peers == self.block
            and self.each * 8 * self.run == 16 * LANES
            and ch == 4
            and channels % 2048 == 0
            and channels // self.peers <= 64
            and all(p & (p - 1) == 0 for p in powers)
        )

    def deal(self):
        ways = np.zeros((8, 64), np.int32)
        for way in range(64):
            step = 2 * (way // 2) + 1
            ways[:3, way] = (pow(step, -1, self.block), self.each // 2 * (way % 2), step)
        return ways

    def seat(self, group, way):
        turn, start, _ = way
        return (turn * (group & (self.block - 1)) + start) & (self.block - 1)

    def owner(self, group, way):
        return lax.shift_right_logical(self.seat(group, way), bits(self.each))

    def place(self, group, way):
        block = lax.shift_right_logical(group, bits(self.block))
        return block * self.each + (self.seat(group, way) & (self.each - 1))

    def group_at(self, seat, way):
        _, start, step = way
        return (step * (seat - start)) & (self.block - 1)

    def group_here(self, place, me, way):
        block = lax.shift_right_logical(place, bits(self.each))
        seat = me * self.each + (place & (self.each - 1))
        return block * self.block + self.group_at(seat, way)


def bits(power):
    return power.bit_length() - 1


def way_of(dest_ref):
    return tuple(dest_ref[row : row + 1, 0:1] for row in (3, 4, 5))


def running_counts(marks, upper):
    width = upper.shape[0]
    before, counts = jnp.zeros((marks.shape[0], 1), F32), []
    for start in range(0, marks.shape[1], width):
        part = marks[:, start : start + width]
        counts.append(dot(part, upper) + before)
        before = before + jnp.sum(part.astype(F32), axis=1, keepdims=True)
    return jnp.concatenate(counts, axis=1), before


def upper_ones(width):
    return hot(iota((width, width), 0) < iota((width, width), 1))


def choose_way(sizes, group, ways):
    count = ways.shape[1]
    low = 16
    group = group & (sizes.block - 1)
    loads = []
    for source in range(sizes.ch):
        row = group[source : source + 1]
        high_hot = hot(iota((sizes.block // low, sizes.channels), 0) == lax.shift_right_logical(row, 4))
        low_hot = hot(iota((low, sizes.channels), 0) == (row & (low - 1)))
        table = dot_lanes(high_hot, low_hot)
        spread = hot((iota((low, sizes.block), 1) & (low - 1)) == iota((low, sizes.block), 0))
        wide = dot(table.astype(BF16), spread)
        own = lax.shift_right_logical(iota(wide.shape, 1), 4) == iota(wide.shape, 0)
        loads.append(jnp.sum(jnp.where(own, wide, 0.0), axis=0, keepdims=True))
    loads = jnp.concatenate(loads + [jnp.zeros((8 - sizes.ch, sizes.block), F32)], axis=0)
    lanes = sizes.peers * count
    spread_ways = jnp.concatenate([ways] * sizes.peers, axis=1)
    seat = sizes.seat(iota((sizes.block, lanes), 0), (spread_ways[0:1], spread_ways[1:2], None))
    peer = lax.shift_right_logical(iota((1, lanes), 1), bits(count))
    dealt = hot(lax.shift_right_logical(seat, bits(sizes.each)) == peer)
    sums = dot(loads.astype(BF16), dealt)
    fullest = sums[:, :LANES]
    for start in range(LANES, lanes, LANES):
        fullest = jnp.maximum(fullest, sums[:, start : start + LANES])
    fullest = jnp.max(jnp.maximum(fullest, pltpu.roll(fullest, count, 1)), axis=0, keepdims=True)
    score = fullest[:, :count] * float(count) + iota((1, count), 1).astype(F32)
    best = jnp.min(score, axis=1, keepdims=True)
    mine = jnp.where(score == best, ways[0:3].astype(F32), 0.0)
    chosen = jnp.sum(mine, axis=1, keepdims=True).astype(I32)
    return chosen[0:1], chosen[1:2], chosen[2:3]


def pack_kernel(
    sizes,
    place_ref,
    ways_ref,
    all_ref,
    group_ref,
    key_ref,
    value_ref,
    cot_ref,
    query_ref,
    out_ref,
    dest_ref,
    data,
):
    part = out_ref.shape[0]

    @pl.when(pl.program_id(0) == 0)
    def _():
        way = choose_way(sizes, all_ref[...], ways_ref[...])
        owner = sizes.owner(group_ref[...], way)
        marks = iota((sizes.peers, sizes.channels), 0) == owner
        counts, _ = running_counts(hot(marks), upper_ones(256))
        slot = jnp.sum(jnp.where(marks, counts, 0.0), axis=0, keepdims=True).astype(I32)
        dest_ref[0:1, :] = jnp.where(slot < sizes.cap - 1, owner * sizes.cap + slot, -1)
        dest_ref[1:2, :] = owner
        dest_ref[2:3, :] = slot
        for row in range(3):
            dest_ref[3 + row : 4 + row, :] = jnp.broadcast_to(way[row], (1, sizes.channels))
        dest_ref[6:8, :] = jnp.zeros((2, sizes.channels), I32)
        data[:, :LANES] = (key_ref[...].astype(F32) * value_ref[...].astype(F32)).astype(BF16)
        data[:, LANES:] = (cot_ref[...].astype(F32) * query_ref[...].astype(F32)).astype(BF16)

    shift = bits(sizes.run)
    first = lax.shift_right_logical(place_ref[0], shift)
    second = lax.shift_right_logical(place_ref[sizes.run], shift)
    run_row = jnp.where(iota((1, 1, 2 * LANES), 2) < LANES, first, second).astype(F32)
    base = pl.program_id(0) * part * sizes.cap
    chosen = hot(iota((part * sizes.cap, sizes.channels), 0) == dest_ref[0:1, :] - base)
    rows = dot(chosen, data[...]).reshape(part, sizes.cap, 2 * LANES)
    spare = iota((part, sizes.cap, 1), 1) == sizes.cap - 1
    out_ref[...] = jnp.where(spare, run_row, rows).astype(BF16)


def pack(sizes, positions, ways, all_groups, shard_groups, key_proj, value_proj, cotangent, query_proj):
    part = 8
    whole = lambda shape: pl.BlockSpec(shape, lambda step: (0, 0))
    rows = (sizes.channels, sizes.tokens)
    return pl.pallas_call(
        functools.partial(pack_kernel, sizes),
        grid=(sizes.peers // part,),
        in_specs=[
            pl.BlockSpec(memory_space=pltpu.SMEM),
            whole(ways.shape),
            whole((sizes.ch, sizes.channels)),
            whole((1, sizes.channels)),
            whole(rows),
            whole(rows),
            whole(rows),
            whole(rows),
        ],
        out_specs=[
            pl.BlockSpec((part, sizes.cap, 2 * LANES), lambda step: (step, 0, 0)),
            whole((8, sizes.channels)),
        ],
        out_shape=[
            jax.ShapeDtypeStruct((sizes.peers, sizes.cap, 2 * LANES), BF16),
            jax.ShapeDtypeStruct((8, sizes.channels), I32),
        ],
        scratch_shapes=[pltpu.VMEM((sizes.channels, 2 * LANES), BF16)],
        compiler_params=pltpu.CompilerParams(vmem_limit_bytes=VMEM_LIMIT),
        name="pack_rows",
    )(positions, ways, all_groups, shard_groups, key_proj, value_proj, cotangent, query_proj)


def index_kernel(
    sizes,
    me_ref,
    group_ref,
    dest_ref,
    param_ref,
    into_ref,
    back_ref,
    over_ref,
    table_ref,
    leap_ref,
):
    me = me_ref[0]
    way = way_of(dest_ref)
    upper = upper_ones(256)
    group = group_ref[...]
    owner, place = sizes.owner(group, way), sizes.place(group, way)
    most = jnp.zeros((sizes.peers, 1), F32)
    for source in range(sizes.ch):
        marks = iota((sizes.peers, sizes.channels), 0) == owner[source : source + 1]
        most = jnp.maximum(most, jnp.sum(jnp.where(marks, 1.0, 0.0), axis=1, keepdims=True))
    over_ref[...] = jnp.broadcast_to(jnp.max(most, axis=0, keepdims=True), (8, LANES)).astype(I32)

    earlier = jnp.zeros((sizes.own, 1), F32)
    into = jnp.zeros((256, sizes.ch * sizes.cap), F32)
    for source in range(sizes.ch):
        mine = owner[source : source + 1] == me
        where = jnp.where(mine, place[source : source + 1], -1)
        marks = iota((sizes.own, sizes.channels), 0) == where
        counts, totals = running_counts(hot(marks), upper)
        slot = jnp.sum(counts, axis=0, keepdims=True).astype(I32)
        nth = jnp.sum(jnp.where(marks, counts + earlier, 0.0), axis=0, keepdims=True).astype(I32)
        earlier = earlier + totals
        row = jnp.where(mine, where * sizes.size + nth, -1)
        column = jnp.where(mine & (slot < sizes.cap - 1), slot, -1)
        to_row = hot(iota((256, sizes.channels), 0) == row)
        to_column = hot(iota((LANES, sizes.channels), 0) == column)
        found = dot_lanes(to_row, to_column).astype(BF16)
        back_ref[:, source * LANES : (source + 1) * LANES] = found
        shape = (LANES, sizes.ch * sizes.cap)
        moved = hot(
            (iota(shape, 1) == iota(shape, 0) + source * sizes.cap)
            & (iota(shape, 0) < sizes.cap)
        )
        into = into + dot(found, moved)
    into_ref[...] = into.astype(BF16)

    modes = leap_ref.shape[0]
    terms = three_terms(param_ref[...])
    shape = (256, sizes.groups)
    wanted = sizes.group_here(lax.shift_right_logical(iota((256, 1), 0), bits(modes)), me, way)
    found = dot_lanes(hot(iota(shape, 1) == wanted), terms)
    found = three_sum(found, 1)
    mode = iota((256, 2 * modes), 0) & (modes - 1)
    lane = iota((256, 2 * modes), 1)
    rate = jnp.sum(jnp.where(lane == mode, found, 0.0), axis=1, keepdims=True)
    gain = jnp.sum(jnp.where(lane == mode + modes, found, 0.0), axis=1, keepdims=True)
    step = iota((256, sizes.run), 1).astype(F32)
    high, low = two_terms(gain * jnp.exp(-rate * step))
    table_ref[...] = jnp.concatenate([high, low], axis=1)
    shape = (sizes.groups, 256)
    wanted = sizes.group_here(lax.shift_right_logical(iota((1, 256), 1), bits(sizes.size)), me, way)
    found = three_sum(dot(terms, hot(iota(shape, 0) == wanted)), 0)
    leap_ref[...] = jnp.exp(found[:modes] * -float(sizes.run))


def three_terms(exact):
    high, rest = two_terms(exact)
    low, _ = two_terms(exact - high.astype(F32) - rest.astype(F32))
    return jnp.concatenate([high, rest, low], axis=0)


def three_sum(found, dim):
    high, rest, low = jnp.split(found, 3, axis=dim)
    return high + rest + low


def index(sizes, me, all_groups, dest, params):
    modes = params.shape[0] // 2
    return pl.pallas_call(
        functools.partial(index_kernel, sizes),
        in_specs=[pl.BlockSpec(memory_space=pltpu.SMEM)]
        + [pl.BlockSpec(memory_space=pltpu.VMEM)] * 3,
        out_shape=[
            jax.ShapeDtypeStruct((256, sizes.ch * sizes.cap), BF16),
            jax.ShapeDtypeStruct((256, sizes.ch * LANES), BF16),
            jax.ShapeDtypeStruct((8, LANES), I32),
            jax.ShapeDtypeStruct((256, 2 * sizes.run), BF16),
            jax.ShapeDtypeStruct((modes, 256), F32),
        ],
        compiler_params=pltpu.CompilerParams(vmem_limit_bytes=VMEM_LIMIT),
        cost_estimate=pl.CostEstimate(flops=2 * 10**9, bytes_accessed=10**6, transcendentals=0),
        name="index_rows",
    )(me, all_groups, dest, params)


def local_kernel(
    sizes, group_ref, param_ref, key_ref, value_ref, conv_ref, decay_ref, params, turned
):
    modes = param_ref.shape[0] // 2
    blocks = sizes.channels // LANES
    stacked = three_terms(param_ref[...])
    rows = 2 * modes
    for start in range(0, sizes.channels, 256):
        chosen = hot(iota((sizes.groups, 256), 0) == group_ref[:, start : start + 256])
        found = three_sum(dot(stacked, chosen), 0)
        for half in range(2):
            block = start // LANES + half
            params[block * rows : (block + 1) * rows, :] = found[
                :, half * LANES : (half + 1) * LANES
            ]

    def turn(block, carry):
        at = pl.ds(pl.multiple_of(block * LANES, LANES), LANES)
        gated = (key_ref[at, :].astype(F32) * value_ref[at, :].astype(F32)).astype(BF16)
        turned[pl.ds(block, sizes.tokens, stride=blocks), :] = gated.astype(F32).T
        return carry

    lax.fori_loop(0, blocks, turn, 0)
    for first in range(0, blocks, 8):
        decays, gains = [], []
        for mode in range(modes):
            rate = params[pl.ds(first * rows + mode, 8, stride=rows), :]
            gains.append(params[pl.ds(first * rows + modes + mode, 8, stride=rows), :])
            decays.append(jnp.exp(-rate))
            decay_ref[mode * blocks + first : mode * blocks + first + 8, :] = decays[-1]
        for half in range(2):

            def step(token, states):
                at = (half * sizes.run + token) * blocks + first
                at = pl.ds(pl.multiple_of(at, 8), 8)
                value = turned[at, :]
                states = [a * s + c * value for a, c, s in zip(decays, gains, states)]
                conv_ref[at, :] = tree_sum(states)
                return states

            lax.fori_loop(0, sizes.run, step, [jnp.zeros((8, LANES), F32)] * modes)


def tree_sum(terms):
    while len(terms) > 1:
        terms = [
            terms[i] + terms[i + 1] if i + 1 < len(terms) else terms[i]
            for i in range(0, len(terms), 2)
        ]
    return terms[0]


def local(sizes, shard_groups, params, key_proj, value_proj):
    modes = params.shape[0] // 2
    blocks = sizes.channels // LANES
    return pl.pallas_call(
        functools.partial(local_kernel, sizes),
        in_specs=[pl.BlockSpec(memory_space=pltpu.VMEM)] * 4,
        out_shape=[
            jax.ShapeDtypeStruct((sizes.tokens * blocks, LANES), F32),
            jax.ShapeDtypeStruct((modes * blocks, LANES), F32),
        ],
        scratch_shapes=[
            pltpu.VMEM((blocks * 2 * modes, LANES), F32),
            pltpu.VMEM((sizes.tokens * blocks, LANES), F32),
        ],
        compiler_params=pltpu.CompilerParams(vmem_limit_bytes=VMEM_LIMIT),
        cost_estimate=pl.CostEstimate(flops=4 * 10**9, bytes_accessed=3 * 10**6, transcendentals=0),
        name="local_runs",
    )(shard_groups, params, key_proj, value_proj)


def owner_kernel(
    sizes,
    recv_ref,
    into_ref,
    back_ref,
    table_ref,
    leap_ref,
    out_ref,
    gated,
    weighted,
    states,
    sums,
    run_at,
):
    run, runs, own, size = sizes.run, sizes.runs, sizes.own, sizes.size
    rows = own * size
    lane = iota((rows, LANES), 1)
    mirror = hot(iota((LANES, LANES), 0) + iota((LANES, LANES), 1) == LANES - 1)
    weighted[runs : 2 * runs + 1] = jnp.zeros((runs + 1, rows, LANES), BF16)
    for source in range(sizes.ctx):
        tail = recv_ref[source * sizes.ch, sizes.cap - 16 : sizes.cap, :].astype(F32)
        ids = tail[15:16, :]
        first = jnp.max(ids[:, :LANES]).astype(I32)
        second = jnp.max(ids[:, LANES:]).astype(I32)
        run_at[2 * source] = first
        run_at[2 * source + 1] = second
        block = recv_ref[source * sizes.ch : (source + 1) * sizes.ch]
        block = block.reshape(sizes.ch * sizes.cap, 2 * LANES)
        found = dot(into_ref[...], block)
        mirrored = dot(found[:, :LANES].astype(BF16), mirror)
        swapped = pltpu.roll(mirrored, run, 1)
        gated[second] = jnp.where(lane < run, mirrored, swapped).astype(BF16)
        gated[first] = jnp.where(lane < run, swapped, mirrored).astype(BF16)
        value = found[:, LANES:]
        turned = pltpu.roll(value, run, 1).astype(BF16)
        value = value.astype(BF16)
        weighted[first + 1, :, :run] = value[:, :run]
        weighted[first, :, run:] = turned[:, run:]
        weighted[second + 1, :, :run] = turned[:, :run]
        weighted[second, :, run:] = value[:, run:]

    modes = states.shape[1]
    group_lane = lax.shift_right_logical(iota((modes, rows), 1), bits(size))
    carried = jnp.zeros((modes, rows), F32)
    leap = leap_ref[...]
    for at in range(runs):
        states[at] = carried
        if at + 1 < runs:
            ends = dot_lanes(table_ref[...], gated[at])
            total = jnp.zeros((modes, rows), F32)
            for group in range(own):
                piece = ends[group * modes : (group + 1) * modes]
                total = total + jnp.where(group_lane == group, piece, 0.0)
            carried = carried * leap + total

    seq = run * runs

    def one_group(group, carry):
        at = pl.ds(pl.multiple_of(group * size, size), size)
        left = gated[:, at, :].reshape(runs * size, LANES).T[:run]
        right = jnp.concatenate(
            [
                weighted[1 + lag : 1 + lag + runs, at, :].reshape(runs * size, LANES)
                for lag in range(0, runs, 2)
            ],
            axis=1,
        )
        gram = jnp.concatenate([dot(left, right), jnp.zeros((run, LANES), F32)], axis=1)
        skewed = pltpu.roll(gram, seq + LANES - (run - 1), 1, stride=1, stride_axis=0)
        sums[pl.ds(group, 1), :] = jnp.sum(skewed, axis=0, keepdims=True)[:, :seq]
        return carry

    lax.fori_loop(0, own, one_group, 0, unroll=True)

    each = sizes.each
    quarter = LANES // 4
    out_lane = iota((32, LANES), 1)
    for target in range(sizes.ctx):
        pair = jnp.concatenate(
            [states[run_at[2 * target]], states[run_at[2 * target + 1]]], axis=0
        )
        sent = dot(pair.astype(BF16), back_ref[...])
        lags = sums[:, target * LANES : (target + 1) * LANES]
        high = lags.astype(BF16).astype(F32)
        low = lags - high
        moved = [
            [pltpu.roll(term, (7 * quarter - q * quarter) % LANES, 1) for q in range(4)]
            for term in (high, low)
        ]
        for chan in range(sizes.ch):
            lag_rows = jnp.concatenate(
                [part[chan * each : (chan + 1) * each] for term in moved for part in term], axis=0
            )
            mine = sent[:, chan * LANES : (chan + 1) * LANES]
            out_ref[target * sizes.ch + chan] = jnp.where(
                out_lane < 3 * quarter, mine, lag_rows
            ).astype(BF16)


def owner(sizes, recv, into, back, table, leap):
    rows = sizes.own * sizes.size
    modes = leap.shape[0]
    return pl.pallas_call(
        functools.partial(owner_kernel, sizes),
        in_specs=[pl.BlockSpec(memory_space=pltpu.VMEM)] * 5,
        out_shape=jax.ShapeDtypeStruct((sizes.peers, 2 * modes, LANES), BF16),
        scratch_shapes=[
            pltpu.VMEM((sizes.runs, rows, LANES), BF16),
            pltpu.VMEM((2 * sizes.runs + 1, rows, LANES), BF16),
            pltpu.VMEM((sizes.runs, modes, rows), F32),
            pltpu.VMEM((sizes.own, sizes.run * sizes.runs), F32),
            pltpu.SMEM((sizes.runs,), I32),
        ],
        compiler_params=pltpu.CompilerParams(vmem_limit_bytes=VMEM_LIMIT),
        name="owner_sums",
    )(recv, into, back, table, leap)


def finish_kernel(
    sizes, recv_ref, dest_ref, conv_ref, decay_ref, query_ref, out_ref, grad_ref, found, total
):
    blocks = sizes.channels // LANES
    rows = recv_ref.shape[1]
    modes = rows // 2
    everything = recv_ref[...].reshape(sizes.peers * rows, LANES)

    def fetch(part, carry):
        at = pl.ds(pl.multiple_of(part * 256, 256), 256)
        owner, slot = dest_ref[1:2, at], dest_ref[2:3, at]
        chosen = hot(iota((LANES, 256), 0) == slot)
        picked = dot(everything, chosen)
        mine = jnp.zeros((rows, 256), F32)
        for peer in range(sizes.peers):
            mine = mine + jnp.where(owner == peer, picked[peer * rows : (peer + 1) * rows], 0.0)
        for half in range(2):
            start = pl.multiple_of((2 * part + half) * rows, rows)
            found[pl.ds(start, rows), :] = mine[:, half * LANES : (half + 1) * LANES]
        return carry

    lax.fori_loop(0, sizes.channels // 256, fetch, 0, unroll=True)
    for first in range(0, blocks, 8):
        decays = [
            decay_ref[mode * blocks + first : mode * blocks + first + 8, :]
            for mode in range(modes)
        ]
        for half in range(2):
            states = [
                found[pl.ds(first * rows + half * modes + mode, 8, stride=rows), :]
                for mode in range(modes)
            ]

            def step(token, states):
                at = (half * sizes.run + token) * blocks + first
                at = pl.ds(pl.multiple_of(at, 8), 8)
                states = [a * s for a, s in zip(decays, states)]
                total[at, :] = conv_ref[at, :] + tree_sum(states)
                return states

            lax.fori_loop(0, sizes.run, step, states, unroll=8)

    def turn(block, carry):
        at = pl.ds(pl.multiple_of(block * LANES, LANES), LANES)
        conv = total[pl.ds(block, sizes.tokens, stride=blocks), :].T.astype(BF16)
        out_ref[at, :] = (query_ref[at, :].astype(F32) * conv.astype(F32)).astype(BF16)
        return carry

    lax.fori_loop(0, blocks, turn, 0, unroll=True)

    each, quarter = sizes.each, LANES // 4
    high_low = recv_ref[...].astype(F32)
    terms = []
    lane_part = lax.shift_right_logical(iota((sizes.peers * 16, LANES), 1), 5)
    row = iota((sizes.peers * 16, LANES), 0)
    row_part = lax.shift_right_logical(row & 15, bits(each))
    for term in range(2):
        piece = high_low[:, term * 16 : (term + 1) * 16, :].reshape(sizes.peers * 16, LANES)
        placed = jnp.zeros((sizes.peers * 16, LANES), F32)
        for part in range(4):
            moved = pltpu.roll(piece, (part * quarter + quarter) % LANES, 1)
            placed = jnp.where((row_part == part) & (lane_part == part), moved, placed)
        terms.append(placed.astype(BF16))
    come = iota((1, sizes.peers * 16), 1)
    seat = lax.shift_right_logical(come, 4) * each + (come & (each - 1))
    wanted = sizes.group_at(seat, way_of(dest_ref))
    chosen = hot(iota((sizes.block, sizes.peers * 16), 0) == wanted)
    grad_ref[...] = dot(chosen, terms[0]) + dot(chosen, terms[1])


def finish(sizes, recv, dest, conv, decay, query_proj):
    blocks = sizes.channels // LANES
    return pl.pallas_call(
        functools.partial(finish_kernel, sizes),
        in_specs=[pl.BlockSpec(memory_space=pltpu.VMEM)] * 5,
        out_shape=[
            jax.ShapeDtypeStruct((sizes.channels, sizes.tokens), BF16),
            jax.ShapeDtypeStruct((sizes.block, LANES), F32),
        ],
        scratch_shapes=[
            pltpu.VMEM((blocks * recv.shape[1], LANES), F32),
            pltpu.VMEM((sizes.tokens * blocks, LANES), F32),
        ],
        compiler_params=pltpu.CompilerParams(vmem_limit_bytes=VMEM_LIMIT),
        name="finish_rows",
    )(recv, dest, conv, decay, query_proj)


def exchange(blocks):
    return lax.all_to_all(blocks, ("ctx", "ch"), split_axis=0, concat_axis=0, tiled=True)


def owners_way(sizes, args):
    query_proj, key_proj, value_proj, cotangent, positions, group_of, decay_rates, residues = args
    ch_rank = lax.axis_index("ch")
    me = lax.axis_index("ctx") * sizes.ch + ch_rank
    all_groups = group_of.reshape(sizes.ch, sizes.channels)
    shard_groups = lax.dynamic_slice_in_dim(all_groups, ch_rank, 1)
    sent, dest = pack(
        sizes,
        positions,
        jnp.asarray(sizes.deal()),
        all_groups,
        shard_groups,
        key_proj,
        value_proj,
        cotangent,
        query_proj,
    )
    recv = exchange(sent)

    gains = residues * jnp.sqrt(2.0 * decay_rates)
    params = jnp.concatenate([decay_rates, gains], axis=1).T
    conv, decay = local(sizes, shard_groups, params, key_proj, value_proj)
    into, back, most, table, leap = index(
        sizes, me.reshape(1).astype(I32), all_groups, dest, params
    )

    def fast(recv, into, back, table, leap, dest, conv, decay, *args):
        returned = exchange(owner(sizes, recv, into, back, table, leap))
        return tuple(finish(sizes, returned, dest, conv, decay, args[0]))

    def slow(recv, into, back, table, leap, dest, conv, decay, *args):
        return general_way(*args)

    return lax.cond(
        most[0, 0] <= sizes.cap - 1,
        fast,
        slow,
        recv,
        into,
        back,
        table,
        leap,
        dest,
        conv,
        decay,
        *args,
    )


def shards(*args):
    sizes = Sizes(
        lax.axis_size("ctx"), lax.axis_size("ch"), *args[0].shape, args[6].shape[0]
    )
    if not sizes.fits:
        return general_way(*args)
    return owners_way(sizes, args)


def solution(mesh):
    placed = (
        P("ch", "ctx"),
        P("ch", "ctx"),
        P("ch", "ctx"),
        P("ch", "ctx"),
        P("ctx"),
        P(),
        P(),
        P(),
    )
    return jax.shard_map(
        shards,
        mesh=mesh,
        in_specs=placed,
        out_specs=(P("ch", "ctx"), P("ch", "ctx")),
        check_vma=False,
    )
```

```python
import functools
import math

import jax
import jax.numpy as jnp
from jax import lax
from jax.experimental import pallas as pl
from jax.experimental.pallas import tpu as pltpu
from jax.sharding import PartitionSpec as P

F32 = jnp.float32
BF16 = jnp.bfloat16
I32 = jnp.int32
LANES = 128
VMEM_LIMIT = 48 * 1024 * 1024


def product(form, left, right):
    return jnp.einsum(form, left, right, precision=lax.Precision.HIGHEST)


def split_rows(extent):
    chosen = 2
    for divisor in range(2, math.isqrt(extent) + 1, 2):
        if extent % divisor == 0:
            chosen = divisor
    return chosen


def dft_tables(row_count, col_count, extent):
    row_index = jnp.arange(row_count, dtype=jnp.int32)
    col_index = jnp.arange(col_count, dtype=jnp.int32)

    def angles(left_index, right_index, modulus):
        phase = left_index[:, None] * right_index[None, :] % modulus
        return phase.astype(jnp.float32) * (2.0 * math.pi / modulus)

    row_angle = angles(row_index, row_index, row_count)
    col_angle = angles(col_index, col_index, col_count)
    twist_angle = angles(row_index, col_index, extent)
    return (
        jnp.cos(row_angle),
        jnp.sin(row_angle),
        jnp.cos(col_angle),
        jnp.sin(col_angle),
        jnp.cos(twist_angle),
        jnp.sin(twist_angle),
    )


def forward_transform(signal, tables, row_count, col_count):
    row_cos, row_sin, col_cos, col_sin, twist_cos, twist_sin = tables
    folded = signal.reshape(signal.shape[0], row_count // 2, col_count)
    mid_real = product("ka,cab->ckb", row_cos[:, : row_count // 2], folded)
    mid_imag = -product("ka,cab->ckb", row_sin[:, : row_count // 2], folded)
    turned_real = mid_real * twist_cos + mid_imag * twist_sin
    turned_imag = mid_imag * twist_cos - mid_real * twist_sin
    spec_real = product("ckb,bm->ckm", turned_real, col_cos) + product(
        "ckb,bm->ckm", turned_imag, col_sin
    )
    spec_imag = product("ckb,bm->ckm", turned_imag, col_cos) - product(
        "ckb,bm->ckm", turned_real, col_sin
    )
    return (spec_real, spec_imag)


def inverse_transform(spec_real, spec_imag, tables, row_count, col_count):
    row_cos, row_sin, col_cos, col_sin, twist_cos, twist_sin = tables
    mid_real = product("ckm,bm->ckb", spec_real, col_cos) - product(
        "ckm,bm->ckb", spec_imag, col_sin
    )
    mid_imag = product("ckm,bm->ckb", spec_imag, col_cos) + product(
        "ckm,bm->ckb", spec_real, col_sin
    )
    turned_real = mid_real * twist_cos - mid_imag * twist_sin
    turned_imag = mid_imag * twist_cos + mid_real * twist_sin
    folded = product("ak,ckb->cab", row_cos[: row_count // 2, :], turned_real) - product(
        "ak,ckb->cab", row_sin[: row_count // 2, :], turned_imag
    )
    return folded.reshape(spec_real.shape[0], -1) / float(row_count * col_count)


def spectra(gated_seq, weighted_seq, chan_groups, decay_rates, residues, seq_length):
    extent = 2 * seq_length
    row_count = split_rows(extent)
    col_count = extent // row_count
    decay_rows = decay_rates[chan_groups]
    gain_rows = residues[chan_groups]
    tap_index = jnp.arange(seq_length, dtype=jnp.float32)
    coefs = gain_rows * jnp.sqrt(2.0 * decay_rows)
    filters = jnp.sum(coefs[:, :, None] * jnp.exp(-decay_rows[:, :, None] * tap_index), axis=1)
    tables = dft_tables(row_count, col_count, extent)
    gated_real, gated_imag = forward_transform(
        gated_seq.astype(jnp.float32), tables, row_count, col_count
    )
    filter_real, filter_imag = forward_transform(filters, tables, row_count, col_count)
    weight_real, weight_imag = forward_transform(
        weighted_seq.astype(jnp.float32), tables, row_count, col_count
    )
    convolved = inverse_transform(
        filter_real * gated_real - filter_imag * gated_imag,
        filter_real * gated_imag + filter_imag * gated_real,
        tables,
        row_count,
        col_count,
    )
    lagged = inverse_transform(
        weight_real * gated_real + weight_imag * gated_imag,
        weight_imag * gated_real - weight_real * gated_imag,
        tables,
        row_count,
        col_count,
    )
    return (convolved, lagged)


def general_way(
    query_proj, key_proj, value_proj, cotangent, positions, group_of, decay_rates, residues
):
    ctx_count = lax.axis_size("ctx")
    ch_count = lax.axis_size("ch")
    ctx_rank = lax.axis_index("ctx")
    ch_rank = lax.axis_index("ch")
    local_channels, local_tokens = query_proj.shape
    half_run = local_tokens // 2
    run_count = 2 * ctx_count
    seq_length = local_tokens * ctx_count
    per_device = local_channels // ctx_count
    groups_total = decay_rates.shape[0]
    gated = (key_proj.astype(jnp.float32) * value_proj.astype(jnp.float32)).astype(jnp.bfloat16)
    weighted = (cotangent.astype(jnp.float32) * query_proj.astype(jnp.float32)).astype(jnp.bfloat16)
    run_ids = jnp.stack([positions[0], positions[half_run]]) // half_run
    all_runs = lax.all_to_all(
        jnp.broadcast_to(run_ids[None, :], (ctx_count, 2)),
        "ctx",
        split_axis=0,
        concat_axis=0,
        tiled=True,
    ).reshape(run_count)
    source_run = (
        jnp.zeros((run_count,), jnp.int32).at[all_runs].set(jnp.arange(run_count, dtype=jnp.int32))
    )

    def to_sequence(stored):
        return stored.reshape(per_device, run_count, half_run)[:, source_run, :].reshape(
            per_device, seq_length
        )

    shard_groups = lax.dynamic_slice_in_dim(group_of, ch_rank * local_channels, local_channels)
    gated_cols, weighted_cols = (
        lax.all_to_all(gated, "ctx", split_axis=0, concat_axis=1, tiled=True),
        lax.all_to_all(weighted, "ctx", split_axis=0, concat_axis=1, tiled=True),
    )
    first_channel = ch_rank * local_channels + ctx_rank * per_device
    chan_groups = lax.dynamic_slice_in_dim(group_of, first_channel, per_device)
    convolved, lagged = spectra(
        to_sequence(gated_cols),
        to_sequence(weighted_cols),
        chan_groups,
        decay_rates,
        residues,
        seq_length,
    )
    ordered = convolved.astype(jnp.bfloat16).reshape(per_device, run_count, half_run)[
        :, all_runs, :
    ]
    conv_tokens = lax.all_to_all(
        ordered.reshape(per_device, seq_length), "ctx", split_axis=1, concat_axis=0, tiled=True
    )
    output = (query_proj.astype(jnp.float32) * conv_tokens.astype(jnp.float32)).astype(jnp.bfloat16)
    lag_rows = lax.all_to_all(lagged, "ctx", split_axis=1, concat_axis=0, tiled=True)
    select_all = (
        jnp.arange(groups_total, dtype=jnp.int32)[:, None] == shard_groups[None, :]
    ).astype(jnp.float32)
    partial = jnp.dot(
        select_all, lag_rows, precision=lax.Precision.HIGHEST, preferred_element_type=jnp.float32
    ).reshape(ch_count, groups_total // ch_count, local_tokens)
    filter_grad = jnp.sum(
        lax.all_to_all(partial, "ch", split_axis=0, concat_axis=0, tiled=True), axis=0
    )
    return (output, filter_grad)


def iota(shape, dim):
    return lax.broadcasted_iota(I32, shape, dim)


def hot(flags):
    return jnp.where(flags, 1.0, 0.0).astype(BF16)


def dot(left, right):
    return jnp.dot(left, right, preferred_element_type=F32)


def dot_lanes(left, right):
    return lax.dot_general(left, right, (((1,), (1,)), ((), ())), preferred_element_type=F32)


def two_terms(values):
    high = values.astype(BF16)
    return high, (values - high.astype(F32)).astype(BF16)


class Sizes:
    def __init__(self, ctx, ch, channels, tokens, groups):
        self.ctx, self.ch = ctx, ch
        self.peers = ctx * ch
        self.channels = channels
        self.tokens = tokens
        self.run = tokens // 2
        self.runs = 2 * ctx
        self.groups = groups
        self.block = groups // ch
        self.each = self.block // self.peers
        self.own = groups // self.peers
        self.size = channels * ch // groups
        self.cap = 80
        powers = [self.block, max(self.each, 1), self.own, self.size]
        self.fits = (
            tokens == LANES
            and self.block == LANES
            and self.runs == 16
            and self.own == 16
            and self.size == 16
            and self.each * self.peers == self.block
            and self.each * 8 * self.run == 16 * LANES
            and ch == 4
            and channels % 2048 == 0
            and channels // self.peers <= 64
            and all(p & (p - 1) == 0 for p in powers)
        )

    def deal(self, count):
        way = iota((1, count), 1)
        step = 2 * lax.shift_right_logical(way, 1) + 1
        turn = step
        for _ in range(3):
            turn = (turn * (2 - step * turn)) & (self.block - 1)
        return turn, (self.each // 2) * (way & 1), step

    def seat(self, group, way):
        turn, start, _ = way
        return (turn * (group & (self.block - 1)) + start) & (self.block - 1)

    def owner(self, group, way):
        return lax.shift_right_logical(self.seat(group, way), bits(self.each))

    def place(self, group, way):
        block = lax.shift_right_logical(group, bits(self.block))
        return block * self.each + (self.seat(group, way) & (self.each - 1))

    def group_at(self, seat, way):
        _, start, step = way
        return (step * (seat - start)) & (self.block - 1)

    def group_here(self, place, me, way):
        block = lax.shift_right_logical(place, bits(self.each))
        seat = me * self.each + (place & (self.each - 1))
        return block * self.block + self.group_at(seat, way)


def bits(power):
    return power.bit_length() - 1


def way_of(dest_ref):
    return tuple(dest_ref[row : row + 1, 0:1] for row in (3, 4, 5))


def running_counts(marks, upper):
    width = upper.shape[0]
    before, counts = jnp.zeros((marks.shape[0], 1), F32), []
    for start in range(0, marks.shape[1], width):
        part = marks[:, start : start + width]
        counts.append(dot(part, upper) + before)
        before = before + jnp.sum(part.astype(F32), axis=1, keepdims=True)
    return jnp.concatenate(counts, axis=1), before


def upper_ones(width):
    return hot(iota((width, width), 0) < iota((width, width), 1))


def choose_way(sizes, group):
    count = 64
    ways = sizes.deal(count)
    low = 16
    group = group & (sizes.block - 1)
    loads = []
    for source in range(sizes.ch):
        row = group[:, source * sizes.channels : (source + 1) * sizes.channels]
        high_hot = hot(iota((sizes.block // low, sizes.channels), 0) == lax.shift_right_logical(row, 4))
        low_hot = hot(iota((low, sizes.channels), 0) == (row & (low - 1)))
        table = dot_lanes(high_hot, low_hot)
        spread = hot((iota((low, sizes.block), 1) & (low - 1)) == iota((low, sizes.block), 0))
        wide = dot(table.astype(BF16), spread)
        own = lax.shift_right_logical(iota(wide.shape, 1), 4) == iota(wide.shape, 0)
        loads.append(jnp.sum(jnp.where(own, wide, 0.0), axis=0, keepdims=True))
    loads = jnp.concatenate(loads + [jnp.zeros((8 - sizes.ch, sizes.block), F32)], axis=0)
    lanes = sizes.peers * count
    spread = [jnp.concatenate([part] * sizes.peers, axis=1) for part in ways]
    seat = sizes.seat(iota((sizes.block, lanes), 0), spread)
    peer = lax.shift_right_logical(iota((1, lanes), 1), bits(count))
    dealt = hot(lax.shift_right_logical(seat, bits(sizes.each)) == peer)
    sums = dot(loads.astype(BF16), dealt)
    fullest = sums[:, :LANES]
    for start in range(LANES, lanes, LANES):
        fullest = jnp.maximum(fullest, sums[:, start : start + LANES])
    fullest = jnp.max(jnp.maximum(fullest, pltpu.roll(fullest, count, 1)), axis=0, keepdims=True)
    score = fullest[:, :count] * float(count) + iota((1, count), 1).astype(F32)
    best = jnp.min(score, axis=1, keepdims=True)
    return tuple(
        jnp.sum(jnp.where(score == best, part.astype(F32), 0.0), axis=1, keepdims=True).astype(I32)
        for part in ways
    )


def pack_kernel(
    sizes,
    place_hbm,
    group_hbm,
    key_hbm,
    value_hbm,
    cot_hbm,
    query_hbm,
    out_ref,
    dest_ref,
    place_ref,
    group_ref,
    inputs,
    data,
    arrived,
):
    part = out_ref.shape[0]

    @pl.when(pl.program_id(0) == 0)
    def _():
        moves = [(group_hbm, group_ref), (place_hbm, place_ref)]
        for at, source in enumerate((key_hbm, value_hbm, cot_hbm, query_hbm)):
            moves.append((source, inputs.at[at]))
        copies = [
            pltpu.make_async_copy(source, target, arrived.at[at])
            for at, (source, target) in enumerate(moves)
        ]
        for copy in copies:
            copy.start()
        copies[0].wait()
        way = choose_way(sizes, group_ref[...])
        first = pl.multiple_of(lax.axis_index("ch") * sizes.channels, LANES)
        owner = sizes.owner(group_ref[:, pl.ds(first, sizes.channels)], way)
        marks = iota((sizes.peers, sizes.channels), 0) == owner
        counts, _ = running_counts(hot(marks), upper_ones(256))
        slot = jnp.sum(jnp.where(marks, counts, 0.0), axis=0, keepdims=True).astype(I32)
        dest_ref[0:1, :] = jnp.where(slot < sizes.cap - 1, owner * sizes.cap + slot, -1)
        dest_ref[1:2, :] = owner
        dest_ref[2:3, :] = slot
        for row in range(3):
            dest_ref[3 + row : 4 + row, :] = jnp.broadcast_to(way[row], (1, sizes.channels))
        dest_ref[6:8, :] = jnp.zeros((2, sizes.channels), I32)
        for copy in copies[1:]:
            copy.wait()
        across = iota((LANES, LANES), 0) ^ iota((LANES, LANES), 1)
        gated = (inputs[0].astype(F32) * inputs[1].astype(F32)).astype(BF16)
        data[:, :LANES] = dot(gated, hot(across == sizes.run - 1)).astype(BF16)
        data[:, LANES:] = (inputs[2].astype(F32) * inputs[3].astype(F32)).astype(BF16)

    shift = bits(sizes.run)
    first = lax.shift_right_logical(place_ref[0], shift)
    second = lax.shift_right_logical(place_ref[sizes.run], shift)
    run_row = jnp.where(iota((1, 1, 2 * LANES), 2) < LANES, first, second).astype(F32)
    base = pl.program_id(0) * part * sizes.cap
    chosen = hot(iota((part * sizes.cap, sizes.channels), 0) == dest_ref[0:1, :] - base)
    rows = dot(chosen, data[...]).reshape(part, sizes.cap, 2 * LANES)
    spare = iota((part, sizes.cap, 1), 1) == sizes.cap - 1
    out_ref[...] = jnp.where(spare, run_row, rows).astype(BF16)


def pack(sizes, positions, groups, key_proj, value_proj, cotangent, query_proj):
    part = 16
    return pl.pallas_call(
        functools.partial(pack_kernel, sizes),
        grid=(sizes.peers // part,),
        in_specs=[pl.BlockSpec(memory_space=pl.ANY)] * 6,
        out_specs=[
            pl.BlockSpec((part, sizes.cap, 2 * LANES), lambda step: (step, 0, 0)),
            pl.BlockSpec((8, sizes.channels), lambda step: (0, 0)),
        ],
        out_shape=[
            jax.ShapeDtypeStruct((sizes.peers, sizes.cap, 2 * LANES), BF16),
            jax.ShapeDtypeStruct((8, sizes.channels), I32),
        ],
        scratch_shapes=[
            pltpu.SMEM(positions.shape, I32),
            pltpu.VMEM(groups.shape, I32),
            pltpu.VMEM((4, sizes.channels, sizes.tokens), BF16),
            pltpu.VMEM((sizes.channels, 2 * LANES), BF16),
            pltpu.SemaphoreType.DMA((6,)),
        ],
        compiler_params=pltpu.CompilerParams(vmem_limit_bytes=VMEM_LIMIT),
        name="pack_rows",
    )(positions, groups, key_proj, value_proj, cotangent, query_proj)


def index_kernel(
    sizes,
    me_ref,
    group_ref,
    dest_ref,
    param_ref,
    into_ref,
    back_ref,
    over_ref,
    table_ref,
    leap_ref,
):
    me = me_ref[0]
    way = way_of(dest_ref)
    upper = upper_ones(256)
    group = group_ref[...]
    owner, place = sizes.owner(group, way), sizes.place(group, way)
    owner, place = jnp.split(owner, sizes.ch, axis=1), jnp.split(place, sizes.ch, axis=1)
    most = jnp.zeros((sizes.peers, 1), F32)
    for source in range(sizes.ch):
        marks = iota((sizes.peers, sizes.channels), 0) == owner[source]
        most = jnp.maximum(most, jnp.sum(jnp.where(marks, 1.0, 0.0), axis=1, keepdims=True))
    over_ref[...] = jnp.broadcast_to(jnp.max(most, axis=0, keepdims=True), (8, LANES)).astype(I32)

    earlier = jnp.zeros((sizes.own, 1), F32)
    into = jnp.zeros((256, sizes.ch * sizes.cap), F32)
    for source in range(sizes.ch):
        mine = owner[source] == me
        where = jnp.where(mine, place[source], -1)
        marks = iota((sizes.own, sizes.channels), 0) == where
        counts, totals = running_counts(hot(marks), upper)
        slot = jnp.sum(counts, axis=0, keepdims=True).astype(I32)
        nth = jnp.sum(jnp.where(marks, counts + earlier, 0.0), axis=0, keepdims=True).astype(I32)
        earlier = earlier + totals
        row = jnp.where(mine, where * sizes.size + nth, -1)
        column = jnp.where(mine & (slot < sizes.cap - 1), slot, -1)
        to_row = hot(iota((256, sizes.channels), 0) == row)
        to_column = hot(iota((LANES, sizes.channels), 0) == column)
        found = dot_lanes(to_row, to_column).astype(BF16)
        back_ref[:, source * LANES : (source + 1) * LANES] = found
        shape = (LANES, sizes.ch * sizes.cap)
        moved = hot(
            (iota(shape, 1) == iota(shape, 0) + source * sizes.cap)
            & (iota(shape, 0) < sizes.cap)
        )
        into = into + dot(found, moved)
    into_ref[...] = into.astype(BF16)

    modes = leap_ref.shape[0]
    terms = three_terms(param_ref[...])
    shape = (256, sizes.groups)
    wanted = sizes.group_here(lax.shift_right_logical(iota((256, 1), 0), bits(modes)), me, way)
    found = dot_lanes(hot(iota(shape, 1) == wanted), terms)
    found = three_sum(found, 1)
    mode = iota((256, 2 * modes), 0) & (modes - 1)
    lane = iota((256, 2 * modes), 1)
    rate = jnp.sum(jnp.where(lane == mode, found, 0.0), axis=1, keepdims=True)
    gain = jnp.sum(jnp.where(lane == mode + modes, found, 0.0), axis=1, keepdims=True)
    step = iota((256, sizes.run), 1).astype(F32)
    high, low = two_terms(gain * jnp.exp(-rate * step))
    table_ref[...] = jnp.concatenate([high, low], axis=1)
    shape = (sizes.groups, 256)
    wanted = sizes.group_here(lax.shift_right_logical(iota((1, 256), 1), bits(sizes.size)), me, way)
    found = three_sum(dot(terms, hot(iota(shape, 0) == wanted)), 0)
    leap_ref[...] = jnp.exp(found[:modes] * -float(sizes.run))


def three_terms(exact):
    high, rest = two_terms(exact)
    low, _ = two_terms(exact - high.astype(F32) - rest.astype(F32))
    return jnp.concatenate([high, rest, low], axis=0)


def three_sum(found, dim):
    high, rest, low = jnp.split(found, 3, axis=dim)
    return high + rest + low


def index(sizes, me, groups, dest, params):
    modes = params.shape[0] // 2
    return pl.pallas_call(
        functools.partial(index_kernel, sizes),
        in_specs=[pl.BlockSpec(memory_space=pltpu.SMEM)]
        + [pl.BlockSpec(memory_space=pltpu.VMEM)] * 3,
        out_shape=[
            jax.ShapeDtypeStruct((256, sizes.ch * sizes.cap), BF16),
            jax.ShapeDtypeStruct((256, sizes.ch * LANES), BF16),
            jax.ShapeDtypeStruct((8, LANES), I32),
            jax.ShapeDtypeStruct((256, 2 * sizes.run), BF16),
            jax.ShapeDtypeStruct((modes, 256), F32),
        ],
        compiler_params=pltpu.CompilerParams(vmem_limit_bytes=VMEM_LIMIT),
        cost_estimate=pl.CostEstimate(flops=2 * 10**9, bytes_accessed=10**6, transcendentals=0),
        name="index_rows",
    )(me, groups, dest, params)


def local_kernel(
    sizes, me_ref, group_ref, param_ref, key_ref, value_ref, conv_ref, decay_ref, params, turned
):
    modes = param_ref.shape[0] // 2
    blocks = sizes.channels // LANES
    stacked = three_terms(param_ref[...])
    rows = 2 * modes
    first_lane = pl.multiple_of((me_ref[0] & (sizes.ch - 1)) * sizes.channels, LANES)
    groups = group_ref[:, pl.ds(first_lane, sizes.channels)]
    for start in range(0, sizes.channels, 256):
        chosen = hot(iota((sizes.groups, 256), 0) == groups[:, start : start + 256])
        found = three_sum(dot(stacked, chosen), 0)
        for half in range(2):
            block = start // LANES + half
            params[block * rows : (block + 1) * rows, :] = found[
                :, half * LANES : (half + 1) * LANES
            ]

    def turn(block, carry):
        at = pl.ds(pl.multiple_of(block * LANES, LANES), LANES)
        gated = (key_ref[at, :].astype(F32) * value_ref[at, :].astype(F32)).astype(BF16)
        turned[pl.ds(block, sizes.tokens, stride=blocks), :] = gated.astype(F32).T
        return carry

    lax.fori_loop(0, blocks, turn, 0)
    for first in range(0, blocks, 8):
        decays, gains = [], []
        for mode in range(modes):
            rate = params[pl.ds(first * rows + mode, 8, stride=rows), :]
            gains.append(params[pl.ds(first * rows + modes + mode, 8, stride=rows), :])
            decays.append(jnp.exp(-rate))
            decay_ref[mode * blocks + first : mode * blocks + first + 8, :] = decays[-1]
        for half in range(2):

            def step(token, states):
                at = (half * sizes.run + token) * blocks + first
                at = pl.ds(pl.multiple_of(at, 8), 8)
                value = turned[at, :]
                states = [a * s + c * value for a, c, s in zip(decays, gains, states)]
                conv_ref[at, :] = tree_sum(states)
                return states

            lax.fori_loop(0, sizes.run, step, [jnp.zeros((8, LANES), F32)] * modes)


def tree_sum(terms):
    while len(terms) > 1:
        terms = [
            terms[i] + terms[i + 1] if i + 1 < len(terms) else terms[i]
            for i in range(0, len(terms), 2)
        ]
    return terms[0]


def local(sizes, me, groups, params, key_proj, value_proj):
    modes = params.shape[0] // 2
    blocks = sizes.channels // LANES
    return pl.pallas_call(
        functools.partial(local_kernel, sizes),
        in_specs=[pl.BlockSpec(memory_space=pltpu.SMEM)]
        + [pl.BlockSpec(memory_space=pltpu.VMEM)] * 4,
        out_shape=[
            jax.ShapeDtypeStruct((sizes.tokens * blocks, LANES), F32),
            jax.ShapeDtypeStruct((modes * blocks, LANES), F32),
        ],
        scratch_shapes=[
            pltpu.VMEM((blocks * 2 * modes, LANES), F32),
            pltpu.VMEM((sizes.tokens * blocks, LANES), F32),
        ],
        compiler_params=pltpu.CompilerParams(vmem_limit_bytes=VMEM_LIMIT),
        cost_estimate=pl.CostEstimate(flops=4 * 10**9, bytes_accessed=3 * 10**6, transcendentals=0),
        name="local_runs",
    )(me, groups, params, key_proj, value_proj)


def owner_kernel(
    sizes,
    recv_ref,
    into_ref,
    back_ref,
    table_ref,
    leap_ref,
    out_ref,
    merged,
    gated,
    weighted,
    states,
    sums,
    run_at,
):
    run, runs, own, size = sizes.run, sizes.runs, sizes.own, sizes.size
    rows = own * size
    weighted[runs : 2 * runs + 1] = jnp.zeros((runs + 1, rows, LANES), BF16)
    for source in range(sizes.ctx):
        tail = recv_ref[source * sizes.ch, sizes.cap - 16 : sizes.cap, :].astype(F32)
        run_at[2 * source] = tail[15, 0].astype(I32)
        run_at[2 * source + 1] = tail[15, LANES].astype(I32)
    lane = iota((rows, LANES), 1)
    for source in range(sizes.ctx):
        block = recv_ref[source * sizes.ch : (source + 1) * sizes.ch]
        found = dot(into_ref[...], block.reshape(sizes.ch * sizes.cap, 2 * LANES))
        value = found[:, :LANES]
        turned = pltpu.roll(value, run, 1)
        merged[source, 0] = jnp.where(lane < run, value, turned).astype(BF16)
        merged[source, 1] = jnp.where(lane < run, turned, value).astype(BF16)
        merged[source, 2] = found[:, LANES:].astype(BF16)
        merged[source, 3] = pltpu.roll(found[:, LANES:], run, 1).astype(BF16)
    for source in range(sizes.ctx):
        first, second = run_at[2 * source], run_at[2 * source + 1]
        gated[first] = merged[source, 0]
        gated[second] = merged[source, 1]
        weighted[first + 1, :, :run] = merged[source, 2, :, :run]
        weighted[first, :, run:] = merged[source, 3, :, run:]
        weighted[second + 1, :, :run] = merged[source, 3, :, :run]
        weighted[second, :, run:] = merged[source, 2, :, run:]

    modes = states.shape[1]
    group_lane = lax.shift_right_logical(iota((modes, rows), 1), bits(size))
    carried = jnp.zeros((modes, rows), F32)
    leap = leap_ref[...]
    for at in range(runs):
        states[at] = carried
        if at + 1 < runs:
            ends = dot_lanes(table_ref[...], gated[at])
            total = jnp.zeros((modes, rows), F32)
            for group in range(own):
                piece = ends[group * modes : (group + 1) * modes]
                total = total + jnp.where(group_lane == group, piece, 0.0)
            carried = carried * leap + total

    seq = run * runs

    def one_group(group, carry):
        at = pl.ds(pl.multiple_of(group * size, size), size)
        left = gated[:, at, :].reshape(runs * size, LANES).T[:run]
        right = jnp.concatenate(
            [
                weighted[1 + lag : 1 + lag + runs, at, :].reshape(runs * size, LANES)
                for lag in range(0, runs, 2)
            ],
            axis=1,
        )
        gram = jnp.concatenate([dot(left, right), jnp.zeros((run, LANES), F32)], axis=1)
        skewed = pltpu.roll(gram, seq + LANES - (run - 1), 1, stride=1, stride_axis=0)
        sums[pl.ds(group, 1), :] = jnp.sum(skewed, axis=0, keepdims=True)[:, :seq]
        return carry

    lax.fori_loop(0, own, one_group, 0, unroll=True)

    each = sizes.each
    quarter = LANES // 4
    out_lane = iota((32, LANES), 1)
    for target in range(sizes.ctx):
        pair = jnp.concatenate(
            [states[run_at[2 * target]], states[run_at[2 * target + 1]]], axis=0
        )
        sent = dot(pair.astype(BF16), back_ref[...])
        lags = sums[:, target * LANES : (target + 1) * LANES]
        high = lags.astype(BF16).astype(F32)
        low = lags - high
        moved = [
            [pltpu.roll(term, (7 * quarter - q * quarter) % LANES, 1) for q in range(4)]
            for term in (high, low)
        ]
        for chan in range(sizes.ch):
            lag_rows = jnp.concatenate(
                [part[chan * each : (chan + 1) * each] for term in moved for part in term], axis=0
            )
            mine = sent[:, chan * LANES : (chan + 1) * LANES]
            out_ref[target * sizes.ch + chan] = jnp.where(
                out_lane < 3 * quarter, mine, lag_rows
            ).astype(BF16)


def owner(sizes, recv, into, back, table, leap):
    rows = sizes.own * sizes.size
    modes = leap.shape[0]
    return pl.pallas_call(
        functools.partial(owner_kernel, sizes),
        in_specs=[pl.BlockSpec(memory_space=pltpu.VMEM)] * 5,
        out_shape=jax.ShapeDtypeStruct((sizes.peers, 2 * modes, LANES), BF16),
        scratch_shapes=[
            pltpu.VMEM((sizes.ctx, 4, rows, LANES), BF16),
            pltpu.VMEM((sizes.runs, rows, LANES), BF16),
            pltpu.VMEM((2 * sizes.runs + 1, rows, LANES), BF16),
            pltpu.VMEM((sizes.runs, modes, rows), F32),
            pltpu.VMEM((sizes.own, sizes.run * sizes.runs), F32),
            pltpu.SMEM((sizes.runs,), I32),
        ],
        compiler_params=pltpu.CompilerParams(vmem_limit_bytes=VMEM_LIMIT),
        name="owner_sums",
    )(recv, into, back, table, leap)


def finish_kernel(
    sizes, recv_ref, dest_ref, conv_ref, decay_ref, query_ref, out_ref, grad_ref, found, total
):
    blocks = sizes.channels // LANES
    rows = recv_ref.shape[1]
    modes = rows // 2
    everything = recv_ref[...].reshape(sizes.peers * rows, LANES)

    def fetch(part, carry):
        at = pl.ds(pl.multiple_of(part * 256, 256), 256)
        owner, slot = dest_ref[1:2, at], dest_ref[2:3, at]
        chosen = hot(iota((LANES, 256), 0) == slot)
        picked = dot(everything, chosen)
        mine = jnp.zeros((rows, 256), F32)
        for peer in range(sizes.peers):
            mine = mine + jnp.where(owner == peer, picked[peer * rows : (peer + 1) * rows], 0.0)
        for half in range(2):
            start = pl.multiple_of((2 * part + half) * rows, rows)
            found[pl.ds(start, rows), :] = mine[:, half * LANES : (half + 1) * LANES]
        return carry

    lax.fori_loop(0, sizes.channels // 256, fetch, 0, unroll=True)
    for first in range(0, blocks, 8):
        decays = [
            decay_ref[mode * blocks + first : mode * blocks + first + 8, :]
            for mode in range(modes)
        ]
        for half in range(2):
            states = [
                found[pl.ds(first * rows + half * modes + mode, 8, stride=rows), :]
                for mode in range(modes)
            ]

            def step(token, states):
                at = (half * sizes.run + token) * blocks + first
                at = pl.ds(pl.multiple_of(at, 8), 8)
                states = [a * s for a, s in zip(decays, states)]
                total[at, :] = conv_ref[at, :] + tree_sum(states)
                return states

            lax.fori_loop(0, sizes.run, step, states, unroll=8)

    def turn(block, carry):
        at = pl.ds(pl.multiple_of(block * LANES, LANES), LANES)
        conv = total[pl.ds(block, sizes.tokens, stride=blocks), :].T.astype(BF16)
        out_ref[at, :] = (query_ref[at, :].astype(F32) * conv.astype(F32)).astype(BF16)
        return carry

    lax.fori_loop(0, blocks, turn, 0, unroll=True)

    each, quarter = sizes.each, LANES // 4
    high_low = recv_ref[...].astype(F32)
    terms = []
    lane_part = lax.shift_right_logical(iota((sizes.peers * 16, LANES), 1), 5)
    row = iota((sizes.peers * 16, LANES), 0)
    row_part = lax.shift_right_logical(row & 15, bits(each))
    for term in range(2):
        piece = high_low[:, term * 16 : (term + 1) * 16, :].reshape(sizes.peers * 16, LANES)
        placed = jnp.zeros((sizes.peers * 16, LANES), F32)
        for part in range(4):
            moved = pltpu.roll(piece, (part * quarter + quarter) % LANES, 1)
            placed = jnp.where((row_part == part) & (lane_part == part), moved, placed)
        terms.append(placed.astype(BF16))
    come = iota((1, sizes.peers * 16), 1)
    seat = lax.shift_right_logical(come, 4) * each + (come & (each - 1))
    wanted = sizes.group_at(seat, way_of(dest_ref))
    chosen = hot(iota((sizes.block, sizes.peers * 16), 0) == wanted)
    grad_ref[...] = dot(chosen, terms[0]) + dot(chosen, terms[1])


def finish(sizes, recv, dest, conv, decay, query_proj):
    blocks = sizes.channels // LANES
    return pl.pallas_call(
        functools.partial(finish_kernel, sizes),
        in_specs=[pl.BlockSpec(memory_space=pltpu.VMEM)] * 5,
        out_shape=[
            jax.ShapeDtypeStruct((sizes.channels, sizes.tokens), BF16),
            jax.ShapeDtypeStruct((sizes.block, LANES), F32),
        ],
        scratch_shapes=[
            pltpu.VMEM((blocks * recv.shape[1], LANES), F32),
            pltpu.VMEM((sizes.tokens * blocks, LANES), F32),
        ],
        compiler_params=pltpu.CompilerParams(vmem_limit_bytes=VMEM_LIMIT),
        name="finish_rows",
    )(recv, dest, conv, decay, query_proj)


def exchange(blocks):
    return lax.all_to_all(blocks, ("ctx", "ch"), split_axis=0, concat_axis=0, tiled=True)


def owners_way(sizes, args):
    query_proj, key_proj, value_proj, cotangent, positions, group_of, decay_rates, residues = args
    me = (lax.axis_index("ctx") * sizes.ch + lax.axis_index("ch")).reshape(1).astype(I32)
    groups = group_of.reshape(1, -1)
    sent, dest = pack(sizes, positions, groups, key_proj, value_proj, cotangent, query_proj)
    recv = exchange(sent)

    gains = residues * jnp.sqrt(2.0 * decay_rates)
    params = jnp.concatenate([decay_rates, gains], axis=1).T
    conv, decay = local(sizes, me, groups, params, key_proj, value_proj)
    into, back, most, table, leap = index(sizes, me, groups, dest, params)

    def fast(recv, into, back, table, leap, dest, conv, decay, *args):
        returned = exchange(owner(sizes, recv, into, back, table, leap))
        return tuple(finish(sizes, returned, dest, conv, decay, args[0]))

    def slow(recv, into, back, table, leap, dest, conv, decay, *args):
        return general_way(*args)

    return lax.cond(
        most[0, 0] <= sizes.cap - 1,
        fast,
        slow,
        recv,
        into,
        back,
        table,
        leap,
        dest,
        conv,
        decay,
        *args,
    )


def shards(*args):
    sizes = Sizes(
        lax.axis_size("ctx"), lax.axis_size("ch"), *args[0].shape, args[6].shape[0]
    )
    if not sizes.fits:
        return general_way(*args)
    return owners_way(sizes, args)


def solution(mesh):
    placed = (
        P("ch", "ctx"),
        P("ch", "ctx"),
        P("ch", "ctx"),
        P("ch", "ctx"),
        P("ctx"),
        P(),
        P(),
        P(),
    )
    return jax.shard_map(
        shards,
        mesh=mesh,
        in_specs=placed,
        out_specs=(P("ch", "ctx"), P("ch", "ctx")),
        check_vma=False,
    )
```

```python
import functools
import math

import jax
import jax.numpy as jnp
from jax import lax
from jax.experimental import pallas as pl
from jax.experimental.pallas import tpu as pltpu
from jax.sharding import PartitionSpec as P

F32 = jnp.float32
BF16 = jnp.bfloat16
I32 = jnp.int32
LANES = 128
VMEM_LIMIT = 48 * 1024 * 1024


def product(form, left, right):
    return jnp.einsum(form, left, right, precision=lax.Precision.HIGHEST)


def split_rows(extent):
    chosen = 2
    for divisor in range(2, math.isqrt(extent) + 1, 2):
        if extent % divisor == 0:
            chosen = divisor
    return chosen


def dft_tables(row_count, col_count, extent):
    row_index = jnp.arange(row_count, dtype=jnp.int32)
    col_index = jnp.arange(col_count, dtype=jnp.int32)

    def angles(left_index, right_index, modulus):
        phase = left_index[:, None] * right_index[None, :] % modulus
        return phase.astype(jnp.float32) * (2.0 * math.pi / modulus)

    row_angle = angles(row_index, row_index, row_count)
    col_angle = angles(col_index, col_index, col_count)
    twist_angle = angles(row_index, col_index, extent)
    return (
        jnp.cos(row_angle),
        jnp.sin(row_angle),
        jnp.cos(col_angle),
        jnp.sin(col_angle),
        jnp.cos(twist_angle),
        jnp.sin(twist_angle),
    )


def forward_transform(signal, tables, row_count, col_count):
    row_cos, row_sin, col_cos, col_sin, twist_cos, twist_sin = tables
    folded = signal.reshape(signal.shape[0], row_count // 2, col_count)
    mid_real = product("ka,cab->ckb", row_cos[:, : row_count // 2], folded)
    mid_imag = -product("ka,cab->ckb", row_sin[:, : row_count // 2], folded)
    turned_real = mid_real * twist_cos + mid_imag * twist_sin
    turned_imag = mid_imag * twist_cos - mid_real * twist_sin
    spec_real = product("ckb,bm->ckm", turned_real, col_cos) + product(
        "ckb,bm->ckm", turned_imag, col_sin
    )
    spec_imag = product("ckb,bm->ckm", turned_imag, col_cos) - product(
        "ckb,bm->ckm", turned_real, col_sin
    )
    return (spec_real, spec_imag)


def inverse_transform(spec_real, spec_imag, tables, row_count, col_count):
    row_cos, row_sin, col_cos, col_sin, twist_cos, twist_sin = tables
    mid_real = product("ckm,bm->ckb", spec_real, col_cos) - product(
        "ckm,bm->ckb", spec_imag, col_sin
    )
    mid_imag = product("ckm,bm->ckb", spec_imag, col_cos) + product(
        "ckm,bm->ckb", spec_real, col_sin
    )
    turned_real = mid_real * twist_cos - mid_imag * twist_sin
    turned_imag = mid_imag * twist_cos + mid_real * twist_sin
    folded = product("ak,ckb->cab", row_cos[: row_count // 2, :], turned_real) - product(
        "ak,ckb->cab", row_sin[: row_count // 2, :], turned_imag
    )
    return folded.reshape(spec_real.shape[0], -1) / float(row_count * col_count)


def spectra(gated_seq, weighted_seq, chan_groups, decay_rates, residues, seq_length):
    extent = 2 * seq_length
    row_count = split_rows(extent)
    col_count = extent // row_count
    decay_rows = decay_rates[chan_groups]
    gain_rows = residues[chan_groups]
    tap_index = jnp.arange(seq_length, dtype=jnp.float32)
    coefs = gain_rows * jnp.sqrt(2.0 * decay_rows)
    filters = jnp.sum(coefs[:, :, None] * jnp.exp(-decay_rows[:, :, None] * tap_index), axis=1)
    tables = dft_tables(row_count, col_count, extent)
    gated_real, gated_imag = forward_transform(
        gated_seq.astype(jnp.float32), tables, row_count, col_count
    )
    filter_real, filter_imag = forward_transform(filters, tables, row_count, col_count)
    weight_real, weight_imag = forward_transform(
        weighted_seq.astype(jnp.float32), tables, row_count, col_count
    )
    convolved = inverse_transform(
        filter_real * gated_real - filter_imag * gated_imag,
        filter_real * gated_imag + filter_imag * gated_real,
        tables,
        row_count,
        col_count,
    )
    lagged = inverse_transform(
        weight_real * gated_real + weight_imag * gated_imag,
        weight_imag * gated_real - weight_real * gated_imag,
        tables,
        row_count,
        col_count,
    )
    return (convolved, lagged)


def general_way(
    query_proj, key_proj, value_proj, cotangent, positions, group_of, decay_rates, residues
):
    ctx_count = lax.axis_size("ctx")
    ch_count = lax.axis_size("ch")
    ctx_rank = lax.axis_index("ctx")
    ch_rank = lax.axis_index("ch")
    local_channels, local_tokens = query_proj.shape
    half_run = local_tokens // 2
    run_count = 2 * ctx_count
    seq_length = local_tokens * ctx_count
    per_device = local_channels // ctx_count
    groups_total = decay_rates.shape[0]
    gated = (key_proj.astype(jnp.float32) * value_proj.astype(jnp.float32)).astype(jnp.bfloat16)
    weighted = (cotangent.astype(jnp.float32) * query_proj.astype(jnp.float32)).astype(jnp.bfloat16)
    run_ids = jnp.stack([positions[0], positions[half_run]]) // half_run
    all_runs = lax.all_to_all(
        jnp.broadcast_to(run_ids[None, :], (ctx_count, 2)),
        "ctx",
        split_axis=0,
        concat_axis=0,
        tiled=True,
    ).reshape(run_count)
    source_run = (
        jnp.zeros((run_count,), jnp.int32).at[all_runs].set(jnp.arange(run_count, dtype=jnp.int32))
    )

    def to_sequence(stored):
        return stored.reshape(per_device, run_count, half_run)[:, source_run, :].reshape(
            per_device, seq_length
        )

    shard_groups = lax.dynamic_slice_in_dim(group_of, ch_rank * local_channels, local_channels)
    gated_cols, weighted_cols = (
        lax.all_to_all(gated, "ctx", split_axis=0, concat_axis=1, tiled=True),
        lax.all_to_all(weighted, "ctx", split_axis=0, concat_axis=1, tiled=True),
    )
    first_channel = ch_rank * local_channels + ctx_rank * per_device
    chan_groups = lax.dynamic_slice_in_dim(group_of, first_channel, per_device)
    convolved, lagged = spectra(
        to_sequence(gated_cols),
        to_sequence(weighted_cols),
        chan_groups,
        decay_rates,
        residues,
        seq_length,
    )
    ordered = convolved.astype(jnp.bfloat16).reshape(per_device, run_count, half_run)[
        :, all_runs, :
    ]
    conv_tokens = lax.all_to_all(
        ordered.reshape(per_device, seq_length), "ctx", split_axis=1, concat_axis=0, tiled=True
    )
    output = (query_proj.astype(jnp.float32) * conv_tokens.astype(jnp.float32)).astype(jnp.bfloat16)
    lag_rows = lax.all_to_all(lagged, "ctx", split_axis=1, concat_axis=0, tiled=True)
    select_all = (
        jnp.arange(groups_total, dtype=jnp.int32)[:, None] == shard_groups[None, :]
    ).astype(jnp.float32)
    partial = jnp.dot(
        select_all, lag_rows, precision=lax.Precision.HIGHEST, preferred_element_type=jnp.float32
    ).reshape(ch_count, groups_total // ch_count, local_tokens)
    filter_grad = jnp.sum(
        lax.all_to_all(partial, "ch", split_axis=0, concat_axis=0, tiled=True), axis=0
    )
    return (output, filter_grad)


def iota(shape, dim):
    return lax.broadcasted_iota(I32, shape, dim)


def hot(flags):
    return jnp.where(flags, 1.0, 0.0).astype(BF16)


def dot(left, right):
    return jnp.dot(left, right, preferred_element_type=F32)


def dot_lanes(left, right):
    return lax.dot_general(left, right, (((1,), (1,)), ((), ())), preferred_element_type=F32)


def two_terms(values):
    high = values.astype(BF16)
    return high, (values - high.astype(F32)).astype(BF16)


class Sizes:
    def __init__(self, ctx, ch, channels, tokens, groups):
        self.ctx, self.ch = ctx, ch
        self.peers = ctx * ch
        self.channels = channels
        self.tokens = tokens
        self.run = tokens // 2
        self.runs = 2 * ctx
        self.groups = groups
        self.block = groups // ch
        self.each = self.block // self.peers
        self.own = groups // self.peers
        self.size = channels * ch // groups
        self.cap = 80
        self.rest = LANES - self.cap
        powers = [self.block, max(self.each, 1), self.own, self.size]
        self.fits = (
            tokens == LANES
            and self.block == LANES
            and self.runs == 16
            and self.own == 16
            and self.size == 16
            and self.each * self.peers == self.block
            and self.each * 8 * self.run == 16 * LANES
            and ch == 4
            and channels % 2048 == 0
            and channels // self.peers <= 64
            and all(p & (p - 1) == 0 for p in powers)
        )

    def deal(self, count):
        way = iota((1, count), 1)
        step = 2 * lax.shift_right_logical(way, 1) + 1
        turn = step
        for _ in range(3):
            turn = (turn * (2 - step * turn)) & (self.block - 1)
        return turn, (self.each // 2) * (way & 1), step

    def seat(self, group, way):
        turn, start, _ = way
        return (turn * (group & (self.block - 1)) + start) & (self.block - 1)

    def owner(self, group, way):
        return lax.shift_right_logical(self.seat(group, way), bits(self.each))

    def place(self, group, way):
        block = lax.shift_right_logical(group, bits(self.block))
        return block * self.each + (self.seat(group, way) & (self.each - 1))

    def group_at(self, seat, way):
        _, start, step = way
        return (step * (seat - start)) & (self.block - 1)

    def group_here(self, place, me, way):
        block = lax.shift_right_logical(place, bits(self.each))
        seat = me * self.each + (place & (self.each - 1))
        return block * self.block + self.group_at(seat, way)


def bits(power):
    return power.bit_length() - 1


def way_of(dest_ref):
    return tuple(dest_ref[row : row + 1, 0:1] for row in (3, 4, 5))


def running_counts(marks, upper):
    width = upper.shape[0]
    before, counts = jnp.zeros((marks.shape[0], 1), F32), []
    for start in range(0, marks.shape[1], width):
        part = marks[:, start : start + width]
        counts.append(dot(part, upper) + before)
        before = before + jnp.sum(part.astype(F32), axis=1, keepdims=True)
    return jnp.concatenate(counts, axis=1), before


def upper_ones(width):
    return hot(iota((width, width), 0) < iota((width, width), 1))


def choose_way(sizes, group):
    count = 64
    ways = sizes.deal(count)
    low = 16
    group = group & (sizes.block - 1)
    loads = []
    for source in range(sizes.ch):
        row = group[:, source * sizes.channels : (source + 1) * sizes.channels]
        high_hot = hot(iota((sizes.block // low, sizes.channels), 0) == lax.shift_right_logical(row, 4))
        low_hot = hot(iota((low, sizes.channels), 0) == (row & (low - 1)))
        table = dot_lanes(high_hot, low_hot)
        spread = hot((iota((low, sizes.block), 1) & (low - 1)) == iota((low, sizes.block), 0))
        wide = dot(table.astype(BF16), spread)
        own = lax.shift_right_logical(iota(wide.shape, 1), 4) == iota(wide.shape, 0)
        loads.append(jnp.sum(jnp.where(own, wide, 0.0), axis=0, keepdims=True))
    loads = jnp.concatenate(loads + [jnp.zeros((8 - sizes.ch, sizes.block), F32)], axis=0)
    lanes = sizes.peers * count
    spread = [jnp.concatenate([part] * sizes.peers, axis=1) for part in ways]
    seat = sizes.seat(iota((sizes.block, lanes), 0), spread)
    peer = lax.shift_right_logical(iota((1, lanes), 1), bits(count))
    dealt = hot(lax.shift_right_logical(seat, bits(sizes.each)) == peer)
    sums = dot(loads.astype(BF16), dealt)
    fullest = sums[:, :LANES]
    for start in range(LANES, lanes, LANES):
        fullest = jnp.maximum(fullest, sums[:, start : start + LANES])
    fullest = jnp.max(jnp.maximum(fullest, pltpu.roll(fullest, count, 1)), axis=0, keepdims=True)
    score = fullest[:, :count] * float(count) + iota((1, count), 1).astype(F32)
    best = jnp.min(score, axis=1, keepdims=True)
    return tuple(
        jnp.sum(jnp.where(score == best, part.astype(F32), 0.0), axis=1, keepdims=True).astype(I32)
        for part in ways
    )


def pack_kernel(
    sizes,
    place_hbm,
    group_hbm,
    key_hbm,
    value_hbm,
    cot_hbm,
    query_hbm,
    out_ref,
    dest_ref,
    place_ref,
    group_ref,
    inputs,
    data,
    arrived,
):
    moves = [(group_hbm, group_ref), (place_hbm, place_ref)]
    for at, source in enumerate((key_hbm, value_hbm, cot_hbm, query_hbm)):
        moves.append((source, inputs.at[at]))
    copies = [
        pltpu.make_async_copy(source, target, arrived.at[at])
        for at, (source, target) in enumerate(moves)
    ]
    for copy in copies:
        copy.start()
    copies[0].wait()
    way = choose_way(sizes, group_ref[...])
    first = pl.multiple_of(lax.axis_index("ch") * sizes.channels, LANES)
    owner = sizes.owner(group_ref[:, pl.ds(first, sizes.channels)], way)
    marks = iota((sizes.peers, sizes.channels), 0) == owner
    counts, _ = running_counts(hot(marks), upper_ones(256))
    slot = jnp.sum(jnp.where(marks, counts, 0.0), axis=0, keepdims=True).astype(I32)
    dest_ref[0:1, :] = jnp.where(slot < sizes.cap - 1, owner * sizes.cap + slot, -1)
    dest_ref[1:2, :] = owner
    dest_ref[2:3, :] = slot
    for row in range(3):
        dest_ref[3 + row : 4 + row, :] = jnp.broadcast_to(way[row], (1, sizes.channels))
    dest_ref[6:8, :] = jnp.zeros((2, sizes.channels), I32)
    for copy in copies[1:]:
        copy.wait()
    across = iota((LANES, LANES), 0) ^ iota((LANES, LANES), 1)
    gated = (inputs[0].astype(F32) * inputs[1].astype(F32)).astype(BF16)
    data[:, :LANES] = dot(gated, hot(across == sizes.run - 1)).astype(BF16)
    data[:, LANES:] = (inputs[2].astype(F32) * inputs[3].astype(F32)).astype(BF16)

    shift = bits(sizes.run)
    first = lax.shift_right_logical(place_ref[0], shift)
    second = lax.shift_right_logical(place_ref[sizes.run], shift)
    run_row = jnp.where(iota((1, 1, 2 * LANES), 2) < LANES, first, second).astype(F32)
    part = 16
    spare = iota((part, sizes.cap, 1), 1) == sizes.cap - 1
    for start in range(0, sizes.peers, part):
        base = start * sizes.cap
        chosen = hot(iota((part * sizes.cap, sizes.channels), 0) == dest_ref[0:1, :] - base)
        rows = dot(chosen, data[...]).reshape(part, sizes.cap, 2 * LANES)
        out_ref[start : start + part] = jnp.where(spare, run_row, rows).astype(BF16)


def pack(sizes, positions, groups, key_proj, value_proj, cotangent, query_proj):
    return pl.pallas_call(
        functools.partial(pack_kernel, sizes),
        in_specs=[pl.BlockSpec(memory_space=pl.ANY)] * 6,
        out_specs=[pl.BlockSpec(memory_space=pltpu.VMEM)] * 2,
        out_shape=[
            jax.ShapeDtypeStruct((sizes.peers, sizes.cap, 2 * LANES), BF16),
            jax.ShapeDtypeStruct((8, sizes.channels), I32),
        ],
        scratch_shapes=[
            pltpu.SMEM(positions.shape, I32),
            pltpu.VMEM(groups.shape, I32),
            pltpu.VMEM((4, sizes.channels, sizes.tokens), BF16),
            pltpu.VMEM((sizes.channels, 2 * LANES), BF16),
            pltpu.SemaphoreType.DMA((6,)),
        ],
        compiler_params=pltpu.CompilerParams(vmem_limit_bytes=VMEM_LIMIT),
        name="pack_rows",
    )(positions, groups, key_proj, value_proj, cotangent, query_proj)


def index_kernel(
    sizes,
    me_ref,
    group_ref,
    dest_ref,
    param_ref,
    into_ref,
    back_ref,
    over_ref,
    table_ref,
    leap_ref,
):
    me = me_ref[0]
    way = way_of(dest_ref)
    upper = upper_ones(256)
    group = group_ref[...]
    owner, place = sizes.owner(group, way), sizes.place(group, way)
    owner, place = jnp.split(owner, sizes.ch, axis=1), jnp.split(place, sizes.ch, axis=1)
    most = jnp.zeros((sizes.peers, 1), F32)
    for source in range(sizes.ch):
        marks = iota((sizes.peers, sizes.channels), 0) == owner[source]
        most = jnp.maximum(most, jnp.sum(jnp.where(marks, 1.0, 0.0), axis=1, keepdims=True))
    over_ref[...] = jnp.broadcast_to(jnp.max(most, axis=0, keepdims=True), (8, LANES)).astype(I32)

    earlier = jnp.zeros((sizes.own, 1), F32)
    into = jnp.zeros((256, sizes.ch * sizes.cap), F32)
    for source in range(sizes.ch):
        mine = owner[source] == me
        where = jnp.where(mine, place[source], -1)
        marks = iota((sizes.own, sizes.channels), 0) == where
        counts, totals = running_counts(hot(marks), upper)
        slot = jnp.sum(counts, axis=0, keepdims=True).astype(I32)
        nth = jnp.sum(jnp.where(marks, counts + earlier, 0.0), axis=0, keepdims=True).astype(I32)
        earlier = earlier + totals
        row = jnp.where(mine, where * sizes.size + nth, -1)
        column = jnp.where(mine & (slot < sizes.cap - 1), slot, -1)
        to_row = hot(iota((256, sizes.channels), 0) == row)
        in_front = (column >= 0) & (column < sizes.rest)
        columns = (
            column,
            jnp.where(in_front, column + sizes.cap, -1),
            jnp.where(column >= sizes.rest, column + sizes.cap - sizes.rest, -1),
        )
        for at, wanted in enumerate(columns):
            to_column = hot(iota((LANES, sizes.channels), 0) == wanted)
            back_ref[at, :, source * LANES : (source + 1) * LANES] = dot_lanes(
                to_row, to_column
            ).astype(BF16)
        found = back_ref[0, :, source * LANES : (source + 1) * LANES]
        shape = (LANES, sizes.ch * sizes.cap)
        moved = hot(
            (iota(shape, 1) == iota(shape, 0) + source * sizes.cap)
            & (iota(shape, 0) < sizes.cap)
        )
        into = into + dot(found, moved)
    into_ref[...] = into.astype(BF16)

    modes = leap_ref.shape[0]
    terms = three_terms(param_ref[...])
    shape = (256, sizes.groups)
    wanted = sizes.group_here(lax.shift_right_logical(iota((256, 1), 0), bits(modes)), me, way)
    found = dot_lanes(hot(iota(shape, 1) == wanted), terms)
    found = three_sum(found, 1)
    mode = iota((256, 2 * modes), 0) & (modes - 1)
    lane = iota((256, 2 * modes), 1)
    rate = jnp.sum(jnp.where(lane == mode, found, 0.0), axis=1, keepdims=True)
    gain = jnp.sum(jnp.where(lane == mode + modes, found, 0.0), axis=1, keepdims=True)
    step = iota((256, sizes.run), 1).astype(F32)
    high, low = two_terms(gain * jnp.exp(-rate * step))
    table_ref[...] = jnp.concatenate([high, low], axis=1)
    shape = (sizes.groups, 256)
    wanted = sizes.group_here(lax.shift_right_logical(iota((1, 256), 1), bits(sizes.size)), me, way)
    found = three_sum(dot(terms, hot(iota(shape, 0) == wanted)), 0)
    leap_ref[...] = jnp.exp(found[:modes] * -float(sizes.run))


def three_terms(exact):
    high, rest = two_terms(exact)
    low, _ = two_terms(exact - high.astype(F32) - rest.astype(F32))
    return jnp.concatenate([high, rest, low], axis=0)


def three_sum(found, dim):
    high, rest, low = jnp.split(found, 3, axis=dim)
    return high + rest + low


def index(sizes, me, groups, dest, params):
    modes = params.shape[0] // 2
    return pl.pallas_call(
        functools.partial(index_kernel, sizes),
        in_specs=[pl.BlockSpec(memory_space=pltpu.SMEM)]
        + [pl.BlockSpec(memory_space=pltpu.VMEM)] * 3,
        out_shape=[
            jax.ShapeDtypeStruct((256, sizes.ch * sizes.cap), BF16),
            jax.ShapeDtypeStruct((3, 256, sizes.ch * LANES), BF16),
            jax.ShapeDtypeStruct((8, LANES), I32),
            jax.ShapeDtypeStruct((256, 2 * sizes.run), BF16),
            jax.ShapeDtypeStruct((modes, 256), F32),
        ],
        compiler_params=pltpu.CompilerParams(vmem_limit_bytes=VMEM_LIMIT),
        cost_estimate=pl.CostEstimate(flops=2 * 10**9, bytes_accessed=10**6, transcendentals=0),
        name="index_rows",
    )(me, groups, dest, params)


def local_kernel(
    sizes, me_ref, group_ref, param_ref, key_ref, value_ref, conv_ref, decay_ref, params, turned
):
    modes = param_ref.shape[0] // 2
    blocks = sizes.channels // LANES
    stacked = three_terms(param_ref[...])
    rows = 2 * modes
    first_lane = pl.multiple_of((me_ref[0] & (sizes.ch - 1)) * sizes.channels, LANES)
    groups = group_ref[:, pl.ds(first_lane, sizes.channels)]
    for start in range(0, sizes.channels, 256):
        chosen = hot(iota((sizes.groups, 256), 0) == groups[:, start : start + 256])
        found = three_sum(dot(stacked, chosen), 0)
        for half in range(2):
            block = start // LANES + half
            params[block * rows : (block + 1) * rows, :] = found[
                :, half * LANES : (half + 1) * LANES
            ]

    def turn(block, carry):
        at = pl.ds(pl.multiple_of(block * LANES, LANES), LANES)
        gated = (key_ref[at, :].astype(F32) * value_ref[at, :].astype(F32)).astype(BF16)
        turned[pl.ds(block, sizes.tokens, stride=blocks), :] = gated.astype(F32).T
        return carry

    lax.fori_loop(0, blocks, turn, 0)
    for first in range(0, blocks, 8):
        decays, gains = [], []
        for mode in range(modes):
            rate = params[pl.ds(first * rows + mode, 8, stride=rows), :]
            gains.append(params[pl.ds(first * rows + modes + mode, 8, stride=rows), :])
            decays.append(jnp.exp(-rate))
            decay_ref[mode * blocks + first : mode * blocks + first + 8, :] = decays[-1]
        for half in range(2):

            def step(token, states):
                at = (half * sizes.run + token) * blocks + first
                at = pl.ds(pl.multiple_of(at, 8), 8)
                value = turned[at, :]
                states = [a * s + c * value for a, c, s in zip(decays, gains, states)]
                conv_ref[at, :] = tree_sum(states)
                return states

            lax.fori_loop(0, sizes.run, step, [jnp.zeros((8, LANES), F32)] * modes)


def tree_sum(terms):
    while len(terms) > 1:
        terms = [
            terms[i] + terms[i + 1] if i + 1 < len(terms) else terms[i]
            for i in range(0, len(terms), 2)
        ]
    return terms[0]


def local(sizes, me, groups, params, key_proj, value_proj):
    modes = params.shape[0] // 2
    blocks = sizes.channels // LANES
    return pl.pallas_call(
        functools.partial(local_kernel, sizes),
        in_specs=[pl.BlockSpec(memory_space=pltpu.SMEM)]
        + [pl.BlockSpec(memory_space=pltpu.VMEM)] * 4,
        out_shape=[
            jax.ShapeDtypeStruct((sizes.tokens * blocks, LANES), F32),
            jax.ShapeDtypeStruct((modes * blocks, LANES), F32),
        ],
        scratch_shapes=[
            pltpu.VMEM((blocks * 2 * modes, LANES), F32),
            pltpu.VMEM((sizes.tokens * blocks, LANES), F32),
        ],
        compiler_params=pltpu.CompilerParams(vmem_limit_bytes=VMEM_LIMIT),
        cost_estimate=pl.CostEstimate(flops=4 * 10**9, bytes_accessed=3 * 10**6, transcendentals=0),
        name="local_runs",
    )(me, groups, params, key_proj, value_proj)


def owner_kernel(
    sizes,
    recv_ref,
    into_ref,
    back_ref,
    table_ref,
    leap_ref,
    out_ref,
    merged,
    gated,
    weighted,
    states,
    sums,
    run_at,
):
    run, runs, own, size = sizes.run, sizes.runs, sizes.own, sizes.size
    rows = own * size
    weighted[runs : 2 * runs + 1] = jnp.zeros((runs + 1, rows, LANES), BF16)
    for source in range(sizes.ctx):
        tail = recv_ref[source * sizes.ch, sizes.cap - 16 : sizes.cap, :].astype(F32)
        run_at[2 * source] = tail[15, 0].astype(I32)
        run_at[2 * source + 1] = tail[15, LANES].astype(I32)
    lane = iota((rows, LANES), 1)
    for source in range(sizes.ctx):
        block = recv_ref[source * sizes.ch : (source + 1) * sizes.ch]
        found = dot(into_ref[...], block.reshape(sizes.ch * sizes.cap, 2 * LANES))
        value = found[:, :LANES]
        turned = pltpu.roll(value, run, 1)
        merged[source, 0] = jnp.where(lane < run, value, turned).astype(BF16)
        merged[source, 1] = jnp.where(lane < run, turned, value).astype(BF16)
        merged[source, 2] = found[:, LANES:].astype(BF16)
        merged[source, 3] = pltpu.roll(found[:, LANES:], run, 1).astype(BF16)
    for source in range(sizes.ctx):
        first, second = run_at[2 * source], run_at[2 * source + 1]
        gated[first] = merged[source, 0]
        gated[second] = merged[source, 1]
        weighted[first + 1, :, :run] = merged[source, 2, :, :run]
        weighted[first, :, run:] = merged[source, 3, :, run:]
        weighted[second + 1, :, :run] = merged[source, 3, :, :run]
        weighted[second, :, run:] = merged[source, 2, :, run:]

    modes = states.shape[1]
    group_lane = lax.shift_right_logical(iota((modes, rows), 1), bits(size))
    carried = jnp.zeros((modes, rows), F32)
    leap = leap_ref[...]
    for at in range(runs):
        states[at] = carried
        if at + 1 < runs:
            ends = dot_lanes(table_ref[...], gated[at])
            total = jnp.zeros((modes, rows), F32)
            for group in range(own):
                piece = ends[group * modes : (group + 1) * modes]
                total = total + jnp.where(group_lane == group, piece, 0.0)
            carried = carried * leap + total

    seq = run * runs

    def one_group(group, carry):
        at = pl.ds(pl.multiple_of(group * size, size), size)
        left = gated[:, at, :].reshape(runs * size, LANES).T[:run]
        right = jnp.concatenate(
            [
                weighted[1 + lag : 1 + lag + runs, at, :].reshape(runs * size, LANES)
                for lag in range(0, runs, 2)
            ],
            axis=1,
        )
        gram = jnp.concatenate([dot(left, right), jnp.zeros((run, LANES), F32)], axis=1)
        skewed = pltpu.roll(gram, seq + LANES - (run - 1), 1, stride=1, stride_axis=0)
        sums[pl.ds(group, 1), :] = jnp.sum(skewed, axis=0, keepdims=True)[:, :seq]
        return carry

    lax.fori_loop(0, own, one_group, 0, unroll=True)

    each, cap, rest = sizes.each, sizes.cap, sizes.rest
    wide = 2 * modes - 8
    few_lags = LANES // 2 - rest
    pairs = [
        jnp.concatenate([states[run_at[2 * target]], states[run_at[2 * target + 1]]], axis=0)
        for target in range(sizes.ctx)
    ]
    front = dot(jnp.concatenate(pairs, axis=0).astype(BF16), back_ref[0])
    last = jnp.concatenate([pair[wide:] for pair in pairs], axis=0).astype(BF16)
    second, third = dot(last, back_ref[1]), dot(last, back_ref[2])
    out_lane = iota((8, LANES), 1)
    for target in range(sizes.ctx):
        lags = sums[:, target * LANES : (target + 1) * LANES]
        moves = [(cap, cap - rest), (LANES - few_lags - 2 * rest, LANES - 2 * few_lags - 2 * rest)]
        moved = [[pltpu.roll(lags, shift % LANES, 1) for shift in pair] for pair in moves]
        for chan in range(sizes.ch):
            at = slice(chan * LANES, (chan + 1) * LANES)
            mine = slice(chan * each, (chan + 1) * each)
            most, few = [jnp.concatenate([part[mine] for part in pair], axis=0) for pair in moved]
            head = front[target * 2 * modes : target * 2 * modes + wide, at]
            tail = slice(target * 8, (target + 1) * 8)
            beside = [
                second[tail, at],
                jnp.where(out_lane < LANES - few_lags, third[tail, at], few),
                most,
            ]
            out_ref[target * sizes.ch + chan] = jnp.concatenate(
                [
                    jnp.where(out_lane < cap, head[8 * row : 8 * row + 8], beside[row])
                    for row in range(3)
                ],
                axis=0,
            ).astype(BF16)


def owner(sizes, recv, into, back, table, leap):
    rows = sizes.own * sizes.size
    modes = leap.shape[0]
    return pl.pallas_call(
        functools.partial(owner_kernel, sizes),
        in_specs=[pl.BlockSpec(memory_space=pltpu.VMEM)] * 5,
        out_shape=jax.ShapeDtypeStruct((sizes.peers, 2 * modes - 8, LANES), BF16),
        scratch_shapes=[
            pltpu.VMEM((sizes.ctx, 4, rows, LANES), BF16),
            pltpu.VMEM((sizes.runs, rows, LANES), BF16),
            pltpu.VMEM((2 * sizes.runs + 1, rows, LANES), BF16),
            pltpu.VMEM((sizes.runs, modes, rows), F32),
            pltpu.VMEM((sizes.own, sizes.run * sizes.runs), F32),
            pltpu.SMEM((sizes.runs,), I32),
        ],
        compiler_params=pltpu.CompilerParams(vmem_limit_bytes=VMEM_LIMIT),
        name="owner_sums",
    )(recv, into, back, table, leap)


def finish_kernel(
    sizes, recv_ref, dest_ref, conv_ref, decay_ref, query_ref, out_ref, grad_ref, found, total
):
    blocks = sizes.channels // LANES
    wide = recv_ref.shape[1]
    rows = wide + 8
    modes = rows // 2
    cap, rest = sizes.cap, sizes.rest
    halves = sizes.peers // 2
    both = recv_ref[...].reshape(halves, 2, wide, LANES)
    both = jnp.concatenate([both[:, 0], both[:, 1]], axis=2)
    front = both.reshape(halves * wide, 2 * LANES)
    second = both[:, :8].astype(F32).reshape(halves * 8, 2 * LANES).astype(BF16)
    third = both[:, 8:16].astype(F32).reshape(halves * 8, 2 * LANES).astype(BF16)

    def fetch(part):
        at = pl.ds(part * 256, 256)
        owner, slot = dest_ref[1:2, at], dest_ref[2:3, at]
        half, offset = lax.shift_right_logical(owner, 1), (owner & 1) * LANES
        lane = iota((2 * LANES, 256), 0)
        in_second = jnp.where(slot < rest, slot + cap + offset, -1)
        in_third = jnp.where(slot >= rest, slot + cap - rest + offset, -1)
        most = dot(front, hot(lane == slot + offset))
        few = dot(second, hot(lane == in_second)) + dot(third, hot(lane == in_third))
        mine = [jnp.zeros((wide, 256), F32), jnp.zeros((8, 256), F32)]
        for peer in range(halves):
            mine[0] = mine[0] + jnp.where(half == peer, most[peer * wide : (peer + 1) * wide], 0.0)
            mine[1] = mine[1] + jnp.where(half == peer, few[peer * 8 : (peer + 1) * 8], 0.0)
        for side in range(2):
            start = (2 * part + side) * rows
            for piece, first in zip(mine, (0, wide)):
                found[pl.ds(start + first, piece.shape[0]), :] = piece[
                    :, side * LANES : (side + 1) * LANES
                ]

    def turn(block):
        at = pl.ds(block * LANES, LANES)
        conv = total[pl.ds(block, sizes.tokens, stride=blocks), :].astype(BF16).T
        out_ref[at, :] = (query_ref[at, :].astype(F32) * conv.astype(F32)).astype(BF16)

    for first in range(0, blocks, 8):
        for part in range(first // 2, first // 2 + 4):
            fetch(part)
        decays = [
            decay_ref[mode * blocks + first : mode * blocks + first + 8, :]
            for mode in range(modes)
        ]
        for half in range(2):
            states = [
                found[pl.ds(first * rows + half * modes + mode, 8, stride=rows), :]
                for mode in range(modes)
            ]

            def step(token, states):
                at = (half * sizes.run + token) * blocks + first
                at = pl.ds(pl.multiple_of(at, 8), 8)
                states = [a * s for a, s in zip(decays, states)]
                total[at, :] = conv_ref[at, :] + tree_sum(states)
                return states

            lax.fori_loop(0, sizes.run, step, states, unroll=True)
        for block in range(first, first + 8):
            turn(block)

    each, few_lags = sizes.each, LANES // 2 - rest
    shape = (sizes.peers * 8, LANES)
    upper = lax.shift_right_logical(iota(shape, 0) & 7, bits(each)) == 1
    lane = iota(shape, 1)
    placed = jnp.zeros(shape, F32)
    for rows_at, count, come, go in ((16, rest, cap, 0), (8, few_lags, LANES - few_lags, 2 * rest)):
        piece = recv_ref[:, rows_at : rows_at + 8, :].astype(F32).reshape(shape)
        for part in range(2):
            start = go + part * count
            moved = pltpu.roll(piece, (start - come) % LANES, 1)
            here = (upper == (part == 1)) & (lane >= start) & (lane < start + count)
            placed = jnp.where(here, moved, placed)
    come = iota((1, sizes.peers * 8), 1)
    seat = lax.shift_right_logical(come, 3) * each + (come & (each - 1))
    wanted = sizes.group_at(seat, way_of(dest_ref))
    chosen = hot(iota((sizes.block, sizes.peers * 8), 0) == wanted)
    grad_ref[...] = dot(chosen, placed.astype(BF16))


def finish(sizes, recv, dest, conv, decay, query_proj):
    blocks = sizes.channels // LANES
    return pl.pallas_call(
        functools.partial(finish_kernel, sizes),
        in_specs=[pl.BlockSpec(memory_space=pltpu.VMEM)] * 5,
        out_shape=[
            jax.ShapeDtypeStruct((sizes.channels, sizes.tokens), BF16),
            jax.ShapeDtypeStruct((sizes.block, LANES), F32),
        ],
        scratch_shapes=[
            pltpu.VMEM((blocks * (recv.shape[1] + 8), LANES), F32),
            pltpu.VMEM((sizes.tokens * blocks, LANES), F32),
        ],
        compiler_params=pltpu.CompilerParams(vmem_limit_bytes=VMEM_LIMIT),
        name="finish_rows",
    )(recv, dest, conv, decay, query_proj)


def exchange(blocks):
    return lax.all_to_all(blocks, ("ctx", "ch"), split_axis=0, concat_axis=0, tiled=True)


def owners_way(sizes, args):
    query_proj, key_proj, value_proj, cotangent, positions, group_of, decay_rates, residues = args
    me = (lax.axis_index("ctx") * sizes.ch + lax.axis_index("ch")).reshape(1).astype(I32)
    groups = group_of.reshape(1, -1)
    sent, dest = pack(sizes, positions, groups, key_proj, value_proj, cotangent, query_proj)
    recv = exchange(sent)

    gains = residues * jnp.sqrt(2.0 * decay_rates)
    params = jnp.concatenate([decay_rates, gains], axis=1).T
    conv, decay = local(sizes, me, groups, params, key_proj, value_proj)
    into, back, most, table, leap = index(sizes, me, groups, dest, params)

    def fast(recv, into, back, table, leap, dest, conv, decay, *args):
        returned = exchange(owner(sizes, recv, into, back, table, leap))
        return tuple(finish(sizes, returned, dest, conv, decay, args[0]))

    def slow(recv, into, back, table, leap, dest, conv, decay, *args):
        return general_way(*args)

    return lax.cond(
        most[0, 0] <= sizes.cap - 1,
        fast,
        slow,
        recv,
        into,
        back,
        table,
        leap,
        dest,
        conv,
        decay,
        *args,
    )


def shards(*args):
    sizes = Sizes(
        lax.axis_size("ctx"), lax.axis_size("ch"), *args[0].shape, args[6].shape[0]
    )
    if not sizes.fits:
        return general_way(*args)
    return owners_way(sizes, args)


def solution(mesh):
    placed = (
        P("ch", "ctx"),
        P("ch", "ctx"),
        P("ch", "ctx"),
        P("ch", "ctx"),
        P("ctx"),
        P(),
        P(),
        P(),
    )
    return jax.shard_map(
        shards,
        mesh=mesh,
        in_specs=placed,
        out_specs=(P("ch", "ctx"), P("ch", "ctx")),
        check_vma=False,
    )
```

```python
import functools
import math

import jax
import jax.numpy as jnp
from jax import lax
from jax.experimental import pallas as pl
from jax.experimental.pallas import tpu as pltpu
from jax.sharding import PartitionSpec as P

F32 = jnp.float32
BF16 = jnp.bfloat16
I32 = jnp.int32
LANES = 128
VMEM_LIMIT = 48 * 1024 * 1024


def product(form, left, right):
    return jnp.einsum(form, left, right, precision=lax.Precision.HIGHEST)


def split_rows(extent):
    chosen = 2
    for divisor in range(2, math.isqrt(extent) + 1, 2):
        if extent % divisor == 0:
            chosen = divisor
    return chosen


def dft_tables(row_count, col_count, extent):
    row_index = jnp.arange(row_count, dtype=jnp.int32)
    col_index = jnp.arange(col_count, dtype=jnp.int32)

    def angles(left_index, right_index, modulus):
        phase = left_index[:, None] * right_index[None, :] % modulus
        return phase.astype(jnp.float32) * (2.0 * math.pi / modulus)

    row_angle = angles(row_index, row_index, row_count)
    col_angle = angles(col_index, col_index, col_count)
    twist_angle = angles(row_index, col_index, extent)
    return (
        jnp.cos(row_angle),
        jnp.sin(row_angle),
        jnp.cos(col_angle),
        jnp.sin(col_angle),
        jnp.cos(twist_angle),
        jnp.sin(twist_angle),
    )


def forward_transform(signal, tables, row_count, col_count):
    row_cos, row_sin, col_cos, col_sin, twist_cos, twist_sin = tables
    folded = signal.reshape(signal.shape[0], row_count // 2, col_count)
    mid_real = product("ka,cab->ckb", row_cos[:, : row_count // 2], folded)
    mid_imag = -product("ka,cab->ckb", row_sin[:, : row_count // 2], folded)
    turned_real = mid_real * twist_cos + mid_imag * twist_sin
    turned_imag = mid_imag * twist_cos - mid_real * twist_sin
    spec_real = product("ckb,bm->ckm", turned_real, col_cos) + product(
        "ckb,bm->ckm", turned_imag, col_sin
    )
    spec_imag = product("ckb,bm->ckm", turned_imag, col_cos) - product(
        "ckb,bm->ckm", turned_real, col_sin
    )
    return (spec_real, spec_imag)


def inverse_transform(spec_real, spec_imag, tables, row_count, col_count):
    row_cos, row_sin, col_cos, col_sin, twist_cos, twist_sin = tables
    mid_real = product("ckm,bm->ckb", spec_real, col_cos) - product(
        "ckm,bm->ckb", spec_imag, col_sin
    )
    mid_imag = product("ckm,bm->ckb", spec_imag, col_cos) + product(
        "ckm,bm->ckb", spec_real, col_sin
    )
    turned_real = mid_real * twist_cos - mid_imag * twist_sin
    turned_imag = mid_imag * twist_cos + mid_real * twist_sin
    folded = product("ak,ckb->cab", row_cos[: row_count // 2, :], turned_real) - product(
        "ak,ckb->cab", row_sin[: row_count // 2, :], turned_imag
    )
    return folded.reshape(spec_real.shape[0], -1) / float(row_count * col_count)


def spectra(gated_seq, weighted_seq, chan_groups, decay_rates, residues, seq_length):
    extent = 2 * seq_length
    row_count = split_rows(extent)
    col_count = extent // row_count
    decay_rows = decay_rates[chan_groups]
    gain_rows = residues[chan_groups]
    tap_index = jnp.arange(seq_length, dtype=jnp.float32)
    coefs = gain_rows * jnp.sqrt(2.0 * decay_rows)
    filters = jnp.sum(coefs[:, :, None] * jnp.exp(-decay_rows[:, :, None] * tap_index), axis=1)
    tables = dft_tables(row_count, col_count, extent)
    gated_real, gated_imag = forward_transform(
        gated_seq.astype(jnp.float32), tables, row_count, col_count
    )
    filter_real, filter_imag = forward_transform(filters, tables, row_count, col_count)
    weight_real, weight_imag = forward_transform(
        weighted_seq.astype(jnp.float32), tables, row_count, col_count
    )
    convolved = inverse_transform(
        filter_real * gated_real - filter_imag * gated_imag,
        filter_real * gated_imag + filter_imag * gated_real,
        tables,
        row_count,
        col_count,
    )
    lagged = inverse_transform(
        weight_real * gated_real + weight_imag * gated_imag,
        weight_imag * gated_real - weight_real * gated_imag,
        tables,
        row_count,
        col_count,
    )
    return (convolved, lagged)


def general_way(
    query_proj, key_proj, value_proj, cotangent, positions, group_of, decay_rates, residues
):
    ctx_count = lax.axis_size("ctx")
    ch_count = lax.axis_size("ch")
    ctx_rank = lax.axis_index("ctx")
    ch_rank = lax.axis_index("ch")
    local_channels, local_tokens = query_proj.shape
    half_run = local_tokens // 2
    run_count = 2 * ctx_count
    seq_length = local_tokens * ctx_count
    per_device = local_channels // ctx_count
    groups_total = decay_rates.shape[0]
    gated = (key_proj.astype(jnp.float32) * value_proj.astype(jnp.float32)).astype(jnp.bfloat16)
    weighted = (cotangent.astype(jnp.float32) * query_proj.astype(jnp.float32)).astype(jnp.bfloat16)
    run_ids = jnp.stack([positions[0], positions[half_run]]) // half_run
    all_runs = lax.all_to_all(
        jnp.broadcast_to(run_ids[None, :], (ctx_count, 2)),
        "ctx",
        split_axis=0,
        concat_axis=0,
        tiled=True,
    ).reshape(run_count)
    source_run = (
        jnp.zeros((run_count,), jnp.int32).at[all_runs].set(jnp.arange(run_count, dtype=jnp.int32))
    )

    def to_sequence(stored):
        return stored.reshape(per_device, run_count, half_run)[:, source_run, :].reshape(
            per_device, seq_length
        )

    shard_groups = lax.dynamic_slice_in_dim(group_of, ch_rank * local_channels, local_channels)
    gated_cols, weighted_cols = (
        lax.all_to_all(gated, "ctx", split_axis=0, concat_axis=1, tiled=True),
        lax.all_to_all(weighted, "ctx", split_axis=0, concat_axis=1, tiled=True),
    )
    first_channel = ch_rank * local_channels + ctx_rank * per_device
    chan_groups = lax.dynamic_slice_in_dim(group_of, first_channel, per_device)
    convolved, lagged = spectra(
        to_sequence(gated_cols),
        to_sequence(weighted_cols),
        chan_groups,
        decay_rates,
        residues,
        seq_length,
    )
    ordered = convolved.astype(jnp.bfloat16).reshape(per_device, run_count, half_run)[
        :, all_runs, :
    ]
    conv_tokens = lax.all_to_all(
        ordered.reshape(per_device, seq_length), "ctx", split_axis=1, concat_axis=0, tiled=True
    )
    output = (query_proj.astype(jnp.float32) * conv_tokens.astype(jnp.float32)).astype(jnp.bfloat16)
    lag_rows = lax.all_to_all(lagged, "ctx", split_axis=1, concat_axis=0, tiled=True)
    select_all = (
        jnp.arange(groups_total, dtype=jnp.int32)[:, None] == shard_groups[None, :]
    ).astype(jnp.float32)
    partial = jnp.dot(
        select_all, lag_rows, precision=lax.Precision.HIGHEST, preferred_element_type=jnp.float32
    ).reshape(ch_count, groups_total // ch_count, local_tokens)
    filter_grad = jnp.sum(
        lax.all_to_all(partial, "ch", split_axis=0, concat_axis=0, tiled=True), axis=0
    )
    return (output, filter_grad)


def iota(shape, dim):
    return lax.broadcasted_iota(I32, shape, dim)


def hot(flags):
    return jnp.where(flags, 1.0, 0.0).astype(BF16)


def hot_at(rows, wanted):
    row = iota((rows, wanted.shape[1]), 0).astype(F32).astype(BF16)
    one = jnp.ones((), BF16)
    return jnp.where(row == wanted.astype(F32).astype(BF16), one, jnp.zeros((), BF16))


def dot(left, right):
    return jnp.dot(left, right, preferred_element_type=F32)


def dot_lanes(left, right):
    return lax.dot_general(left, right, (((1,), (1,)), ((), ())), preferred_element_type=F32)


def two_terms(values):
    high = values.astype(BF16)
    return high, (values - high.astype(F32)).astype(BF16)


class Sizes:
    def __init__(self, ctx, ch, channels, tokens, groups):
        self.ctx, self.ch = ctx, ch
        self.peers = ctx * ch
        self.channels = channels
        self.tokens = tokens
        self.run = tokens // 2
        self.runs = 2 * ctx
        self.groups = groups
        self.block = groups // ch
        self.each = self.block // self.peers
        self.own = groups // self.peers
        self.size = channels * ch // groups
        self.cap = 80
        self.rest = LANES - self.cap
        powers = [self.block, max(self.each, 1), self.own, self.size]
        self.fits = (
            tokens == LANES
            and self.block == LANES
            and self.runs == 16
            and self.own == 16
            and self.size == 16
            and self.each * self.peers == self.block
            and self.each * 8 * self.run == 16 * LANES
            and ch == 4
            and channels % 2048 == 0
            and channels // self.peers <= 64
            and all(p & (p - 1) == 0 for p in powers)
        )

    def deal(self, count):
        way = iota((1, count), 1)
        step = 2 * lax.shift_right_logical(way, 1) + 1
        turn = step
        for _ in range(3):
            turn = (turn * (2 - step * turn)) & (self.block - 1)
        return turn, (self.each // 2) * (way & 1), step

    def seat(self, group, way):
        turn, start, _ = way
        return (turn * (group & (self.block - 1)) + start) & (self.block - 1)

    def owner(self, group, way):
        return lax.shift_right_logical(self.seat(group, way), bits(self.each))

    def place(self, group, way):
        block = lax.shift_right_logical(group, bits(self.block))
        return block * self.each + (self.seat(group, way) & (self.each - 1))

    def group_at(self, seat, way):
        _, start, step = way
        return (step * (seat - start)) & (self.block - 1)

    def group_here(self, place, me, way):
        block = lax.shift_right_logical(place, bits(self.each))
        seat = me * self.each + (place & (self.each - 1))
        return block * self.block + self.group_at(seat, way)


def bits(power):
    return power.bit_length() - 1


def way_of(dest_ref):
    return tuple(dest_ref[row : row + 1, 0:1] for row in (3, 4, 5))


def running_counts(marks, upper):
    width = upper.shape[0]
    before, counts = jnp.zeros((marks.shape[0], 1), F32), []
    for start in range(0, marks.shape[1], width):
        part = marks[:, start : start + width]
        counts.append(dot(part, upper) + before)
        before = before + jnp.sum(part.astype(F32), axis=1, keepdims=True)
    return jnp.concatenate(counts, axis=1), before


def upper_ones(width):
    return hot(iota((width, width), 0) < iota((width, width), 1))


def choose_way(sizes, group):
    count = 64
    ways = sizes.deal(count)
    low = 16
    group = group & (sizes.block - 1)
    loads = []
    for source in range(sizes.ch):
        row = group[:, source * sizes.channels : (source + 1) * sizes.channels]
        high_hot = hot(iota((sizes.block // low, sizes.channels), 0) == lax.shift_right_logical(row, 4))
        low_hot = hot(iota((low, sizes.channels), 0) == (row & (low - 1)))
        table = dot_lanes(high_hot, low_hot)
        spread = hot((iota((low, sizes.block), 1) & (low - 1)) == iota((low, sizes.block), 0))
        wide = dot(table.astype(BF16), spread)
        own = lax.shift_right_logical(iota(wide.shape, 1), 4) == iota(wide.shape, 0)
        loads.append(jnp.sum(jnp.where(own, wide, 0.0), axis=0, keepdims=True))
    loads = jnp.concatenate(loads + [jnp.zeros((8 - sizes.ch, sizes.block), F32)], axis=0)
    lanes = sizes.peers * count
    spread = [jnp.concatenate([part] * sizes.peers, axis=1) for part in ways]
    seat = sizes.seat(iota((sizes.block, lanes), 0), spread)
    peer = lax.shift_right_logical(iota((1, lanes), 1), bits(count))
    dealt = hot(lax.shift_right_logical(seat, bits(sizes.each)) == peer)
    sums = dot(loads.astype(BF16), dealt)
    fullest = sums[:, :LANES]
    for start in range(LANES, lanes, LANES):
        fullest = jnp.maximum(fullest, sums[:, start : start + LANES])
    fullest = jnp.max(jnp.maximum(fullest, pltpu.roll(fullest, count, 1)), axis=0, keepdims=True)
    score = fullest[:, :count] * float(count) + iota((1, count), 1).astype(F32)
    best = jnp.min(score, axis=1, keepdims=True)
    return tuple(
        jnp.sum(jnp.where(score == best, part.astype(F32), 0.0), axis=1, keepdims=True).astype(I32)
        for part in ways
    )


def pack_kernel(
    sizes,
    place_hbm,
    group_hbm,
    key_hbm,
    value_hbm,
    cot_hbm,
    query_hbm,
    out_hbm,
    dest_ref,
    place_ref,
    group_ref,
    inputs,
    data,
    outgoing,
    arrived,
    left,
):
    moves = [(group_hbm, group_ref), (place_hbm, place_ref)]
    for at, source in enumerate((key_hbm, value_hbm, cot_hbm, query_hbm)):
        moves.append((source, inputs.at[at]))
    copies = [
        pltpu.make_async_copy(source, target, arrived.at[at])
        for at, (source, target) in enumerate(moves)
    ]
    for copy in copies:
        copy.start()
    copies[0].wait()
    way = choose_way(sizes, group_ref[...])
    first = pl.multiple_of(lax.axis_index("ch") * sizes.channels, LANES)
    owner = sizes.owner(group_ref[:, pl.ds(first, sizes.channels)], way)
    marks = iota((sizes.peers, sizes.channels), 0) == owner
    counts, _ = running_counts(hot(marks), upper_ones(256))
    slot = jnp.sum(jnp.where(marks, counts, 0.0), axis=0, keepdims=True).astype(I32)
    dest_ref[0:1, :] = jnp.where(slot < sizes.cap - 1, owner * sizes.cap + slot, -1)
    dest_ref[1:2, :] = owner
    dest_ref[2:3, :] = slot
    for row in range(3):
        dest_ref[3 + row : 4 + row, :] = jnp.broadcast_to(way[row], (1, sizes.channels))
    dest_ref[6:8, :] = jnp.zeros((2, sizes.channels), I32)
    for copy in copies[1:]:
        copy.wait()
    across = iota((LANES, LANES), 0) ^ iota((LANES, LANES), 1)
    gated = (inputs[0].astype(F32) * inputs[1].astype(F32)).astype(BF16)
    data[:, :LANES] = dot(gated, hot(across == sizes.run - 1)).astype(BF16)
    data[:, LANES:] = (inputs[2].astype(F32) * inputs[3].astype(F32)).astype(BF16)

    shift = bits(sizes.run)
    first = lax.shift_right_logical(place_ref[0], shift)
    second = lax.shift_right_logical(place_ref[sizes.run], shift)
    run_row = jnp.where(iota((1, 1, 2 * LANES), 2) < LANES, first, second).astype(F32)
    part = 8
    spare = iota((part, sizes.cap, 1), 1) == sizes.cap - 1
    copies = []
    for start in range(0, sizes.peers, part):
        base = start * sizes.cap
        chosen = hot(iota((part * sizes.cap, sizes.channels), 0) == dest_ref[0:1, :] - base)
        rows = dot(chosen, data[...]).reshape(part, sizes.cap, 2 * LANES)
        at = pl.ds(start, part)
        outgoing[at] = jnp.where(spare, run_row, rows).astype(BF16)
        copies.append(
            pltpu.make_async_copy(outgoing.at[at], out_hbm.at[at], left.at[start // part])
        )
        copies[-1].start()
    for copy in copies:
        copy.wait()


def pack(sizes, positions, groups, key_proj, value_proj, cotangent, query_proj):
    return pl.pallas_call(
        functools.partial(pack_kernel, sizes),
        in_specs=[pl.BlockSpec(memory_space=pltpu.HBM)] * 6,
        out_specs=[
            pl.BlockSpec(memory_space=pltpu.HBM),
            pl.BlockSpec(memory_space=pltpu.VMEM),
        ],
        out_shape=[
            jax.ShapeDtypeStruct((sizes.peers, sizes.cap, 2 * LANES), BF16),
            jax.ShapeDtypeStruct((8, sizes.channels), I32),
        ],
        scratch_shapes=[
            pltpu.SMEM(positions.shape, I32),
            pltpu.VMEM(groups.shape, I32),
            pltpu.VMEM((4, sizes.channels, sizes.tokens), BF16),
            pltpu.VMEM((sizes.channels, 2 * LANES), BF16),
            pltpu.VMEM((sizes.peers, sizes.cap, 2 * LANES), BF16),
            pltpu.SemaphoreType.DMA((6,)),
            pltpu.SemaphoreType.DMA((sizes.peers // 8,)),
        ],
        compiler_params=pltpu.CompilerParams(vmem_limit_bytes=VMEM_LIMIT),
        name="pack_rows",
    )(positions, groups, key_proj, value_proj, cotangent, query_proj)


def index_kernel(
    sizes,
    me_ref,
    group_ref,
    dest_ref,
    param_ref,
    into_ref,
    back_ref,
    over_ref,
    table_ref,
    leap_ref,
):
    me = me_ref[0]
    way = way_of(dest_ref)
    upper = upper_ones(256)
    group = group_ref[...]
    owner, place = sizes.owner(group, way), sizes.place(group, way)
    owner, place = jnp.split(owner, sizes.ch, axis=1), jnp.split(place, sizes.ch, axis=1)
    most = jnp.zeros((sizes.peers, 1), F32)
    for source in range(sizes.ch):
        marks = iota((sizes.peers, sizes.channels), 0) == owner[source]
        most = jnp.maximum(most, jnp.sum(jnp.where(marks, 1.0, 0.0), axis=1, keepdims=True))
    over_ref[...] = jnp.broadcast_to(jnp.max(most, axis=0, keepdims=True), (8, LANES)).astype(I32)

    earlier = jnp.zeros((sizes.own, 1), F32)
    into = jnp.zeros((256, sizes.ch * sizes.cap), F32)
    for source in range(sizes.ch):
        mine = owner[source] == me
        where = jnp.where(mine, place[source], -1)
        marks = iota((sizes.own, sizes.channels), 0) == where
        counts, totals = running_counts(hot(marks), upper)
        slot = jnp.sum(counts, axis=0, keepdims=True).astype(I32)
        nth = jnp.sum(jnp.where(marks, counts + earlier, 0.0), axis=0, keepdims=True).astype(I32)
        earlier = earlier + totals
        row = jnp.where(mine, where * sizes.size + nth, -1)
        column = jnp.where(mine & (slot < sizes.cap - 1), slot, -1)
        to_row = hot(iota((256, sizes.channels), 0) == row)
        to_column = hot(iota((LANES, sizes.channels), 0) == column)
        found = dot_lanes(to_row, to_column).astype(BF16)
        back_ref[:, source * LANES : (source + 1) * LANES] = found
        shape = (LANES, sizes.ch * sizes.cap)
        moved = hot(
            (iota(shape, 1) == iota(shape, 0) + source * sizes.cap)
            & (iota(shape, 0) < sizes.cap)
        )
        into = into + dot(found, moved)
    into_ref[...] = into.astype(BF16)

    modes = leap_ref.shape[0]
    terms = three_terms(param_ref[...])
    shape = (256, sizes.groups)
    wanted = sizes.group_here(lax.shift_right_logical(iota((256, 1), 0), bits(modes)), me, way)
    found = dot_lanes(hot(iota(shape, 1) == wanted), terms)
    found = three_sum(found, 1)
    mode = iota((256, 2 * modes), 0) & (modes - 1)
    lane = iota((256, 2 * modes), 1)
    rate = jnp.sum(jnp.where(lane == mode, found, 0.0), axis=1, keepdims=True)
    gain = jnp.sum(jnp.where(lane == mode + modes, found, 0.0), axis=1, keepdims=True)
    step = iota((256, sizes.run), 1).astype(F32)
    high, low = two_terms(gain * jnp.exp(-rate * step))
    table_ref[...] = jnp.concatenate([high, low], axis=1)
    shape = (sizes.groups, 256)
    wanted = sizes.group_here(lax.shift_right_logical(iota((1, 256), 1), bits(sizes.size)), me, way)
    found = three_sum(dot(terms, hot(iota(shape, 0) == wanted)), 0)
    leap_ref[...] = jnp.exp(found[:modes] * -float(sizes.run))


def three_terms(exact):
    high, rest = two_terms(exact)
    low, _ = two_terms(exact - high.astype(F32) - rest.astype(F32))
    return jnp.concatenate([high, rest, low], axis=0)


def three_sum(found, dim):
    high, rest, low = jnp.split(found, 3, axis=dim)
    return high + rest + low


def index(sizes, me, groups, dest, params):
    modes = params.shape[0] // 2
    return pl.pallas_call(
        functools.partial(index_kernel, sizes),
        in_specs=[pl.BlockSpec(memory_space=pltpu.SMEM)]
        + [pl.BlockSpec(memory_space=pltpu.VMEM)] * 3,
        out_shape=[
            jax.ShapeDtypeStruct((256, sizes.ch * sizes.cap), BF16),
            jax.ShapeDtypeStruct((256, sizes.ch * LANES), BF16),
            jax.ShapeDtypeStruct((8, LANES), I32),
            jax.ShapeDtypeStruct((256, 2 * sizes.run), BF16),
            jax.ShapeDtypeStruct((modes, 256), F32),
        ],
        compiler_params=pltpu.CompilerParams(vmem_limit_bytes=VMEM_LIMIT),
        cost_estimate=pl.CostEstimate(flops=2 * 10**9, bytes_accessed=10**6, transcendentals=0),
        name="index_rows",
    )(me, groups, dest, params)


def local_kernel(
    sizes, me_ref, group_ref, param_ref, key_ref, value_ref, conv_ref, decay_ref, params, turned
):
    modes = param_ref.shape[0] // 2
    blocks = sizes.channels // LANES
    stacked = three_terms(param_ref[...])
    rows = 2 * modes
    first_lane = pl.multiple_of((me_ref[0] & (sizes.ch - 1)) * sizes.channels, LANES)
    groups = group_ref[:, pl.ds(first_lane, sizes.channels)]
    for start in range(0, sizes.channels, 256):
        chosen = hot(iota((sizes.groups, 256), 0) == groups[:, start : start + 256])
        found = three_sum(dot(stacked, chosen), 0)
        for half in range(2):
            block = start // LANES + half
            params[block * rows : (block + 1) * rows, :] = found[
                :, half * LANES : (half + 1) * LANES
            ]

    def turn(block, carry):
        at = pl.ds(pl.multiple_of(block * LANES, LANES), LANES)
        gated = (key_ref[at, :].astype(F32) * value_ref[at, :].astype(F32)).astype(BF16)
        turned[pl.ds(block, sizes.tokens, stride=blocks), :] = gated.astype(F32).T
        return carry

    lax.fori_loop(0, blocks, turn, 0)
    for first in range(0, blocks, 8):
        decays, gains = [], []
        for mode in range(modes):
            rate = params[pl.ds(first * rows + mode, 8, stride=rows), :]
            gains.append(params[pl.ds(first * rows + modes + mode, 8, stride=rows), :])
            decays.append(jnp.exp(-rate))
            decay_ref[mode * blocks + first : mode * blocks + first + 8, :] = decays[-1]
        for half in range(2):

            def step(token, states):
                at = (half * sizes.run + token) * blocks + first
                at = pl.ds(pl.multiple_of(at, 8), 8)
                value = turned[at, :]
                states = [a * s + c * value for a, c, s in zip(decays, gains, states)]
                conv_ref[at, :] = tree_sum(states)
                return states

            lax.fori_loop(0, sizes.run, step, [jnp.zeros((8, LANES), F32)] * modes)


def tree_sum(terms):
    while len(terms) > 1:
        terms = [
            terms[i] + terms[i + 1] if i + 1 < len(terms) else terms[i]
            for i in range(0, len(terms), 2)
        ]
    return terms[0]


def local(sizes, me, groups, params, key_proj, value_proj):
    modes = params.shape[0] // 2
    blocks = sizes.channels // LANES
    return pl.pallas_call(
        functools.partial(local_kernel, sizes),
        in_specs=[pl.BlockSpec(memory_space=pltpu.SMEM)]
        + [pl.BlockSpec(memory_space=pltpu.VMEM)] * 4,
        out_shape=[
            jax.ShapeDtypeStruct((sizes.tokens * blocks, LANES), F32),
            jax.ShapeDtypeStruct((modes * blocks, LANES), F32),
        ],
        scratch_shapes=[
            pltpu.VMEM((blocks * 2 * modes, LANES), F32),
            pltpu.VMEM((sizes.tokens * blocks, LANES), F32),
        ],
        compiler_params=pltpu.CompilerParams(vmem_limit_bytes=VMEM_LIMIT),
        cost_estimate=pl.CostEstimate(flops=4 * 10**9, bytes_accessed=3 * 10**6, transcendentals=0),
        name="local_runs",
    )(me, groups, params, key_proj, value_proj)


def owner_kernel(
    sizes,
    recv_ref,
    into_ref,
    back_ref,
    table_ref,
    leap_ref,
    out_ref,
    merged,
    gated,
    weighted,
    states,
    sums,
    run_at,
):
    run, runs, own, size = sizes.run, sizes.runs, sizes.own, sizes.size
    rows = own * size
    weighted[runs : 2 * runs + 1] = jnp.zeros((runs + 1, rows, LANES), BF16)
    for source in range(sizes.ctx):
        tail = recv_ref[source * sizes.ch, sizes.cap - 16 : sizes.cap, :].astype(F32)
        run_at[2 * source] = tail[15, 0].astype(I32)
        run_at[2 * source + 1] = tail[15, LANES].astype(I32)
    lane = iota((rows, LANES), 1)
    for source in range(sizes.ctx):
        block = recv_ref[source * sizes.ch : (source + 1) * sizes.ch]
        found = dot(into_ref[...], block.reshape(sizes.ch * sizes.cap, 2 * LANES))
        found = found.astype(BF16)
        value = found[:, :LANES]
        turned = pltpu.roll(value, run, 1)
        merged[source, 0] = jnp.where(lane < run, value, turned)
        merged[source, 1] = jnp.where(lane < run, turned, value)
        merged[source, 2] = found[:, LANES:]
        merged[source, 3] = pltpu.roll(found[:, LANES:], run, 1)
    for source in range(sizes.ctx):
        first, second = run_at[2 * source], run_at[2 * source + 1]
        gated[first] = merged[source, 0]
        gated[second] = merged[source, 1]
        weighted[first + 1, :, :run] = merged[source, 2, :, :run]
        weighted[first, :, run:] = merged[source, 3, :, run:]
        weighted[second + 1, :, :run] = merged[source, 3, :, :run]
        weighted[second, :, run:] = merged[source, 2, :, run:]

    modes = states.shape[1]
    group_lane = lax.shift_right_logical(iota((modes, rows), 1), bits(size))
    carried = jnp.zeros((modes, rows), F32)
    leap = leap_ref[...]
    for at in range(runs):
        states[at] = carried
        if at + 1 < runs:
            ends = dot_lanes(table_ref[...], gated[at])
            total = ends[:modes]
            for group in range(1, own):
                piece = ends[group * modes : (group + 1) * modes]
                total = jnp.where(group_lane == group, piece, total)
            carried = carried * leap + total

    seq = run * runs

    def one_group(group, carry):
        at = pl.ds(pl.multiple_of(group * size, size), size)
        left = gated[:, at, :].reshape(runs * size, LANES).T[:run]
        right = jnp.concatenate(
            [
                weighted[1 + lag : 1 + lag + runs, at, :].reshape(runs * size, LANES)
                for lag in range(0, runs, 2)
            ],
            axis=1,
        )
        gram = jnp.concatenate([dot(left, right), jnp.zeros((run, LANES), F32)], axis=1)
        skewed = pltpu.roll(gram, seq + LANES - (run - 1), 1, stride=1, stride_axis=0)
        sums[pl.ds(group, 1), :] = jnp.sum(skewed, axis=0, keepdims=True)[:, :seq]
        return carry

    lax.fori_loop(0, own, one_group, 0, unroll=True)

    each, cap, rest = sizes.each, sizes.cap, sizes.rest
    wide = 2 * modes - 8
    few_lags = LANES // 2 - rest
    pairs = [
        jnp.concatenate([states[run_at[2 * target]], states[run_at[2 * target + 1]]], axis=0)
        for target in range(sizes.ctx)
    ]
    front = dot(jnp.concatenate(pairs, axis=0).astype(BF16), back_ref[...])
    out_lane = iota((8, LANES), 1)
    for target in range(sizes.ctx):
        lags = sums[:, target * LANES : (target + 1) * LANES]
        moves = [(cap, cap - rest), (LANES - few_lags - 2 * rest, LANES - 2 * few_lags - 2 * rest)]
        moved = [[pltpu.roll(lags, shift % LANES, 1) for shift in pair] for pair in moves]
        for chan in range(sizes.ch):
            at = slice(chan * LANES, (chan + 1) * LANES)
            mine = slice(chan * each, (chan + 1) * each)
            most, few = [jnp.concatenate([part[mine] for part in pair], axis=0) for pair in moved]
            head = front[target * 2 * modes : target * 2 * modes + wide, at]
            last = front[target * 2 * modes + wide : (target + 1) * 2 * modes, at]
            third = pltpu.roll(last, cap - rest, 1)
            beside = [
                pltpu.roll(last, cap, 1),
                jnp.where(out_lane < LANES - few_lags, third, few),
                most,
            ]
            out_ref[target * sizes.ch + chan] = jnp.concatenate(
                [
                    jnp.where(out_lane < cap, head[8 * row : 8 * row + 8], beside[row])
                    for row in range(3)
                ],
                axis=0,
            ).astype(BF16)


def owner(sizes, recv, into, back, table, leap):
    rows = sizes.own * sizes.size
    modes = leap.shape[0]
    return pl.pallas_call(
        functools.partial(owner_kernel, sizes),
        in_specs=[pl.BlockSpec(memory_space=pltpu.VMEM)] * 5,
        out_shape=jax.ShapeDtypeStruct((sizes.peers, 2 * modes - 8, LANES), BF16),
        scratch_shapes=[
            pltpu.VMEM((sizes.ctx, 4, rows, LANES), BF16),
            pltpu.VMEM((sizes.runs, rows, LANES), BF16),
            pltpu.VMEM((2 * sizes.runs + 1, rows, LANES), BF16),
            pltpu.VMEM((sizes.runs, modes, rows), F32),
            pltpu.VMEM((sizes.own, sizes.run * sizes.runs), F32),
            pltpu.SMEM((sizes.runs,), I32),
        ],
        compiler_params=pltpu.CompilerParams(vmem_limit_bytes=VMEM_LIMIT),
        name="owner_sums",
    )(recv, into, back, table, leap)


def finish_kernel(
    sizes,
    recv_ref,
    dest_ref,
    conv_ref,
    decay_ref,
    query_hbm,
    out_ref,
    grad_ref,
    found,
    total,
    query_ref,
    arrived,
):
    copy = pltpu.make_async_copy(query_hbm, query_ref, arrived)
    copy.start()
    blocks = sizes.channels // LANES
    wide = recv_ref.shape[1]
    rows = wide + 8
    modes = rows // 2
    cap, rest = sizes.cap, sizes.rest
    halves = sizes.peers // 2
    both = recv_ref[...].reshape(halves, 2, wide, LANES)
    both = jnp.concatenate([both[:, 0], both[:, 1]], axis=2)
    front = both.reshape(halves * wide, 2 * LANES)
    second = both[:, :8].astype(F32).reshape(halves * 8, 2 * LANES).astype(BF16)
    third = both[:, 8:16].astype(F32).reshape(halves * 8, 2 * LANES).astype(BF16)

    def fetch(part):
        at = pl.ds(part * 256, 256)
        owner, slot = dest_ref[1:2, at], dest_ref[2:3, at]
        half, offset = lax.shift_right_logical(owner, 1), (owner & 1) * LANES
        in_second = jnp.where(slot < rest, slot + cap + offset, -1)
        in_third = jnp.where(slot >= rest, slot + cap - rest + offset, -1)
        most = dot(front, hot_at(2 * LANES, slot + offset))
        few = dot(second, hot_at(2 * LANES, in_second)) + dot(third, hot_at(2 * LANES, in_third))
        mine = [jnp.zeros((wide, 256), F32), jnp.zeros((8, 256), F32)]
        for peer in range(halves):
            mine[0] = mine[0] + jnp.where(half == peer, most[peer * wide : (peer + 1) * wide], 0.0)
            mine[1] = mine[1] + jnp.where(half == peer, few[peer * 8 : (peer + 1) * 8], 0.0)
        for side in range(2):
            start = (2 * part + side) * rows
            for piece, first in zip(mine, (0, wide)):
                found[pl.ds(start + first, piece.shape[0]), :] = piece[
                    :, side * LANES : (side + 1) * LANES
                ]

    def turn(block):
        at = pl.ds(block * LANES, LANES)
        conv = total[pl.ds(block, sizes.tokens, stride=blocks), :].astype(BF16).T
        out_ref[at, :] = (query_ref[at, :].astype(F32) * conv.astype(F32)).astype(BF16)

    for first in range(0, blocks, 8):
        for part in range(first // 2, first // 2 + 4):
            fetch(part)
        decays = [
            decay_ref[mode * blocks + first : mode * blocks + first + 8, :]
            for mode in range(modes)
        ]
        for half in range(2):
            states = [
                found[pl.ds(first * rows + half * modes + mode, 8, stride=rows), :]
                for mode in range(modes)
            ]

            def step(token, states):
                at = (half * sizes.run + token) * blocks + first
                at = pl.ds(pl.multiple_of(at, 8), 8)
                states = [a * s for a, s in zip(decays, states)]
                total[at, :] = conv_ref[at, :] + tree_sum(states)
                return states

            lax.fori_loop(0, sizes.run, step, states, unroll=True)
        if first == 0:
            copy.wait()
        for block in range(first, first + 8):
            turn(block)

    each, few_lags = sizes.each, LANES // 2 - rest
    shape = (sizes.peers * 8, LANES)
    upper = lax.shift_right_logical(iota(shape, 0) & 7, bits(each)) == 1
    lane = iota(shape, 1)
    placed = jnp.zeros(shape, F32)
    for rows_at, count, come, go in ((16, rest, cap, 0), (8, few_lags, LANES - few_lags, 2 * rest)):
        piece = recv_ref[:, rows_at : rows_at + 8, :].astype(F32).reshape(shape)
        for part in range(2):
            start = go + part * count
            moved = pltpu.roll(piece, (start - come) % LANES, 1)
            here = (upper == (part == 1)) & (lane >= start) & (lane < start + count)
            placed = jnp.where(here, moved, placed)
    come = iota((1, sizes.peers * 8), 1)
    seat = lax.shift_right_logical(come, 3) * each + (come & (each - 1))
    wanted = sizes.group_at(seat, way_of(dest_ref))
    chosen = hot(iota((sizes.block, sizes.peers * 8), 0) == wanted)
    grad_ref[...] = dot(chosen, placed.astype(BF16))


def finish(sizes, recv, dest, conv, decay, query_proj):
    blocks = sizes.channels // LANES
    return pl.pallas_call(
        functools.partial(finish_kernel, sizes),
        in_specs=[pl.BlockSpec(memory_space=pltpu.VMEM)] * 4
        + [pl.BlockSpec(memory_space=pltpu.HBM)],
        out_shape=[
            jax.ShapeDtypeStruct((sizes.channels, sizes.tokens), BF16),
            jax.ShapeDtypeStruct((sizes.block, LANES), F32),
        ],
        scratch_shapes=[
            pltpu.VMEM((blocks * (recv.shape[1] + 8), LANES), F32),
            pltpu.VMEM((sizes.tokens * blocks, LANES), F32),
            pltpu.VMEM(query_proj.shape, BF16),
            pltpu.SemaphoreType.DMA,
        ],
        compiler_params=pltpu.CompilerParams(vmem_limit_bytes=VMEM_LIMIT),
        name="finish_rows",
    )(recv, dest, conv, decay, query_proj)


def exchange(blocks):
    return lax.all_to_all(blocks, ("ctx", "ch"), split_axis=0, concat_axis=0, tiled=True)


def owners_way(sizes, args):
    query_proj, key_proj, value_proj, cotangent, positions, group_of, decay_rates, residues = args
    me = (lax.axis_index("ctx") * sizes.ch + lax.axis_index("ch")).reshape(1).astype(I32)
    groups = group_of.reshape(1, -1)
    sent, dest = pack(sizes, positions, groups, key_proj, value_proj, cotangent, query_proj)
    recv = exchange(sent)

    gains = residues * jnp.sqrt(2.0 * decay_rates)
    params = jnp.concatenate([decay_rates, gains], axis=1).T
    conv, decay = local(sizes, me, groups, params, key_proj, value_proj)
    into, back, most, table, leap = index(sizes, me, groups, dest, params)

    into, conv, decay = lax.optimization_barrier((into, conv, decay))
    returned = exchange(owner(sizes, recv, into, back, table, leap))
    output, filter_grad = finish(sizes, returned, dest, conv, decay, query_proj)

    def again(state):
        return (jnp.zeros((), jnp.bool_), *general_way(*args))

    over = most[0, 0] > sizes.cap - 1
    _, output, filter_grad = lax.while_loop(
        lambda state: state[0], again, (over, output, filter_grad)
    )
    return (output, filter_grad)


def shards(*args):
    sizes = Sizes(
        lax.axis_size("ctx"), lax.axis_size("ch"), *args[0].shape, args[6].shape[0]
    )
    if not sizes.fits:
        return general_way(*args)
    return owners_way(sizes, args)


def solution(mesh):
    placed = (
        P("ch", "ctx"),
        P("ch", "ctx"),
        P("ch", "ctx"),
        P("ch", "ctx"),
        P("ctx"),
        P(),
        P(),
        P(),
    )
    return jax.shard_map(
        shards,
        mesh=mesh,
        in_specs=placed,
        out_specs=(P("ch", "ctx"), P("ch", "ctx")),
        check_vma=False,
    )
```

```python
import functools
import math

import jax
import jax.numpy as jnp
from jax import lax
from jax.experimental import pallas as pl
from jax.experimental.pallas import tpu as pltpu
from jax.sharding import PartitionSpec as P

F32 = jnp.float32
BF16 = jnp.bfloat16
I32 = jnp.int32
LANES = 128
VMEM_LIMIT = 48 * 1024 * 1024


def product(form, left, right):
    return jnp.einsum(form, left, right, precision=lax.Precision.HIGHEST)


def split_rows(extent):
    chosen = 2
    for divisor in range(2, math.isqrt(extent) + 1, 2):
        if extent % divisor == 0:
            chosen = divisor
    return chosen


def dft_tables(row_count, col_count, extent):
    row_index = jnp.arange(row_count, dtype=jnp.int32)
    col_index = jnp.arange(col_count, dtype=jnp.int32)

    def angles(left_index, right_index, modulus):
        phase = left_index[:, None] * right_index[None, :] % modulus
        return phase.astype(jnp.float32) * (2.0 * math.pi / modulus)

    row_angle = angles(row_index, row_index, row_count)
    col_angle = angles(col_index, col_index, col_count)
    twist_angle = angles(row_index, col_index, extent)
    return (
        jnp.cos(row_angle),
        jnp.sin(row_angle),
        jnp.cos(col_angle),
        jnp.sin(col_angle),
        jnp.cos(twist_angle),
        jnp.sin(twist_angle),
    )


def forward_transform(signal, tables, row_count, col_count):
    row_cos, row_sin, col_cos, col_sin, twist_cos, twist_sin = tables
    folded = signal.reshape(signal.shape[0], row_count // 2, col_count)
    mid_real = product("ka,cab->ckb", row_cos[:, : row_count // 2], folded)
    mid_imag = -product("ka,cab->ckb", row_sin[:, : row_count // 2], folded)
    turned_real = mid_real * twist_cos + mid_imag * twist_sin
    turned_imag = mid_imag * twist_cos - mid_real * twist_sin
    spec_real = product("ckb,bm->ckm", turned_real, col_cos) + product(
        "ckb,bm->ckm", turned_imag, col_sin
    )
    spec_imag = product("ckb,bm->ckm", turned_imag, col_cos) - product(
        "ckb,bm->ckm", turned_real, col_sin
    )
    return (spec_real, spec_imag)


def inverse_transform(spec_real, spec_imag, tables, row_count, col_count):
    row_cos, row_sin, col_cos, col_sin, twist_cos, twist_sin = tables
    mid_real = product("ckm,bm->ckb", spec_real, col_cos) - product(
        "ckm,bm->ckb", spec_imag, col_sin
    )
    mid_imag = product("ckm,bm->ckb", spec_imag, col_cos) + product(
        "ckm,bm->ckb", spec_real, col_sin
    )
    turned_real = mid_real * twist_cos - mid_imag * twist_sin
    turned_imag = mid_imag * twist_cos + mid_real * twist_sin
    folded = product("ak,ckb->cab", row_cos[: row_count // 2, :], turned_real) - product(
        "ak,ckb->cab", row_sin[: row_count // 2, :], turned_imag
    )
    return folded.reshape(spec_real.shape[0], -1) / float(row_count * col_count)


def spectra(gated_seq, weighted_seq, chan_groups, decay_rates, residues, seq_length):
    extent = 2 * seq_length
    row_count = split_rows(extent)
    col_count = extent // row_count
    decay_rows = decay_rates[chan_groups]
    gain_rows = residues[chan_groups]
    tap_index = jnp.arange(seq_length, dtype=jnp.float32)
    coefs = gain_rows * jnp.sqrt(2.0 * decay_rows)
    filters = jnp.sum(coefs[:, :, None] * jnp.exp(-decay_rows[:, :, None] * tap_index), axis=1)
    tables = dft_tables(row_count, col_count, extent)
    gated_real, gated_imag = forward_transform(
        gated_seq.astype(jnp.float32), tables, row_count, col_count
    )
    filter_real, filter_imag = forward_transform(filters, tables, row_count, col_count)
    weight_real, weight_imag = forward_transform(
        weighted_seq.astype(jnp.float32), tables, row_count, col_count
    )
    convolved = inverse_transform(
        filter_real * gated_real - filter_imag * gated_imag,
        filter_real * gated_imag + filter_imag * gated_real,
        tables,
        row_count,
        col_count,
    )
    lagged = inverse_transform(
        weight_real * gated_real + weight_imag * gated_imag,
        weight_imag * gated_real - weight_real * gated_imag,
        tables,
        row_count,
        col_count,
    )
    return (convolved, lagged)


def general_way(
    query_proj, key_proj, value_proj, cotangent, positions, group_of, decay_rates, residues
):
    ctx_count = lax.axis_size("ctx")
    ch_count = lax.axis_size("ch")
    ctx_rank = lax.axis_index("ctx")
    ch_rank = lax.axis_index("ch")
    local_channels, local_tokens = query_proj.shape
    half_run = local_tokens // 2
    run_count = 2 * ctx_count
    seq_length = local_tokens * ctx_count
    per_device = local_channels // ctx_count
    groups_total = decay_rates.shape[0]
    gated = (key_proj.astype(jnp.float32) * value_proj.astype(jnp.float32)).astype(jnp.bfloat16)
    weighted = (cotangent.astype(jnp.float32) * query_proj.astype(jnp.float32)).astype(jnp.bfloat16)
    run_ids = jnp.stack([positions[0], positions[half_run]]) // half_run
    all_runs = lax.all_to_all(
        jnp.broadcast_to(run_ids[None, :], (ctx_count, 2)),
        "ctx",
        split_axis=0,
        concat_axis=0,
        tiled=True,
    ).reshape(run_count)
    source_run = (
        jnp.zeros((run_count,), jnp.int32).at[all_runs].set(jnp.arange(run_count, dtype=jnp.int32))
    )

    def to_sequence(stored):
        return stored.reshape(per_device, run_count, half_run)[:, source_run, :].reshape(
            per_device, seq_length
        )

    shard_groups = lax.dynamic_slice_in_dim(group_of, ch_rank * local_channels, local_channels)
    gated_cols, weighted_cols = (
        lax.all_to_all(gated, "ctx", split_axis=0, concat_axis=1, tiled=True),
        lax.all_to_all(weighted, "ctx", split_axis=0, concat_axis=1, tiled=True),
    )
    first_channel = ch_rank * local_channels + ctx_rank * per_device
    chan_groups = lax.dynamic_slice_in_dim(group_of, first_channel, per_device)
    convolved, lagged = spectra(
        to_sequence(gated_cols),
        to_sequence(weighted_cols),
        chan_groups,
        decay_rates,
        residues,
        seq_length,
    )
    ordered = convolved.astype(jnp.bfloat16).reshape(per_device, run_count, half_run)[
        :, all_runs, :
    ]
    conv_tokens = lax.all_to_all(
        ordered.reshape(per_device, seq_length), "ctx", split_axis=1, concat_axis=0, tiled=True
    )
    output = (query_proj.astype(jnp.float32) * conv_tokens.astype(jnp.float32)).astype(jnp.bfloat16)
    lag_rows = lax.all_to_all(lagged, "ctx", split_axis=1, concat_axis=0, tiled=True)
    select_all = (
        jnp.arange(groups_total, dtype=jnp.int32)[:, None] == shard_groups[None, :]
    ).astype(jnp.float32)
    partial = jnp.dot(
        select_all, lag_rows, precision=lax.Precision.HIGHEST, preferred_element_type=jnp.float32
    ).reshape(ch_count, groups_total // ch_count, local_tokens)
    filter_grad = jnp.sum(
        lax.all_to_all(partial, "ch", split_axis=0, concat_axis=0, tiled=True), axis=0
    )
    return (output, filter_grad)


def iota(shape, dim):
    return lax.broadcasted_iota(I32, shape, dim)


def hot(flags):
    return jnp.where(flags, 1.0, 0.0).astype(BF16)


def hot_at(rows, wanted):
    row = iota((rows, wanted.shape[1]), 0).astype(F32).astype(BF16)
    one = jnp.ones((), BF16)
    return jnp.where(row == wanted.astype(F32).astype(BF16), one, jnp.zeros((), BF16))


def dot(left, right):
    return jnp.dot(left, right, preferred_element_type=F32)


def dot_lanes(left, right):
    return lax.dot_general(left, right, (((1,), (1,)), ((), ())), preferred_element_type=F32)


def two_terms(values):
    high = values.astype(BF16)
    return high, (values - high.astype(F32)).astype(BF16)


class Sizes:
    def __init__(self, ctx, ch, channels, tokens, groups):
        self.ctx, self.ch = ctx, ch
        self.peers = ctx * ch
        self.channels = channels
        self.tokens = tokens
        self.run = tokens // 2
        self.runs = 2 * ctx
        self.groups = groups
        self.block = groups // ch
        self.each = self.block // self.peers
        self.own = groups // self.peers
        self.size = channels * ch // groups
        self.cap = 80
        self.rest = LANES - self.cap
        powers = [self.block, max(self.each, 1), self.own, self.size]
        self.fits = (
            tokens == LANES
            and self.block == LANES
            and self.runs == 16
            and self.own == 16
            and self.size == 16
            and self.each * self.peers == self.block
            and self.each * 8 * self.run == 16 * LANES
            and ch == 4
            and channels % 2048 == 0
            and channels // self.peers <= 64
            and all(p & (p - 1) == 0 for p in powers)
        )

    def deal(self, count):
        way = iota((1, count), 1)
        step = 2 * lax.shift_right_logical(way, 1) + 1
        turn = step
        for _ in range(3):
            turn = (turn * (2 - step * turn)) & (self.block - 1)
        return turn, (self.each // 2) * (way & 1), step

    def seat(self, group, way):
        turn, start, _ = way
        return (turn * (group & (self.block - 1)) + start) & (self.block - 1)

    def owner(self, group, way):
        return lax.shift_right_logical(self.seat(group, way), bits(self.each))

    def place(self, group, way):
        block = lax.shift_right_logical(group, bits(self.block))
        return block * self.each + (self.seat(group, way) & (self.each - 1))

    def group_at(self, seat, way):
        _, start, step = way
        return (step * (seat - start)) & (self.block - 1)

    def group_here(self, place, me, way):
        block = lax.shift_right_logical(place, bits(self.each))
        seat = me * self.each + (place & (self.each - 1))
        return block * self.block + self.group_at(seat, way)


def bits(power):
    return power.bit_length() - 1


def way_of(dest_ref):
    return tuple(dest_ref[row : row + 1, 0:1] for row in (3, 4, 5))


def running_counts(marks, upper):
    width = upper.shape[0]
    before, counts = jnp.zeros((marks.shape[0], 1), F32), []
    for start in range(0, marks.shape[1], width):
        part = marks[:, start : start + width]
        counts.append(dot(part, upper) + before)
        before = before + jnp.sum(part.astype(F32), axis=1, keepdims=True)
    return jnp.concatenate(counts, axis=1), before


def upper_ones(width):
    return hot(iota((width, width), 0) < iota((width, width), 1))


def choose_way(sizes, group):
    count = 64
    ways = sizes.deal(count)
    low = 16
    group = group & (sizes.block - 1)
    loads = []
    for source in range(sizes.ch):
        row = group[:, source * sizes.channels : (source + 1) * sizes.channels]
        high_hot = hot(iota((sizes.block // low, sizes.channels), 0) == lax.shift_right_logical(row, 4))
        low_hot = hot(iota((low, sizes.channels), 0) == (row & (low - 1)))
        table = dot_lanes(high_hot, low_hot)
        spread = hot((iota((low, sizes.block), 1) & (low - 1)) == iota((low, sizes.block), 0))
        wide = dot(table.astype(BF16), spread)
        own = lax.shift_right_logical(iota(wide.shape, 1), 4) == iota(wide.shape, 0)
        loads.append(jnp.sum(jnp.where(own, wide, 0.0), axis=0, keepdims=True))
    loads = jnp.concatenate(loads + [jnp.zeros((8 - sizes.ch, sizes.block), F32)], axis=0)
    lanes = sizes.peers * count
    spread = [jnp.concatenate([part] * sizes.peers, axis=1) for part in ways]
    seat = sizes.seat(iota((sizes.block, lanes), 0), spread)
    peer = lax.shift_right_logical(iota((1, lanes), 1), bits(count))
    dealt = hot(lax.shift_right_logical(seat, bits(sizes.each)) == peer)
    sums = dot(loads.astype(BF16), dealt)
    fullest = sums[:, :LANES]
    for start in range(LANES, lanes, LANES):
        fullest = jnp.maximum(fullest, sums[:, start : start + LANES])
    fullest = jnp.max(jnp.maximum(fullest, pltpu.roll(fullest, count, 1)), axis=0, keepdims=True)
    score = fullest[:, :count] * float(count) + iota((1, count), 1).astype(F32)
    best = jnp.min(score, axis=1, keepdims=True)
    return tuple(
        jnp.sum(jnp.where(score == best, part.astype(F32), 0.0), axis=1, keepdims=True).astype(I32)
        for part in ways
    )


def pack_kernel(
    sizes,
    place_hbm,
    group_hbm,
    key_hbm,
    value_hbm,
    cot_hbm,
    query_hbm,
    out_ref,
    dest_ref,
    place_ref,
    group_ref,
    inputs,
    data,
    arrived,
):
    moves = [(group_hbm, group_ref), (place_hbm, place_ref)]
    for at, source in enumerate((key_hbm, value_hbm, cot_hbm, query_hbm)):
        moves.append((source, inputs.at[at]))
    copies = [
        pltpu.make_async_copy(source, target, arrived.at[at])
        for at, (source, target) in enumerate(moves)
    ]
    for copy in copies:
        copy.start()
    copies[0].wait()
    way = choose_way(sizes, group_ref[...])
    first = pl.multiple_of(lax.axis_index("ch") * sizes.channels, LANES)
    owner = sizes.owner(group_ref[:, pl.ds(first, sizes.channels)], way)
    marks = iota((sizes.peers, sizes.channels), 0) == owner
    counts, _ = running_counts(hot(marks), upper_ones(256))
    slot = jnp.sum(jnp.where(marks, counts, 0.0), axis=0, keepdims=True).astype(I32)
    dest_ref[0:1, :] = jnp.where(slot < sizes.cap - 1, owner * sizes.cap + slot, -1)
    dest_ref[1:2, :] = owner
    dest_ref[2:3, :] = slot
    for row in range(3):
        dest_ref[3 + row : 4 + row, :] = jnp.broadcast_to(way[row], (1, sizes.channels))
    dest_ref[6:8, :] = jnp.zeros((2, sizes.channels), I32)
    for copy in copies[1:]:
        copy.wait()
    across = iota((LANES, LANES), 0) ^ iota((LANES, LANES), 1)
    gated = (inputs[0].astype(F32) * inputs[1].astype(F32)).astype(BF16)
    data[:, :LANES] = dot(gated, hot(across == sizes.run - 1)).astype(BF16)
    data[:, LANES:] = (inputs[2].astype(F32) * inputs[3].astype(F32)).astype(BF16)

    shift = bits(sizes.run)
    first = lax.shift_right_logical(place_ref[0], shift)
    second = lax.shift_right_logical(place_ref[sizes.run], shift)
    run_row = jnp.where(iota((1, 1, 2 * LANES), 2) < LANES, first, second).astype(F32)
    part = 16
    spare = iota((part, sizes.cap, 1), 1) == sizes.cap - 1
    for start in range(0, sizes.peers, part):
        base = start * sizes.cap
        chosen = hot(iota((part * sizes.cap, sizes.channels), 0) == dest_ref[0:1, :] - base)
        rows = dot(chosen, data[...]).reshape(part, sizes.cap, 2 * LANES)
        out_ref[start : start + part] = jnp.where(spare, run_row, rows).astype(BF16)


def pack(sizes, positions, groups, key_proj, value_proj, cotangent, query_proj):
    return pl.pallas_call(
        functools.partial(pack_kernel, sizes),
        in_specs=[pl.BlockSpec(memory_space=pl.ANY)] * 6,
        out_specs=[pl.BlockSpec(memory_space=pltpu.VMEM)] * 2,
        out_shape=[
            jax.ShapeDtypeStruct((sizes.peers, sizes.cap, 2 * LANES), BF16),
            jax.ShapeDtypeStruct((8, sizes.channels), I32),
        ],
        scratch_shapes=[
            pltpu.SMEM(positions.shape, I32),
            pltpu.VMEM(groups.shape, I32),
            pltpu.VMEM((4, sizes.channels, sizes.tokens), BF16),
            pltpu.VMEM((sizes.channels, 2 * LANES), BF16),
            pltpu.SemaphoreType.DMA((6,)),
        ],
        compiler_params=pltpu.CompilerParams(vmem_limit_bytes=VMEM_LIMIT),
        name="pack_rows",
    )(positions, groups, key_proj, value_proj, cotangent, query_proj)


def index_kernel(
    sizes,
    me_ref,
    group_ref,
    dest_ref,
    param_ref,
    into_ref,
    back_ref,
    over_ref,
    table_ref,
    leap_ref,
):
    me = me_ref[0]
    way = way_of(dest_ref)
    upper = upper_ones(256)
    group = group_ref[...]
    owner, place = sizes.owner(group, way), sizes.place(group, way)
    owner, place = jnp.split(owner, sizes.ch, axis=1), jnp.split(place, sizes.ch, axis=1)
    most = jnp.zeros((sizes.peers, 1), F32)
    for source in range(sizes.ch):
        marks = iota((sizes.peers, sizes.channels), 0) == owner[source]
        most = jnp.maximum(most, jnp.sum(jnp.where(marks, 1.0, 0.0), axis=1, keepdims=True))
    over_ref[...] = jnp.broadcast_to(jnp.max(most, axis=0, keepdims=True), (8, LANES)).astype(I32)

    earlier = jnp.zeros((sizes.own, 1), F32)
    into = jnp.zeros((256, sizes.ch * sizes.cap), F32)
    for source in range(sizes.ch):
        mine = owner[source] == me
        where = jnp.where(mine, place[source], -1)
        marks = iota((sizes.own, sizes.channels), 0) == where
        counts, totals = running_counts(hot(marks), upper)
        slot = jnp.sum(counts, axis=0, keepdims=True).astype(I32)
        nth = jnp.sum(jnp.where(marks, counts + earlier, 0.0), axis=0, keepdims=True).astype(I32)
        earlier = earlier + totals
        row = jnp.where(mine, where * sizes.size + nth, -1)
        column = jnp.where(mine & (slot < sizes.cap - 1), slot, -1)
        to_row = hot(iota((256, sizes.channels), 0) == row)
        to_column = hot(iota((LANES, sizes.channels), 0) == column)
        found = dot_lanes(to_row, to_column).astype(BF16)
        back_ref[:, source * LANES : (source + 1) * LANES] = found
        shape = (LANES, sizes.ch * sizes.cap)
        moved = hot(
            (iota(shape, 1) == iota(shape, 0) + source * sizes.cap)
            & (iota(shape, 0) < sizes.cap)
        )
        into = into + dot(found, moved)
    into_ref[...] = into.astype(BF16)

    modes = leap_ref.shape[0]
    terms = three_terms(param_ref[...])
    shape = (256, sizes.groups)
    wanted = sizes.group_here(lax.shift_right_logical(iota((256, 1), 0), bits(modes)), me, way)
    found = dot_lanes(hot(iota(shape, 1) == wanted), terms)
    found = three_sum(found, 1)
    mode = iota((256, 2 * modes), 0) & (modes - 1)
    lane = iota((256, 2 * modes), 1)
    rate = jnp.sum(jnp.where(lane == mode, found, 0.0), axis=1, keepdims=True)
    gain = jnp.sum(jnp.where(lane == mode + modes, found, 0.0), axis=1, keepdims=True)
    step = iota((256, sizes.run), 1).astype(F32)
    high, low = two_terms(gain * jnp.exp(-rate * step))
    table_ref[...] = jnp.concatenate([high, low], axis=1)
    shape = (sizes.groups, 256)
    wanted = sizes.group_here(lax.shift_right_logical(iota((1, 256), 1), bits(sizes.size)), me, way)
    found = three_sum(dot(terms, hot(iota(shape, 0) == wanted)), 0)
    leap_ref[...] = jnp.exp(found[:modes] * -float(sizes.run))


def three_terms(exact):
    high, rest = two_terms(exact)
    low, _ = two_terms(exact - high.astype(F32) - rest.astype(F32))
    return jnp.concatenate([high, rest, low], axis=0)


def three_sum(found, dim):
    high, rest, low = jnp.split(found, 3, axis=dim)
    return high + rest + low


def index(sizes, me, groups, dest, params):
    modes = params.shape[0] // 2
    return pl.pallas_call(
        functools.partial(index_kernel, sizes),
        in_specs=[pl.BlockSpec(memory_space=pltpu.SMEM)]
        + [pl.BlockSpec(memory_space=pltpu.VMEM)] * 3,
        out_shape=[
            jax.ShapeDtypeStruct((256, sizes.ch * sizes.cap), BF16),
            jax.ShapeDtypeStruct((256, sizes.ch * LANES), BF16),
            jax.ShapeDtypeStruct((8, LANES), I32),
            jax.ShapeDtypeStruct((256, 2 * sizes.run), BF16),
            jax.ShapeDtypeStruct((modes, 256), F32),
        ],
        compiler_params=pltpu.CompilerParams(vmem_limit_bytes=VMEM_LIMIT),
        cost_estimate=pl.CostEstimate(flops=2 * 10**9, bytes_accessed=10**6, transcendentals=0),
        name="index_rows",
    )(me, groups, dest, params)


def local_kernel(
    sizes, me_ref, group_ref, param_ref, key_ref, value_ref, conv_ref, decay_ref, params, turned
):
    modes = param_ref.shape[0] // 2
    blocks = sizes.channels // LANES
    stacked = three_terms(param_ref[...])
    rows = 2 * modes
    first_lane = pl.multiple_of((me_ref[0] & (sizes.ch - 1)) * sizes.channels, LANES)
    groups = group_ref[:, pl.ds(first_lane, sizes.channels)]
    for start in range(0, sizes.channels, 256):
        chosen = hot(iota((sizes.groups, 256), 0) == groups[:, start : start + 256])
        found = three_sum(dot(stacked, chosen), 0)
        for half in range(2):
            block = start // LANES + half
            params[block * rows : (block + 1) * rows, :] = found[
                :, half * LANES : (half + 1) * LANES
            ]

    def turn(block, carry):
        at = pl.ds(pl.multiple_of(block * LANES, LANES), LANES)
        gated = (key_ref[at, :].astype(F32) * value_ref[at, :].astype(F32)).astype(BF16)
        turned[pl.ds(block, sizes.tokens, stride=blocks), :] = gated.astype(F32).T
        return carry

    lax.fori_loop(0, blocks, turn, 0)
    for first in range(0, blocks, 8):
        decays, gains = [], []
        for mode in range(modes):
            rate = params[pl.ds(first * rows + mode, 8, stride=rows), :]
            gains.append(params[pl.ds(first * rows + modes + mode, 8, stride=rows), :])
            decays.append(jnp.exp(-rate))
            decay_ref[mode * blocks + first : mode * blocks + first + 8, :] = decays[-1]
        for half in range(2):

            def step(token, states):
                at = (half * sizes.run + token) * blocks + first
                at = pl.ds(pl.multiple_of(at, 8), 8)
                value = turned[at, :]
                states = [a * s + c * value for a, c, s in zip(decays, gains, states)]
                conv_ref[at, :] = tree_sum(states)
                return states

            lax.fori_loop(0, sizes.run, step, [jnp.zeros((8, LANES), F32)] * modes)


def tree_sum(terms):
    while len(terms) > 1:
        terms = [
            terms[i] + terms[i + 1] if i + 1 < len(terms) else terms[i]
            for i in range(0, len(terms), 2)
        ]
    return terms[0]


def local(sizes, me, groups, params, key_proj, value_proj):
    modes = params.shape[0] // 2
    blocks = sizes.channels // LANES
    return pl.pallas_call(
        functools.partial(local_kernel, sizes),
        in_specs=[pl.BlockSpec(memory_space=pltpu.SMEM)]
        + [pl.BlockSpec(memory_space=pltpu.VMEM)] * 4,
        out_shape=[
            jax.ShapeDtypeStruct((sizes.tokens * blocks, LANES), F32),
            jax.ShapeDtypeStruct((modes * blocks, LANES), F32),
        ],
        scratch_shapes=[
            pltpu.VMEM(((blocks + 1) * 2 * modes, LANES), F32),
            pltpu.VMEM(((sizes.tokens + 1) * blocks, LANES), F32),
        ],
        compiler_params=pltpu.CompilerParams(vmem_limit_bytes=VMEM_LIMIT),
        cost_estimate=pl.CostEstimate(flops=4 * 10**9, bytes_accessed=3 * 10**6, transcendentals=0),
        name="local_runs",
    )(me, groups, params, key_proj, value_proj)


def owner_kernel(
    sizes,
    recv_ref,
    into_ref,
    back_ref,
    table_ref,
    leap_ref,
    out_ref,
    merged,
    gated,
    weighted,
    states,
    sums,
    run_at,
):
    run, runs, own, size = sizes.run, sizes.runs, sizes.own, sizes.size
    rows = own * size
    weighted[runs : 2 * runs + 1] = jnp.zeros((runs + 1, rows, LANES), BF16)
    for source in range(sizes.ctx):
        tail = recv_ref[source * sizes.ch, sizes.cap - 16 : sizes.cap, :].astype(F32)
        run_at[2 * source] = tail[15, 0].astype(I32)
        run_at[2 * source + 1] = tail[15, LANES].astype(I32)
    lane = iota((rows, LANES), 1)
    for source in range(sizes.ctx):
        block = recv_ref[source * sizes.ch : (source + 1) * sizes.ch]
        found = dot(into_ref[...], block.reshape(sizes.ch * sizes.cap, 2 * LANES))
        found = found.astype(BF16)
        value = found[:, :LANES]
        turned = pltpu.roll(value, run, 1)
        merged[source, 0] = jnp.where(lane < run, value, turned)
        merged[source, 1] = jnp.where(lane < run, turned, value)
        merged[source, 2] = found[:, LANES:]
        merged[source, 3] = pltpu.roll(found[:, LANES:], run, 1)
    for source in range(sizes.ctx):
        first, second = run_at[2 * source], run_at[2 * source + 1]
        gated[first] = merged[source, 0]
        gated[second] = merged[source, 1]
        weighted[first + 1, :, :run] = merged[source, 2, :, :run]
        weighted[first, :, run:] = merged[source, 3, :, run:]
        weighted[second + 1, :, :run] = merged[source, 3, :, :run]
        weighted[second, :, run:] = merged[source, 2, :, run:]

    modes = states.shape[1]
    group_lane = lax.shift_right_logical(iota((modes, rows), 1), bits(size))
    carried = jnp.zeros((modes, rows), F32)
    leap = leap_ref[...]
    for at in range(runs):
        states[at] = carried
        if at + 1 < runs:
            ends = dot_lanes(table_ref[...], gated[at])
            total = ends[:modes]
            for group in range(1, own):
                piece = ends[group * modes : (group + 1) * modes]
                total = jnp.where(group_lane == group, piece, total)
            carried = carried * leap + total

    seq = run * runs

    def one_group(group, carry):
        at = pl.ds(pl.multiple_of(group * size, size), size)
        left = gated[:, at, :].reshape(runs * size, LANES).T[:run]
        right = jnp.concatenate(
            [
                weighted[1 + lag : 1 + lag + runs, at, :].reshape(runs * size, LANES)
                for lag in range(0, runs, 2)
            ],
            axis=1,
        )
        gram = jnp.concatenate([dot(left, right), jnp.zeros((run, LANES), F32)], axis=1)
        skewed = pltpu.roll(gram, seq + LANES - (run - 1), 1, stride=1, stride_axis=0)
        sums[pl.ds(group, 1), :] = jnp.sum(skewed, axis=0, keepdims=True)[:, :seq]
        return carry

    lax.fori_loop(0, own, one_group, 0, unroll=True)

    each, cap, rest = sizes.each, sizes.cap, sizes.rest
    wide = 2 * modes - 8
    few_lags = LANES // 2 - rest
    pairs = [
        jnp.concatenate([states[run_at[2 * target]], states[run_at[2 * target + 1]]], axis=0)
        for target in range(sizes.ctx)
    ]
    front = dot(jnp.concatenate(pairs, axis=0).astype(BF16), back_ref[...])
    out_lane = iota((8, LANES), 1)
    for target in range(sizes.ctx):
        lags = sums[:, target * LANES : (target + 1) * LANES]
        moves = [(cap, cap - rest), (LANES - few_lags - 2 * rest, LANES - 2 * few_lags - 2 * rest)]
        moved = [[pltpu.roll(lags, shift % LANES, 1) for shift in pair] for pair in moves]
        for chan in range(sizes.ch):
            at = slice(chan * LANES, (chan + 1) * LANES)
            mine = slice(chan * each, (chan + 1) * each)
            most, few = [jnp.concatenate([part[mine] for part in pair], axis=0) for pair in moved]
            head = front[target * 2 * modes : target * 2 * modes + wide, at]
            last = front[target * 2 * modes + wide : (target + 1) * 2 * modes, at]
            third = pltpu.roll(last, cap - rest, 1)
            beside = [
                pltpu.roll(last, cap, 1),
                jnp.where(out_lane < LANES - few_lags, third, few),
                most,
            ]
            out_ref[target * sizes.ch + chan] = jnp.concatenate(
                [
                    jnp.where(out_lane < cap, head[8 * row : 8 * row + 8], beside[row])
                    for row in range(3)
                ],
                axis=0,
            ).astype(BF16)


def owner(sizes, recv, into, back, table, leap):
    rows = sizes.own * sizes.size
    modes = leap.shape[0]
    return pl.pallas_call(
        functools.partial(owner_kernel, sizes),
        in_specs=[pl.BlockSpec(memory_space=pltpu.VMEM)] * 5,
        out_shape=jax.ShapeDtypeStruct((sizes.peers, 2 * modes - 8, LANES), BF16),
        scratch_shapes=[
            pltpu.VMEM((sizes.ctx, 4, rows, LANES), BF16),
            pltpu.VMEM((sizes.runs, rows, LANES), BF16),
            pltpu.VMEM((2 * sizes.runs + 1, rows, LANES), BF16),
            pltpu.VMEM((sizes.runs, modes, rows), F32),
            pltpu.VMEM((sizes.own, sizes.run * sizes.runs), F32),
            pltpu.SMEM((sizes.runs,), I32),
        ],
        compiler_params=pltpu.CompilerParams(vmem_limit_bytes=VMEM_LIMIT),
        name="owner_sums",
    )(recv, into, back, table, leap)


def finish_kernel(
    sizes, recv_ref, dest_ref, conv_ref, decay_ref, query_ref, out_ref, grad_ref, found, total
):
    blocks = sizes.channels // LANES
    wide = recv_ref.shape[1]
    rows = wide + 8
    modes = rows // 2
    cap, rest = sizes.cap, sizes.rest
    halves = sizes.peers // 2
    both = recv_ref[...].reshape(halves, 2, wide, LANES)
    both = jnp.concatenate([both[:, 0], both[:, 1]], axis=2)
    front = both.reshape(halves * wide, 2 * LANES)
    second = both[:, :8].astype(F32).reshape(halves * 8, 2 * LANES).astype(BF16)
    third = both[:, 8:16].astype(F32).reshape(halves * 8, 2 * LANES).astype(BF16)

    def fetch(part):
        at = pl.ds(part * 256, 256)
        owner, slot = dest_ref[1:2, at], dest_ref[2:3, at]
        half, offset = lax.shift_right_logical(owner, 1), (owner & 1) * LANES
        in_second = jnp.where(slot < rest, slot + cap + offset, -1)
        in_third = jnp.where(slot >= rest, slot + cap - rest + offset, -1)
        most = dot(front, hot_at(2 * LANES, slot + offset))
        few = dot(second, hot_at(2 * LANES, in_second)) + dot(third, hot_at(2 * LANES, in_third))
        mine = [jnp.zeros((wide, 256), F32), jnp.zeros((8, 256), F32)]
        for peer in range(halves):
            mine[0] = mine[0] + jnp.where(half == peer, most[peer * wide : (peer + 1) * wide], 0.0)
            mine[1] = mine[1] + jnp.where(half == peer, few[peer * 8 : (peer + 1) * 8], 0.0)
        for side in range(2):
            start = (2 * part + side) * rows
            for piece, first in zip(mine, (0, wide)):
                found[pl.ds(start + first, piece.shape[0]), :] = piece[
                    :, side * LANES : (side + 1) * LANES
                ]

    def turn(block):
        at = pl.ds(block * LANES, LANES)
        conv = total[pl.ds(block, sizes.tokens, stride=blocks), :].astype(BF16).T
        out_ref[at, :] = (query_ref[at, :].astype(F32) * conv.astype(F32)).astype(BF16)

    for first in range(0, blocks, 8):
        for part in range(first // 2, first // 2 + 4):
            fetch(part)
        decays = [
            decay_ref[mode * blocks + first : mode * blocks + first + 8, :]
            for mode in range(modes)
        ]
        for half in range(2):
            states = [
                found[pl.ds(first * rows + half * modes + mode, 8, stride=rows), :]
                for mode in range(modes)
            ]

            def step(token, states):
                at = (half * sizes.run + token) * blocks + first
                at = pl.ds(pl.multiple_of(at, 8), 8)
                states = [a * s for a, s in zip(decays, states)]
                total[at, :] = conv_ref[at, :] + tree_sum(states)
                return states

            lax.fori_loop(0, sizes.run, step, states, unroll=True)
        for block in range(first, first + 8):
            turn(block)

    each, few_lags = sizes.each, LANES // 2 - rest
    shape = (sizes.peers * 8, LANES)
    upper = lax.shift_right_logical(iota(shape, 0) & 7, bits(each)) == 1
    lane = iota(shape, 1)
    placed = jnp.zeros(shape, F32)
    for rows_at, count, come, go in ((16, rest, cap, 0), (8, few_lags, LANES - few_lags, 2 * rest)):
        piece = recv_ref[:, rows_at : rows_at + 8, :].astype(F32).reshape(shape)
        for part in range(2):
            start = go + part * count
            moved = pltpu.roll(piece, (start - come) % LANES, 1)
            here = (upper == (part == 1)) & (lane >= start) & (lane < start + count)
            placed = jnp.where(here, moved, placed)
    come = iota((1, sizes.peers * 8), 1)
    seat = lax.shift_right_logical(come, 3) * each + (come & (each - 1))
    wanted = sizes.group_at(seat, way_of(dest_ref))
    chosen = hot(iota((sizes.block, sizes.peers * 8), 0) == wanted)
    grad_ref[...] = dot(chosen, placed.astype(BF16))


def finish(sizes, recv, dest, conv, decay, query_proj):
    blocks = sizes.channels // LANES
    return pl.pallas_call(
        functools.partial(finish_kernel, sizes),
        in_specs=[pl.BlockSpec(memory_space=pltpu.VMEM)] * 5,
        out_shape=[
            jax.ShapeDtypeStruct((sizes.channels, sizes.tokens), BF16),
            jax.ShapeDtypeStruct((sizes.block, LANES), F32),
        ],
        scratch_shapes=[
            pltpu.VMEM(((blocks + 1) * (recv.shape[1] + 8), LANES), F32),
            pltpu.VMEM(((sizes.tokens + 1) * blocks, LANES), F32),
        ],
        compiler_params=pltpu.CompilerParams(vmem_limit_bytes=VMEM_LIMIT),
        name="finish_rows",
    )(recv, dest, conv, decay, query_proj)


def exchange(blocks):
    return lax.all_to_all(blocks, ("ctx", "ch"), split_axis=0, concat_axis=0, tiled=True)


def owners_way(sizes, args):
    query_proj, key_proj, value_proj, cotangent, positions, group_of, decay_rates, residues = args
    me = (lax.axis_index("ctx") * sizes.ch + lax.axis_index("ch")).reshape(1).astype(I32)
    groups = group_of.reshape(1, -1)
    sent, dest = pack(sizes, positions, groups, key_proj, value_proj, cotangent, query_proj)
    recv = exchange(sent)

    gains = residues * jnp.sqrt(2.0 * decay_rates)
    params = jnp.concatenate([decay_rates, gains], axis=1).T
    conv, decay = local(sizes, me, groups, params, key_proj, value_proj)
    into, back, most, table, leap = index(sizes, me, groups, dest, params)

    def fast(recv, into, back, table, leap, dest, conv, decay, *args):
        returned = exchange(owner(sizes, recv, into, back, table, leap))
        return tuple(finish(sizes, returned, dest, conv, decay, args[0]))

    def slow(recv, into, back, table, leap, dest, conv, decay, *args):
        return general_way(*args)

    return lax.cond(
        most[0, 0] <= sizes.cap - 1,
        fast,
        slow,
        recv,
        into,
        back,
        table,
        leap,
        dest,
        conv,
        decay,
        *args,
    )


def shards(*args):
    sizes = Sizes(
        lax.axis_size("ctx"), lax.axis_size("ch"), *args[0].shape, args[6].shape[0]
    )
    if not sizes.fits:
        return general_way(*args)
    return owners_way(sizes, args)


def solution(mesh):
    placed = (
        P("ch", "ctx"),
        P("ch", "ctx"),
        P("ch", "ctx"),
        P("ch", "ctx"),
        P("ctx"),
        P(),
        P(),
        P(),
    )
    return jax.shard_map(
        shards,
        mesh=mesh,
        in_specs=placed,
        out_specs=(P("ch", "ctx"), P("ch", "ctx")),
        check_vma=False,
    )
```

```python
import functools
import math

import jax
import jax.numpy as jnp
from jax import lax
from jax.experimental import pallas as pl
from jax.experimental.pallas import tpu as pltpu
from jax.sharding import PartitionSpec as P

F32 = jnp.float32
BF16 = jnp.bfloat16
I32 = jnp.int32
LANES = 128
VMEM_LIMIT = 48 * 1024 * 1024


def product(form, left, right):
    return jnp.einsum(form, left, right, precision=lax.Precision.HIGHEST)


def split_rows(extent):
    chosen = 2
    for divisor in range(2, math.isqrt(extent) + 1, 2):
        if extent % divisor == 0:
            chosen = divisor
    return chosen


def dft_tables(row_count, col_count, extent):
    row_index = jnp.arange(row_count, dtype=jnp.int32)
    col_index = jnp.arange(col_count, dtype=jnp.int32)

    def angles(left_index, right_index, modulus):
        phase = left_index[:, None] * right_index[None, :] % modulus
        return phase.astype(jnp.float32) * (2.0 * math.pi / modulus)

    row_angle = angles(row_index, row_index, row_count)
    col_angle = angles(col_index, col_index, col_count)
    twist_angle = angles(row_index, col_index, extent)
    return (
        jnp.cos(row_angle),
        jnp.sin(row_angle),
        jnp.cos(col_angle),
        jnp.sin(col_angle),
        jnp.cos(twist_angle),
        jnp.sin(twist_angle),
    )


def forward_transform(signal, tables, row_count, col_count):
    row_cos, row_sin, col_cos, col_sin, twist_cos, twist_sin = tables
    folded = signal.reshape(signal.shape[0], row_count // 2, col_count)
    mid_real = product("ka,cab->ckb", row_cos[:, : row_count // 2], folded)
    mid_imag = -product("ka,cab->ckb", row_sin[:, : row_count // 2], folded)
    turned_real = mid_real * twist_cos + mid_imag * twist_sin
    turned_imag = mid_imag * twist_cos - mid_real * twist_sin
    spec_real = product("ckb,bm->ckm", turned_real, col_cos) + product(
        "ckb,bm->ckm", turned_imag, col_sin
    )
    spec_imag = product("ckb,bm->ckm", turned_imag, col_cos) - product(
        "ckb,bm->ckm", turned_real, col_sin
    )
    return (spec_real, spec_imag)


def inverse_transform(spec_real, spec_imag, tables, row_count, col_count):
    row_cos, row_sin, col_cos, col_sin, twist_cos, twist_sin = tables
    mid_real = product("ckm,bm->ckb", spec_real, col_cos) - product(
        "ckm,bm->ckb", spec_imag, col_sin
    )
    mid_imag = product("ckm,bm->ckb", spec_imag, col_cos) + product(
        "ckm,bm->ckb", spec_real, col_sin
    )
    turned_real = mid_real * twist_cos - mid_imag * twist_sin
    turned_imag = mid_imag * twist_cos + mid_real * twist_sin
    folded = product("ak,ckb->cab", row_cos[: row_count // 2, :], turned_real) - product(
        "ak,ckb->cab", row_sin[: row_count // 2, :], turned_imag
    )
    return folded.reshape(spec_real.shape[0], -1) / float(row_count * col_count)


def spectra(gated_seq, weighted_seq, chan_groups, decay_rates, residues, seq_length):
    extent = 2 * seq_length
    row_count = split_rows(extent)
    col_count = extent // row_count
    decay_rows = decay_rates[chan_groups]
    gain_rows = residues[chan_groups]
    tap_index = jnp.arange(seq_length, dtype=jnp.float32)
    coefs = gain_rows * jnp.sqrt(2.0 * decay_rows)
    filters = jnp.sum(coefs[:, :, None] * jnp.exp(-decay_rows[:, :, None] * tap_index), axis=1)
    tables = dft_tables(row_count, col_count, extent)
    gated_real, gated_imag = forward_transform(
        gated_seq.astype(jnp.float32), tables, row_count, col_count
    )
    filter_real, filter_imag = forward_transform(filters, tables, row_count, col_count)
    weight_real, weight_imag = forward_transform(
        weighted_seq.astype(jnp.float32), tables, row_count, col_count
    )
    convolved = inverse_transform(
        filter_real * gated_real - filter_imag * gated_imag,
        filter_real * gated_imag + filter_imag * gated_real,
        tables,
        row_count,
        col_count,
    )
    lagged = inverse_transform(
        weight_real * gated_real + weight_imag * gated_imag,
        weight_imag * gated_real - weight_real * gated_imag,
        tables,
        row_count,
        col_count,
    )
    return (convolved, lagged)


def general_way(
    query_proj, key_proj, value_proj, cotangent, positions, group_of, decay_rates, residues
):
    ctx_count = lax.axis_size("ctx")
    ch_count = lax.axis_size("ch")
    ctx_rank = lax.axis_index("ctx")
    ch_rank = lax.axis_index("ch")
    local_channels, local_tokens = query_proj.shape
    half_run = local_tokens // 2
    run_count = 2 * ctx_count
    seq_length = local_tokens * ctx_count
    per_device = local_channels // ctx_count
    groups_total = decay_rates.shape[0]
    gated = (key_proj.astype(jnp.float32) * value_proj.astype(jnp.float32)).astype(jnp.bfloat16)
    weighted = (cotangent.astype(jnp.float32) * query_proj.astype(jnp.float32)).astype(jnp.bfloat16)
    run_ids = jnp.stack([positions[0], positions[half_run]]) // half_run
    all_runs = lax.all_to_all(
        jnp.broadcast_to(run_ids[None, :], (ctx_count, 2)),
        "ctx",
        split_axis=0,
        concat_axis=0,
        tiled=True,
    ).reshape(run_count)
    source_run = (
        jnp.zeros((run_count,), jnp.int32).at[all_runs].set(jnp.arange(run_count, dtype=jnp.int32))
    )

    def to_sequence(stored):
        return stored.reshape(per_device, run_count, half_run)[:, source_run, :].reshape(
            per_device, seq_length
        )

    shard_groups = lax.dynamic_slice_in_dim(group_of, ch_rank * local_channels, local_channels)
    gated_cols, weighted_cols = (
        lax.all_to_all(gated, "ctx", split_axis=0, concat_axis=1, tiled=True),
        lax.all_to_all(weighted, "ctx", split_axis=0, concat_axis=1, tiled=True),
    )
    first_channel = ch_rank * local_channels + ctx_rank * per_device
    chan_groups = lax.dynamic_slice_in_dim(group_of, first_channel, per_device)
    convolved, lagged = spectra(
        to_sequence(gated_cols),
        to_sequence(weighted_cols),
        chan_groups,
        decay_rates,
        residues,
        seq_length,
    )
    ordered = convolved.astype(jnp.bfloat16).reshape(per_device, run_count, half_run)[
        :, all_runs, :
    ]
    conv_tokens = lax.all_to_all(
        ordered.reshape(per_device, seq_length), "ctx", split_axis=1, concat_axis=0, tiled=True
    )
    output = (query_proj.astype(jnp.float32) * conv_tokens.astype(jnp.float32)).astype(jnp.bfloat16)
    lag_rows = lax.all_to_all(lagged, "ctx", split_axis=1, concat_axis=0, tiled=True)
    select_all = (
        jnp.arange(groups_total, dtype=jnp.int32)[:, None] == shard_groups[None, :]
    ).astype(jnp.float32)
    partial = jnp.dot(
        select_all, lag_rows, precision=lax.Precision.HIGHEST, preferred_element_type=jnp.float32
    ).reshape(ch_count, groups_total // ch_count, local_tokens)
    filter_grad = jnp.sum(
        lax.all_to_all(partial, "ch", split_axis=0, concat_axis=0, tiled=True), axis=0
    )
    return (output, filter_grad)


def iota(shape, dim):
    return lax.broadcasted_iota(I32, shape, dim)


def hot(flags):
    return jnp.where(flags, 1.0, 0.0).astype(BF16)


def hot_at(rows, wanted):
    row = iota((rows, wanted.shape[1]), 0).astype(F32).astype(BF16)
    one = jnp.ones((), BF16)
    return jnp.where(row == wanted.astype(F32).astype(BF16), one, jnp.zeros((), BF16))


def dot(left, right):
    return jnp.dot(left, right, preferred_element_type=F32)


def dot_lanes(left, right):
    return lax.dot_general(left, right, (((1,), (1,)), ((), ())), preferred_element_type=F32)


def two_terms(values):
    high = values.astype(BF16)
    return high, (values - high.astype(F32)).astype(BF16)


class Sizes:
    def __init__(self, ctx, ch, channels, tokens, groups):
        self.ctx, self.ch = ctx, ch
        self.peers = ctx * ch
        self.channels = channels
        self.tokens = tokens
        self.run = tokens // 2
        self.runs = 2 * ctx
        self.groups = groups
        self.block = groups // ch
        self.each = self.block // self.peers
        self.own = groups // self.peers
        self.size = channels * ch // groups
        self.cap = 80
        self.rest = LANES - self.cap
        powers = [self.block, max(self.each, 1), self.own, self.size]
        self.fits = (
            tokens == LANES
            and self.block == LANES
            and self.runs == 16
            and self.own == 16
            and self.size == 16
            and self.each * self.peers == self.block
            and self.each * 8 * self.run == 16 * LANES
            and ch == 4
            and channels % 2048 == 0
            and channels // self.peers <= 64
            and all(p & (p - 1) == 0 for p in powers)
        )

    def deal(self, count):
        way = iota((1, count), 1)
        step = 2 * lax.shift_right_logical(way, 1) + 1
        turn = step
        for _ in range(3):
            turn = (turn * (2 - step * turn)) & (self.block - 1)
        return turn, (self.each // 2) * (way & 1), step

    def seat(self, group, way):
        turn, start, _ = way
        return (turn * (group & (self.block - 1)) + start) & (self.block - 1)

    def owner(self, group, way):
        return lax.shift_right_logical(self.seat(group, way), bits(self.each))

    def place(self, group, way):
        block = lax.shift_right_logical(group, bits(self.block))
        return block * self.each + (self.seat(group, way) & (self.each - 1))

    def group_at(self, seat, way):
        _, start, step = way
        return (step * (seat - start)) & (self.block - 1)

    def group_here(self, place, me, way):
        block = lax.shift_right_logical(place, bits(self.each))
        seat = me * self.each + (place & (self.each - 1))
        return block * self.block + self.group_at(seat, way)


def bits(power):
    return power.bit_length() - 1


def way_of(dest_ref):
    return tuple(dest_ref[row : row + 1, 0:1] for row in (3, 4, 5))


def running_counts(marks, upper):
    width = upper.shape[0]
    before, counts = jnp.zeros((marks.shape[0], 1), F32), []
    for start in range(0, marks.shape[1], width):
        part = marks[:, start : start + width]
        counts.append(dot(part, upper) + before)
        before = before + jnp.sum(part.astype(F32), axis=1, keepdims=True)
    return jnp.concatenate(counts, axis=1), before


def upper_ones(width):
    return hot(iota((width, width), 0) < iota((width, width), 1))


def choose_way(sizes, group):
    count = 64
    ways = sizes.deal(count)
    low = 16
    group = group & (sizes.block - 1)
    loads = []
    for source in range(sizes.ch):
        row = group[:, source * sizes.channels : (source + 1) * sizes.channels]
        high_hot = hot(iota((sizes.block // low, sizes.channels), 0) == lax.shift_right_logical(row, 4))
        low_hot = hot(iota((low, sizes.channels), 0) == (row & (low - 1)))
        table = dot_lanes(high_hot, low_hot)
        spread = hot((iota((low, sizes.block), 1) & (low - 1)) == iota((low, sizes.block), 0))
        wide = dot(table.astype(BF16), spread)
        own = lax.shift_right_logical(iota(wide.shape, 1), 4) == iota(wide.shape, 0)
        loads.append(jnp.sum(jnp.where(own, wide, 0.0), axis=0, keepdims=True))
    loads = jnp.concatenate(loads + [jnp.zeros((8 - sizes.ch, sizes.block), F32)], axis=0)
    lanes = sizes.peers * count
    spread = [jnp.concatenate([part] * sizes.peers, axis=1) for part in ways]
    seat = sizes.seat(iota((sizes.block, lanes), 0), spread)
    peer = lax.shift_right_logical(iota((1, lanes), 1), bits(count))
    dealt = hot(lax.shift_right_logical(seat, bits(sizes.each)) == peer)
    sums = dot(loads.astype(BF16), dealt)
    fullest = sums[:, :LANES]
    for start in range(LANES, lanes, LANES):
        fullest = jnp.maximum(fullest, sums[:, start : start + LANES])
    fullest = jnp.max(jnp.maximum(fullest, pltpu.roll(fullest, count, 1)), axis=0, keepdims=True)
    score = fullest[:, :count] * float(count) + iota((1, count), 1).astype(F32)
    best = jnp.min(score, axis=1, keepdims=True)
    return tuple(
        jnp.sum(jnp.where(score == best, part.astype(F32), 0.0), axis=1, keepdims=True).astype(I32)
        for part in ways
    )


def pack_kernel(
    sizes,
    place_hbm,
    group_hbm,
    key_hbm,
    value_hbm,
    cot_hbm,
    query_hbm,
    out_ref,
    dest_ref,
    place_ref,
    group_ref,
    inputs,
    data,
    arrived,
):
    moves = [(group_hbm, group_ref), (place_hbm, place_ref)]
    for at, source in enumerate((key_hbm, value_hbm, cot_hbm, query_hbm)):
        moves.append((source, inputs.at[at]))
    copies = [
        pltpu.make_async_copy(source, target, arrived.at[at])
        for at, (source, target) in enumerate(moves)
    ]
    for copy in copies:
        copy.start()
    copies[0].wait()
    way = choose_way(sizes, group_ref[...])
    first = pl.multiple_of(lax.axis_index("ch") * sizes.channels, LANES)
    owner = sizes.owner(group_ref[:, pl.ds(first, sizes.channels)], way)
    marks = iota((sizes.peers, sizes.channels), 0) == owner
    counts, _ = running_counts(hot(marks), upper_ones(256))
    slot = jnp.sum(jnp.where(marks, counts, 0.0), axis=0, keepdims=True).astype(I32)
    dest_ref[0:1, :] = jnp.where(slot < sizes.cap - 1, owner * sizes.cap + slot, -1)
    dest_ref[1:2, :] = owner
    dest_ref[2:3, :] = slot
    for row in range(3):
        dest_ref[3 + row : 4 + row, :] = jnp.broadcast_to(way[row], (1, sizes.channels))
    dest_ref[6:8, :] = jnp.zeros((2, sizes.channels), I32)
    for copy in copies[1:]:
        copy.wait()
    across = iota((LANES, LANES), 0) ^ iota((LANES, LANES), 1)
    gated = (inputs[0].astype(F32) * inputs[1].astype(F32)).astype(BF16)
    data[:, :LANES] = dot(gated, hot(across == sizes.run - 1)).astype(BF16)
    data[:, LANES:] = (inputs[2].astype(F32) * inputs[3].astype(F32)).astype(BF16)

    shift = bits(sizes.run)
    first = lax.shift_right_logical(place_ref[0], shift)
    second = lax.shift_right_logical(place_ref[sizes.run], shift)
    run_row = jnp.where(iota((1, 1, 2 * LANES), 2) < LANES, first, second).astype(F32)
    part = 16
    spare = iota((part, sizes.cap, 1), 1) == sizes.cap - 1
    for start in range(0, sizes.peers, part):
        base = start * sizes.cap
        chosen = hot(iota((part * sizes.cap, sizes.channels), 0) == dest_ref[0:1, :] - base)
        rows = dot(chosen, data[...]).reshape(part, sizes.cap, 2 * LANES)
        out_ref[start : start + part] = jnp.where(spare, run_row, rows).astype(BF16)


def pack(sizes, positions, groups, key_proj, value_proj, cotangent, query_proj):
    return pl.pallas_call(
        functools.partial(pack_kernel, sizes),
        in_specs=[pl.BlockSpec(memory_space=pl.ANY)] * 6,
        out_specs=[pl.BlockSpec(memory_space=pltpu.VMEM)] * 2,
        out_shape=[
            jax.ShapeDtypeStruct((sizes.peers, sizes.cap, 2 * LANES), BF16),
            jax.ShapeDtypeStruct((8, sizes.channels), I32),
        ],
        scratch_shapes=[
            pltpu.SMEM(positions.shape, I32),
            pltpu.VMEM(groups.shape, I32),
            pltpu.VMEM((4, sizes.channels, sizes.tokens), BF16),
            pltpu.VMEM((sizes.channels, 2 * LANES), BF16),
            pltpu.SemaphoreType.DMA((6,)),
        ],
        compiler_params=pltpu.CompilerParams(vmem_limit_bytes=VMEM_LIMIT),
        name="pack_rows",
    )(positions, groups, key_proj, value_proj, cotangent, query_proj)


def index_kernel(
    sizes,
    me_ref,
    group_ref,
    dest_ref,
    param_ref,
    back_ref,
    over_ref,
    table_ref,
    leap_ref,
):
    me = me_ref[0]
    way = way_of(dest_ref)
    upper = upper_ones(256)
    group = group_ref[...]
    owner, place = sizes.owner(group, way), sizes.place(group, way)
    owner, place = jnp.split(owner, sizes.ch, axis=1), jnp.split(place, sizes.ch, axis=1)
    most = jnp.zeros((sizes.peers, 1), F32)
    for source in range(sizes.ch):
        marks = iota((sizes.peers, sizes.channels), 0) == owner[source]
        most = jnp.maximum(most, jnp.sum(jnp.where(marks, 1.0, 0.0), axis=1, keepdims=True))
    over_ref[...] = jnp.broadcast_to(jnp.max(most, axis=0, keepdims=True), (8, LANES)).astype(I32)

    earlier = jnp.zeros((sizes.own, 1), F32)
    for source in range(sizes.ch):
        mine = owner[source] == me
        where = jnp.where(mine, place[source], -1)
        marks = iota((sizes.own, sizes.channels), 0) == where
        counts, totals = running_counts(hot(marks), upper)
        slot = jnp.sum(counts, axis=0, keepdims=True).astype(I32)
        nth = jnp.sum(jnp.where(marks, counts + earlier, 0.0), axis=0, keepdims=True).astype(I32)
        earlier = earlier + totals
        row = jnp.where(mine, where * sizes.size + nth, -1)
        column = jnp.where(mine & (slot < sizes.cap - 1), slot, -1)
        to_row = hot(iota((256, sizes.channels), 0) == row)
        to_column = hot(iota((LANES, sizes.channels), 0) == column)
        at = slice(source * LANES, (source + 1) * LANES)
        back_ref[:, at] = dot_lanes(to_row, to_column).astype(BF16)

    modes = leap_ref.shape[0]
    terms = three_terms(param_ref[...])
    shape = (256, sizes.groups)
    wanted = sizes.group_here(lax.shift_right_logical(iota((256, 1), 0), bits(modes)), me, way)
    found = dot_lanes(hot(iota(shape, 1) == wanted), terms)
    found = three_sum(found, 1)
    mode = iota((256, 2 * modes), 0) & (modes - 1)
    lane = iota((256, 2 * modes), 1)
    rate = jnp.sum(jnp.where(lane == mode, found, 0.0), axis=1, keepdims=True)
    gain = jnp.sum(jnp.where(lane == mode + modes, found, 0.0), axis=1, keepdims=True)
    step = iota((256, sizes.run), 1).astype(F32)
    high, low = two_terms(gain * jnp.exp(-rate * step))
    table_ref[...] = jnp.concatenate([high, low], axis=1)
    shape = (sizes.groups, 256)
    wanted = sizes.group_here(lax.shift_right_logical(iota((1, 256), 1), bits(sizes.size)), me, way)
    found = three_sum(dot(terms, hot(iota(shape, 0) == wanted)), 0)
    leap_ref[...] = jnp.exp(found[:modes] * -float(sizes.run))


def three_terms(exact):
    high, rest = two_terms(exact)
    low, _ = two_terms(exact - high.astype(F32) - rest.astype(F32))
    return jnp.concatenate([high, rest, low], axis=0)


def three_sum(found, dim):
    high, rest, low = jnp.split(found, 3, axis=dim)
    return high + rest + low


def index(sizes, me, groups, dest, params):
    modes = params.shape[0] // 2
    return pl.pallas_call(
        functools.partial(index_kernel, sizes),
        in_specs=[pl.BlockSpec(memory_space=pltpu.SMEM)]
        + [pl.BlockSpec(memory_space=pltpu.VMEM)] * 3,
        out_shape=[
            jax.ShapeDtypeStruct((256, sizes.ch * LANES), BF16),
            jax.ShapeDtypeStruct((8, LANES), I32),
            jax.ShapeDtypeStruct((256, 2 * sizes.run), BF16),
            jax.ShapeDtypeStruct((modes, 256), F32),
        ],
        compiler_params=pltpu.CompilerParams(vmem_limit_bytes=VMEM_LIMIT),
        cost_estimate=pl.CostEstimate(flops=2 * 10**9, bytes_accessed=10**6, transcendentals=0),
        name="index_rows",
    )(me, groups, dest, params)


def local_kernel(
    sizes, me_ref, group_ref, param_ref, key_ref, value_ref, conv_ref, decay_ref, params, turned
):
    modes = param_ref.shape[0] // 2
    blocks = sizes.channels // LANES
    stacked = three_terms(param_ref[...])
    rows = 2 * modes
    first_lane = pl.multiple_of((me_ref[0] & (sizes.ch - 1)) * sizes.channels, LANES)
    groups = group_ref[:, pl.ds(first_lane, sizes.channels)]
    for start in range(0, sizes.channels, 256):
        chosen = hot(iota((sizes.groups, 256), 0) == groups[:, start : start + 256])
        found = three_sum(dot(stacked, chosen), 0)
        for half in range(2):
            block = start // LANES + half
            params[block * rows : (block + 1) * rows, :] = found[
                :, half * LANES : (half + 1) * LANES
            ]

    def turn(block, carry):
        at = pl.ds(pl.multiple_of(block * LANES, LANES), LANES)
        gated = (key_ref[at, :].astype(F32) * value_ref[at, :].astype(F32)).astype(BF16)
        turned[pl.ds(block, sizes.tokens, stride=blocks), :] = gated.astype(F32).T
        return carry

    lax.fori_loop(0, blocks, turn, 0)
    for first in range(0, blocks, 8):
        decays, gains = [], []
        for mode in range(modes):
            rate = params[pl.ds(first * rows + mode, 8, stride=rows), :]
            gains.append(params[pl.ds(first * rows + modes + mode, 8, stride=rows), :])
            decays.append(jnp.exp(-rate))
            decay_ref[mode * blocks + first : mode * blocks + first + 8, :] = decays[-1]
        for half in range(2):

            def step(token, states):
                at = (half * sizes.run + token) * blocks + first
                at = pl.ds(pl.multiple_of(at, 8), 8)
                value = turned[at, :]
                states = [a * s + c * value for a, c, s in zip(decays, gains, states)]
                conv_ref[at, :] = tree_sum(states)
                return states

            lax.fori_loop(0, sizes.run, step, [jnp.zeros((8, LANES), F32)] * modes)


def tree_sum(terms):
    while len(terms) > 1:
        terms = [
            terms[i] + terms[i + 1] if i + 1 < len(terms) else terms[i]
            for i in range(0, len(terms), 2)
        ]
    return terms[0]


def local(sizes, me, groups, params, key_proj, value_proj):
    modes = params.shape[0] // 2
    blocks = sizes.channels // LANES
    return pl.pallas_call(
        functools.partial(local_kernel, sizes),
        in_specs=[pl.BlockSpec(memory_space=pltpu.SMEM)]
        + [pl.BlockSpec(memory_space=pltpu.VMEM)] * 4,
        out_shape=[
            jax.ShapeDtypeStruct((sizes.tokens * blocks, LANES), F32),
            jax.ShapeDtypeStruct((modes * blocks, LANES), F32),
        ],
        scratch_shapes=[
            pltpu.VMEM(((blocks + 1) * 2 * modes, LANES), F32),
            pltpu.VMEM(((sizes.tokens + 1) * blocks, LANES), F32),
        ],
        compiler_params=pltpu.CompilerParams(vmem_limit_bytes=VMEM_LIMIT),
        cost_estimate=pl.CostEstimate(flops=4 * 10**9, bytes_accessed=3 * 10**6, transcendentals=0),
        name="local_runs",
    )(me, groups, params, key_proj, value_proj)


def owner_kernel(
    sizes,
    recv_ref,
    back_ref,
    table_ref,
    leap_ref,
    out_ref,
    merged,
    gated,
    weighted,
    states,
    sums,
    run_at,
):
    run, runs, own, size = sizes.run, sizes.runs, sizes.own, sizes.size
    rows = own * size
    weighted[runs : 2 * runs + 1] = jnp.zeros((runs + 1, rows, LANES), BF16)
    for source in range(sizes.ctx):
        tail = recv_ref[source * sizes.ch, sizes.cap - 16 : sizes.cap, :].astype(F32)
        run_at[2 * source] = tail[15, 0].astype(I32)
        run_at[2 * source + 1] = tail[15, LANES].astype(I32)
    lane = iota((rows, LANES), 1)
    nothing = jnp.zeros((sizes.rest, 2 * LANES), BF16)
    for source in range(sizes.ctx):
        block = []
        for peer in range(source * sizes.ch, (source + 1) * sizes.ch):
            block += [recv_ref[peer], nothing]
        found = dot(back_ref[...], jnp.concatenate(block, axis=0))
        found = found.astype(BF16)
        value = found[:, :LANES]
        turned = pltpu.roll(value, run, 1)
        merged[source, 0] = jnp.where(lane < run, value, turned)
        merged[source, 1] = jnp.where(lane < run, turned, value)
        merged[source, 2] = found[:, LANES:]
        merged[source, 3] = pltpu.roll(found[:, LANES:], run, 1)
    for source in range(sizes.ctx):
        first, second = run_at[2 * source], run_at[2 * source + 1]
        gated[first] = merged[source, 0]
        gated[second] = merged[source, 1]
        weighted[first + 1, :, :run] = merged[source, 2, :, :run]
        weighted[first, :, run:] = merged[source, 3, :, run:]
        weighted[second + 1, :, :run] = merged[source, 3, :, :run]
        weighted[second, :, run:] = merged[source, 2, :, run:]

    modes = states.shape[1]
    group_lane = lax.shift_right_logical(iota((modes, rows), 1), bits(size))
    carried = jnp.zeros((modes, rows), F32)
    leap = leap_ref[...]
    for at in range(runs):
        states[at] = carried
        if at + 1 < runs:
            ends = dot_lanes(table_ref[...], gated[at])
            total = ends[:modes]
            for group in range(1, own):
                piece = ends[group * modes : (group + 1) * modes]
                total = jnp.where(group_lane == group, piece, total)
            carried = carried * leap + total

    seq = run * runs

    def one_group(group, carry):
        at = pl.ds(pl.multiple_of(group * size, size), size)
        left = gated[:, at, :].reshape(runs * size, LANES).T[:run]
        right = jnp.concatenate(
            [
                weighted[1 + lag : 1 + lag + runs, at, :].reshape(runs * size, LANES)
                for lag in range(0, runs, 2)
            ],
            axis=1,
        )
        gram = jnp.concatenate([dot(left, right), jnp.zeros((run, LANES), F32)], axis=1)
        skewed = pltpu.roll(gram, seq + LANES - (run - 1), 1, stride=1, stride_axis=0)
        sums[pl.ds(group, 1), :] = jnp.sum(skewed, axis=0, keepdims=True)[:, :seq]
        return carry

    lax.fori_loop(0, own, one_group, 0, unroll=True)

    each, cap, rest = sizes.each, sizes.cap, sizes.rest
    wide = 2 * modes - 8
    few_lags = LANES // 2 - rest
    pairs = [
        jnp.concatenate([states[run_at[2 * target]], states[run_at[2 * target + 1]]], axis=0)
        for target in range(sizes.ctx)
    ]
    front = dot(jnp.concatenate(pairs, axis=0).astype(BF16), back_ref[...])
    out_lane = iota((8, LANES), 1)
    for target in range(sizes.ctx):
        lags = sums[:, target * LANES : (target + 1) * LANES]
        moves = [(cap, cap - rest), (LANES - few_lags - 2 * rest, LANES - 2 * few_lags - 2 * rest)]
        moved = [[pltpu.roll(lags, shift % LANES, 1) for shift in pair] for pair in moves]
        for chan in range(sizes.ch):
            at = slice(chan * LANES, (chan + 1) * LANES)
            mine = slice(chan * each, (chan + 1) * each)
            most, few = [jnp.concatenate([part[mine] for part in pair], axis=0) for pair in moved]
            head = front[target * 2 * modes : target * 2 * modes + wide, at]
            last = front[target * 2 * modes + wide : (target + 1) * 2 * modes, at]
            third = pltpu.roll(last, cap - rest, 1)
            beside = [
                pltpu.roll(last, cap, 1),
                jnp.where(out_lane < LANES - few_lags, third, few),
                most,
            ]
            out_ref[target * sizes.ch + chan] = jnp.concatenate(
                [
                    jnp.where(out_lane < cap, head[8 * row : 8 * row + 8], beside[row])
                    for row in range(3)
                ],
                axis=0,
            ).astype(BF16)


def owner(sizes, recv, back, table, leap):
    rows = sizes.own * sizes.size
    modes = leap.shape[0]
    return pl.pallas_call(
        functools.partial(owner_kernel, sizes),
        in_specs=[pl.BlockSpec(memory_space=pltpu.VMEM)] * 4,
        out_shape=jax.ShapeDtypeStruct((sizes.peers, 2 * modes - 8, LANES), BF16),
        scratch_shapes=[
            pltpu.VMEM((sizes.ctx, 4, rows, LANES), BF16),
            pltpu.VMEM((sizes.runs, rows, LANES), BF16),
            pltpu.VMEM((2 * sizes.runs + 1, rows, LANES), BF16),
            pltpu.VMEM((sizes.runs, modes, rows), F32),
            pltpu.VMEM((sizes.own, sizes.run * sizes.runs), F32),
            pltpu.SMEM((sizes.runs,), I32),
        ],
        compiler_params=pltpu.CompilerParams(vmem_limit_bytes=VMEM_LIMIT),
        name="owner_sums",
    )(recv, back, table, leap)


def finish_kernel(
    sizes, recv_ref, dest_ref, conv_ref, decay_ref, query_ref, out_ref, grad_ref, found, total
):
    blocks = sizes.channels // LANES
    wide = recv_ref.shape[1]
    rows = wide + 8
    modes = rows // 2
    cap, rest = sizes.cap, sizes.rest
    halves = sizes.peers // 2
    both = recv_ref[...].reshape(halves, 2, wide, LANES)
    both = jnp.concatenate([both[:, 0], both[:, 1]], axis=2)
    front = both.reshape(halves * wide, 2 * LANES)
    second = both[:, :8].astype(F32).reshape(halves * 8, 2 * LANES).astype(BF16)
    third = both[:, 8:16].astype(F32).reshape(halves * 8, 2 * LANES).astype(BF16)

    def fetch(part):
        at = pl.ds(part * 256, 256)
        owner, slot = dest_ref[1:2, at], dest_ref[2:3, at]
        half, offset = lax.shift_right_logical(owner, 1), (owner & 1) * LANES
        in_second = jnp.where(slot < rest, slot + cap + offset, -1)
        in_third = jnp.where(slot >= rest, slot + cap - rest + offset, -1)
        most = dot(front, hot_at(2 * LANES, slot + offset))
        few = dot(second, hot_at(2 * LANES, in_second)) + dot(third, hot_at(2 * LANES, in_third))
        mine = [jnp.zeros((wide, 256), F32), jnp.zeros((8, 256), F32)]
        for peer in range(halves):
            mine[0] = mine[0] + jnp.where(half == peer, most[peer * wide : (peer + 1) * wide], 0.0)
            mine[1] = mine[1] + jnp.where(half == peer, few[peer * 8 : (peer + 1) * 8], 0.0)
        for side in range(2):
            start = (2 * part + side) * rows
            for piece, first in zip(mine, (0, wide)):
                found[pl.ds(start + first, piece.shape[0]), :] = piece[
                    :, side * LANES : (side + 1) * LANES
                ]

    def turn(block):
        at = pl.ds(block * LANES, LANES)
        conv = total[pl.ds(block, sizes.tokens, stride=blocks), :].astype(BF16).T
        out_ref[at, :] = (query_ref[at, :].astype(F32) * conv.astype(F32)).astype(BF16)

    for first in range(0, blocks, 8):
        for part in range(first // 2, first // 2 + 4):
            fetch(part)
        decays = [
            decay_ref[mode * blocks + first : mode * blocks + first + 8, :]
            for mode in range(modes)
        ]
        for half in range(2):
            states = [
                found[pl.ds(first * rows + half * modes + mode, 8, stride=rows), :]
                for mode in range(modes)
            ]

            def step(token, states):
                at = (half * sizes.run + token) * blocks + first
                at = pl.ds(pl.multiple_of(at, 8), 8)
                states = [a * s for a, s in zip(decays, states)]
                total[at, :] = conv_ref[at, :] + tree_sum(states)
                return states

            lax.fori_loop(0, sizes.run, step, states, unroll=True)
        for block in range(first, first + 8):
            turn(block)

    each, few_lags = sizes.each, LANES // 2 - rest
    shape = (sizes.peers * 8, LANES)
    upper = lax.shift_right_logical(iota(shape, 0) & 7, bits(each)) == 1
    lane = iota(shape, 1)
    placed = jnp.zeros(shape, F32)
    for rows_at, count, come, go in ((16, rest, cap, 0), (8, few_lags, LANES - few_lags, 2 * rest)):
        piece = recv_ref[:, rows_at : rows_at + 8, :].astype(F32).reshape(shape)
        for part in range(2):
            start = go + part * count
            moved = pltpu.roll(piece, (start - come) % LANES, 1)
            here = (upper == (part == 1)) & (lane >= start) & (lane < start + count)
            placed = jnp.where(here, moved, placed)
    come = iota((1, sizes.peers * 8), 1)
    seat = lax.shift_right_logical(come, 3) * each + (come & (each - 1))
    wanted = sizes.group_at(seat, way_of(dest_ref))
    chosen = hot(iota((sizes.block, sizes.peers * 8), 0) == wanted)
    grad_ref[...] = dot(chosen, placed.astype(BF16))


def finish(sizes, recv, dest, conv, decay, query_proj):
    blocks = sizes.channels // LANES
    return pl.pallas_call(
        functools.partial(finish_kernel, sizes),
        in_specs=[pl.BlockSpec(memory_space=pltpu.VMEM)] * 5,
        out_shape=[
            jax.ShapeDtypeStruct((sizes.channels, sizes.tokens), BF16),
            jax.ShapeDtypeStruct((sizes.block, LANES), F32),
        ],
        scratch_shapes=[
            pltpu.VMEM(((blocks + 1) * (recv.shape[1] + 8), LANES), F32),
            pltpu.VMEM(((sizes.tokens + 1) * blocks, LANES), F32),
        ],
        compiler_params=pltpu.CompilerParams(vmem_limit_bytes=VMEM_LIMIT),
        name="finish_rows",
    )(recv, dest, conv, decay, query_proj)


def exchange(blocks):
    return lax.all_to_all(blocks, ("ctx", "ch"), split_axis=0, concat_axis=0, tiled=True)


def owners_way(sizes, args):
    query_proj, key_proj, value_proj, cotangent, positions, group_of, decay_rates, residues = args
    me = (lax.axis_index("ctx") * sizes.ch + lax.axis_index("ch")).reshape(1).astype(I32)
    groups = group_of.reshape(1, -1)
    sent, dest = pack(sizes, positions, groups, key_proj, value_proj, cotangent, query_proj)
    recv = exchange(sent)

    gains = residues * jnp.sqrt(2.0 * decay_rates)
    params = jnp.concatenate([decay_rates, gains], axis=1).T
    conv, decay = local(sizes, me, groups, params, key_proj, value_proj)
    back, most, table, leap = index(sizes, me, groups, dest, params)

    def fast(recv, back, table, leap, dest, conv, decay, *args):
        returned = exchange(owner(sizes, recv, back, table, leap))
        return tuple(finish(sizes, returned, dest, conv, decay, args[0]))

    def slow(recv, back, table, leap, dest, conv, decay, *args):
        return general_way(*args)

    return lax.cond(
        most[0, 0] <= sizes.cap - 1,
        fast,
        slow,
        recv,
        back,
        table,
        leap,
        dest,
        conv,
        decay,
        *args,
    )


def shards(*args):
    sizes = Sizes(
        lax.axis_size("ctx"), lax.axis_size("ch"), *args[0].shape, args[6].shape[0]
    )
    if not sizes.fits:
        return general_way(*args)
    return owners_way(sizes, args)


def solution(mesh):
    placed = (
        P("ch", "ctx"),
        P("ch", "ctx"),
        P("ch", "ctx"),
        P("ch", "ctx"),
        P("ctx"),
        P(),
        P(),
        P(),
    )
    return jax.shard_map(
        shards,
        mesh=mesh,
        in_specs=placed,
        out_specs=(P("ch", "ctx"), P("ch", "ctx")),
        check_vma=False,
    )
```

```python
import functools
import math

import jax
import jax.numpy as jnp
from jax import lax
from jax.experimental import pallas as pl
from jax.experimental.pallas import tpu as pltpu
from jax.sharding import PartitionSpec as P

F32 = jnp.float32
BF16 = jnp.bfloat16
I32 = jnp.int32
LANES = 128
VMEM_LIMIT = 48 * 1024 * 1024


def product(form, left, right):
    return jnp.einsum(form, left, right, precision=lax.Precision.HIGHEST)


def split_rows(extent):
    chosen = 2
    for divisor in range(2, math.isqrt(extent) + 1, 2):
        if extent % divisor == 0:
            chosen = divisor
    return chosen


def dft_tables(row_count, col_count, extent):
    row_index = jnp.arange(row_count, dtype=jnp.int32)
    col_index = jnp.arange(col_count, dtype=jnp.int32)

    def angles(left_index, right_index, modulus):
        phase = left_index[:, None] * right_index[None, :] % modulus
        return phase.astype(jnp.float32) * (2.0 * math.pi / modulus)

    row_angle = angles(row_index, row_index, row_count)
    col_angle = angles(col_index, col_index, col_count)
    twist_angle = angles(row_index, col_index, extent)
    return (
        jnp.cos(row_angle),
        jnp.sin(row_angle),
        jnp.cos(col_angle),
        jnp.sin(col_angle),
        jnp.cos(twist_angle),
        jnp.sin(twist_angle),
    )


def forward_transform(signal, tables, row_count, col_count):
    row_cos, row_sin, col_cos, col_sin, twist_cos, twist_sin = tables
    folded = signal.reshape(signal.shape[0], row_count // 2, col_count)
    mid_real = product("ka,cab->ckb", row_cos[:, : row_count // 2], folded)
    mid_imag = -product("ka,cab->ckb", row_sin[:, : row_count // 2], folded)
    turned_real = mid_real * twist_cos + mid_imag * twist_sin
    turned_imag = mid_imag * twist_cos - mid_real * twist_sin
    spec_real = product("ckb,bm->ckm", turned_real, col_cos) + product(
        "ckb,bm->ckm", turned_imag, col_sin
    )
    spec_imag = product("ckb,bm->ckm", turned_imag, col_cos) - product(
        "ckb,bm->ckm", turned_real, col_sin
    )
    return (spec_real, spec_imag)


def inverse_transform(spec_real, spec_imag, tables, row_count, col_count):
    row_cos, row_sin, col_cos, col_sin, twist_cos, twist_sin = tables
    mid_real = product("ckm,bm->ckb", spec_real, col_cos) - product(
        "ckm,bm->ckb", spec_imag, col_sin
    )
    mid_imag = product("ckm,bm->ckb", spec_imag, col_cos) + product(
        "ckm,bm->ckb", spec_real, col_sin
    )
    turned_real = mid_real * twist_cos - mid_imag * twist_sin
    turned_imag = mid_imag * twist_cos + mid_real * twist_sin
    folded = product("ak,ckb->cab", row_cos[: row_count // 2, :], turned_real) - product(
        "ak,ckb->cab", row_sin[: row_count // 2, :], turned_imag
    )
    return folded.reshape(spec_real.shape[0], -1) / float(row_count * col_count)


def spectra(gated_seq, weighted_seq, chan_groups, decay_rates, residues, seq_length):
    extent = 2 * seq_length
    row_count = split_rows(extent)
    col_count = extent // row_count
    decay_rows = decay_rates[chan_groups]
    gain_rows = residues[chan_groups]
    tap_index = jnp.arange(seq_length, dtype=jnp.float32)
    coefs = gain_rows * jnp.sqrt(2.0 * decay_rows)
    filters = jnp.sum(coefs[:, :, None] * jnp.exp(-decay_rows[:, :, None] * tap_index), axis=1)
    tables = dft_tables(row_count, col_count, extent)
    gated_real, gated_imag = forward_transform(
        gated_seq.astype(jnp.float32), tables, row_count, col_count
    )
    filter_real, filter_imag = forward_transform(filters, tables, row_count, col_count)
    weight_real, weight_imag = forward_transform(
        weighted_seq.astype(jnp.float32), tables, row_count, col_count
    )
    convolved = inverse_transform(
        filter_real * gated_real - filter_imag * gated_imag,
        filter_real * gated_imag + filter_imag * gated_real,
        tables,
        row_count,
        col_count,
    )
    lagged = inverse_transform(
        weight_real * gated_real + weight_imag * gated_imag,
        weight_imag * gated_real - weight_real * gated_imag,
        tables,
        row_count,
        col_count,
    )
    return (convolved, lagged)


def general_way(
    query_proj, key_proj, value_proj, cotangent, positions, group_of, decay_rates, residues
):
    ctx_count = lax.axis_size("ctx")
    ch_count = lax.axis_size("ch")
    ctx_rank = lax.axis_index("ctx")
    ch_rank = lax.axis_index("ch")
    local_channels, local_tokens = query_proj.shape
    half_run = local_tokens // 2
    run_count = 2 * ctx_count
    seq_length = local_tokens * ctx_count
    per_device = local_channels // ctx_count
    groups_total = decay_rates.shape[0]
    gated = (key_proj.astype(jnp.float32) * value_proj.astype(jnp.float32)).astype(jnp.bfloat16)
    weighted = (cotangent.astype(jnp.float32) * query_proj.astype(jnp.float32)).astype(jnp.bfloat16)
    run_ids = jnp.stack([positions[0], positions[half_run]]) // half_run
    all_runs = lax.all_to_all(
        jnp.broadcast_to(run_ids[None, :], (ctx_count, 2)),
        "ctx",
        split_axis=0,
        concat_axis=0,
        tiled=True,
    ).reshape(run_count)
    source_run = (
        jnp.zeros((run_count,), jnp.int32).at[all_runs].set(jnp.arange(run_count, dtype=jnp.int32))
    )

    def to_sequence(stored):
        return stored.reshape(per_device, run_count, half_run)[:, source_run, :].reshape(
            per_device, seq_length
        )

    shard_groups = lax.dynamic_slice_in_dim(group_of, ch_rank * local_channels, local_channels)
    gated_cols, weighted_cols = (
        lax.all_to_all(gated, "ctx", split_axis=0, concat_axis=1, tiled=True),
        lax.all_to_all(weighted, "ctx", split_axis=0, concat_axis=1, tiled=True),
    )
    first_channel = ch_rank * local_channels + ctx_rank * per_device
    chan_groups = lax.dynamic_slice_in_dim(group_of, first_channel, per_device)
    convolved, lagged = spectra(
        to_sequence(gated_cols),
        to_sequence(weighted_cols),
        chan_groups,
        decay_rates,
        residues,
        seq_length,
    )
    ordered = convolved.astype(jnp.bfloat16).reshape(per_device, run_count, half_run)[
        :, all_runs, :
    ]
    conv_tokens = lax.all_to_all(
        ordered.reshape(per_device, seq_length), "ctx", split_axis=1, concat_axis=0, tiled=True
    )
    output = (query_proj.astype(jnp.float32) * conv_tokens.astype(jnp.float32)).astype(jnp.bfloat16)
    lag_rows = lax.all_to_all(lagged, "ctx", split_axis=1, concat_axis=0, tiled=True)
    select_all = (
        jnp.arange(groups_total, dtype=jnp.int32)[:, None] == shard_groups[None, :]
    ).astype(jnp.float32)
    partial = jnp.dot(
        select_all, lag_rows, precision=lax.Precision.HIGHEST, preferred_element_type=jnp.float32
    ).reshape(ch_count, groups_total // ch_count, local_tokens)
    filter_grad = jnp.sum(
        lax.all_to_all(partial, "ch", split_axis=0, concat_axis=0, tiled=True), axis=0
    )
    return (output, filter_grad)


def iota(shape, dim):
    return lax.broadcasted_iota(I32, shape, dim)


def hot(flags):
    return jnp.where(flags, 1.0, 0.0).astype(BF16)


def hot_at(rows, wanted):
    row = iota((rows, wanted.shape[1]), 0).astype(F32).astype(BF16)
    one = jnp.ones((), BF16)
    return jnp.where(row == wanted.astype(F32).astype(BF16), one, jnp.zeros((), BF16))


def dot(left, right):
    return jnp.dot(left, right, preferred_element_type=F32)


def dot_lanes(left, right):
    return lax.dot_general(left, right, (((1,), (1,)), ((), ())), preferred_element_type=F32)


def two_terms(values):
    high = values.astype(BF16)
    return high, (values - high.astype(F32)).astype(BF16)


class Sizes:
    def __init__(self, ctx, ch, channels, tokens, groups):
        self.ctx, self.ch = ctx, ch
        self.peers = ctx * ch
        self.channels = channels
        self.tokens = tokens
        self.run = tokens // 2
        self.runs = 2 * ctx
        self.groups = groups
        self.block = groups // ch
        self.each = self.block // self.peers
        self.own = groups // self.peers
        self.size = channels * ch // groups
        self.cap = 80
        self.rest = LANES - self.cap
        powers = [self.block, max(self.each, 1), self.own, self.size]
        self.fits = (
            tokens == LANES
            and self.block == LANES
            and self.runs == 16
            and self.own == 16
            and self.size == 16
            and self.each * self.peers == self.block
            and self.each * 8 * self.run == 16 * LANES
            and ch == 4
            and channels % 2048 == 0
            and channels // self.peers <= 64
            and all(p & (p - 1) == 0 for p in powers)
        )

    def deal(self, count):
        way = iota((1, count), 1)
        step = 2 * lax.shift_right_logical(way, 1) + 1
        turn = step
        for _ in range(3):
            turn = (turn * (2 - step * turn)) & (self.block - 1)
        return turn, (self.each // 2) * (way & 1), step

    def seat(self, group, way):
        turn, start, _ = way
        return (turn * (group & (self.block - 1)) + start) & (self.block - 1)

    def owner(self, group, way):
        return lax.shift_right_logical(self.seat(group, way), bits(self.each))

    def place(self, group, way):
        block = lax.shift_right_logical(group, bits(self.block))
        return block * self.each + (self.seat(group, way) & (self.each - 1))

    def group_at(self, seat, way):
        _, start, step = way
        return (step * (seat - start)) & (self.block - 1)

    def group_here(self, place, me, way):
        block = lax.shift_right_logical(place, bits(self.each))
        seat = me * self.each + (place & (self.each - 1))
        return block * self.block + self.group_at(seat, way)


def bits(power):
    return power.bit_length() - 1


def way_of(dest_ref):
    return tuple(dest_ref[row : row + 1, 0:1] for row in (3, 4, 5))


def running_counts(marks, upper):
    width = upper.shape[0]
    before, counts = jnp.zeros((marks.shape[0], 1), F32), []
    for start in range(0, marks.shape[1], width):
        part = marks[:, start : start + width]
        counts.append(dot(part, upper) + before)
        before = before + jnp.sum(part.astype(F32), axis=1, keepdims=True)
    return jnp.concatenate(counts, axis=1), before


def upper_ones(width):
    return hot(iota((width, width), 0) < iota((width, width), 1))


def choose_way(sizes, group):
    count = 64
    ways = sizes.deal(count)
    low = 16
    group = group & (sizes.block - 1)
    loads = []
    for source in range(sizes.ch):
        row = group[:, source * sizes.channels : (source + 1) * sizes.channels]
        high_hot = hot(iota((sizes.block // low, sizes.channels), 0) == lax.shift_right_logical(row, 4))
        low_hot = hot(iota((low, sizes.channels), 0) == (row & (low - 1)))
        table = dot_lanes(high_hot, low_hot)
        spread = hot((iota((low, sizes.block), 1) & (low - 1)) == iota((low, sizes.block), 0))
        wide = dot(table.astype(BF16), spread)
        own = lax.shift_right_logical(iota(wide.shape, 1), 4) == iota(wide.shape, 0)
        loads.append(jnp.sum(jnp.where(own, wide, 0.0), axis=0, keepdims=True))
    loads = jnp.concatenate(loads + [jnp.zeros((8 - sizes.ch, sizes.block), F32)], axis=0)
    lanes = sizes.peers * count
    spread = [jnp.concatenate([part] * sizes.peers, axis=1) for part in ways]
    seat = sizes.seat(iota((sizes.block, lanes), 0), spread)
    peer = lax.shift_right_logical(iota((1, lanes), 1), bits(count))
    dealt = hot(lax.shift_right_logical(seat, bits(sizes.each)) == peer)
    sums = dot(loads.astype(BF16), dealt)
    fullest = sums[:, :LANES]
    for start in range(LANES, lanes, LANES):
        fullest = jnp.maximum(fullest, sums[:, start : start + LANES])
    fullest = jnp.max(jnp.maximum(fullest, pltpu.roll(fullest, count, 1)), axis=0, keepdims=True)
    score = fullest[:, :count] * float(count) + iota((1, count), 1).astype(F32)
    best = jnp.min(score, axis=1, keepdims=True)
    return tuple(
        jnp.sum(jnp.where(score == best, part.astype(F32), 0.0), axis=1, keepdims=True).astype(I32)
        for part in ways
    )


def pack_kernel(
    sizes,
    place_hbm,
    group_hbm,
    key_hbm,
    value_hbm,
    cot_hbm,
    query_hbm,
    out_ref,
    dest_ref,
    place_ref,
    group_ref,
    inputs,
    data,
    arrived,
):
    moves = [(group_hbm, group_ref), (place_hbm, place_ref)]
    for at, source in enumerate((key_hbm, value_hbm, cot_hbm, query_hbm)):
        moves.append((source, inputs.at[at]))
    copies = [
        pltpu.make_async_copy(source, target, arrived.at[at])
        for at, (source, target) in enumerate(moves)
    ]
    for copy in copies:
        copy.start()
    copies[0].wait()
    way = choose_way(sizes, group_ref[...])
    first = pl.multiple_of(lax.axis_index("ch") * sizes.channels, LANES)
    owner = sizes.owner(group_ref[:, pl.ds(first, sizes.channels)], way)
    marks = iota((sizes.peers, sizes.channels), 0) == owner
    counts, _ = running_counts(hot(marks), upper_ones(256))
    slot = jnp.sum(jnp.where(marks, counts, 0.0), axis=0, keepdims=True).astype(I32)
    dest_ref[0:1, :] = jnp.where(slot < sizes.cap - 1, owner * sizes.cap + slot, -1)
    dest_ref[1:2, :] = owner
    dest_ref[2:3, :] = slot
    for row in range(3):
        dest_ref[3 + row : 4 + row, :] = jnp.broadcast_to(way[row], (1, sizes.channels))
    dest_ref[6:8, :] = jnp.zeros((2, sizes.channels), I32)
    for copy in copies[1:]:
        copy.wait()
    across = iota((LANES, LANES), 0) ^ iota((LANES, LANES), 1)
    gated = (inputs[0].astype(F32) * inputs[1].astype(F32)).astype(BF16)
    data[:, :LANES] = dot(gated, hot(across == sizes.run - 1)).astype(BF16)
    data[:, LANES:] = (inputs[2].astype(F32) * inputs[3].astype(F32)).astype(BF16)

    shift = bits(sizes.run)
    first = lax.shift_right_logical(place_ref[0], shift)
    second = lax.shift_right_logical(place_ref[sizes.run], shift)
    run_row = jnp.where(iota((1, 1, 2 * LANES), 2) < LANES, first, second).astype(F32)
    part = 16
    spare = iota((part, sizes.cap, 1), 1) == sizes.cap - 1
    for start in range(0, sizes.peers, part):
        base = start * sizes.cap
        chosen = hot(iota((part * sizes.cap, sizes.channels), 0) == dest_ref[0:1, :] - base)
        rows = dot(chosen, data[...]).reshape(part, sizes.cap, 2 * LANES)
        out_ref[start : start + part] = jnp.where(spare, run_row, rows).astype(BF16)


def pack(sizes, positions, groups, key_proj, value_proj, cotangent, query_proj):
    return pl.pallas_call(
        functools.partial(pack_kernel, sizes),
        in_specs=[pl.BlockSpec(memory_space=pl.ANY)] * 6,
        out_specs=[pl.BlockSpec(memory_space=pltpu.VMEM)] * 2,
        out_shape=[
            jax.ShapeDtypeStruct((sizes.peers, sizes.cap, 2 * LANES), BF16),
            jax.ShapeDtypeStruct((8, sizes.channels), I32),
        ],
        scratch_shapes=[
            pltpu.SMEM(positions.shape, I32),
            pltpu.VMEM(groups.shape, I32),
            pltpu.VMEM((4, sizes.channels, sizes.tokens), BF16),
            pltpu.VMEM((sizes.channels, 2 * LANES), BF16),
            pltpu.SemaphoreType.DMA((6,)),
        ],
        compiler_params=pltpu.CompilerParams(vmem_limit_bytes=VMEM_LIMIT),
        name="pack_rows",
    )(positions, groups, key_proj, value_proj, cotangent, query_proj)


def index_kernel(
    sizes,
    me_ref,
    group_ref,
    dest_ref,
    param_ref,
    back_ref,
    over_ref,
    table_ref,
    leap_ref,
):
    me = me_ref[0]
    way = way_of(dest_ref)
    upper = upper_ones(256)
    group = group_ref[...]
    owner, place = sizes.owner(group, way), sizes.place(group, way)
    owner, place = jnp.split(owner, sizes.ch, axis=1), jnp.split(place, sizes.ch, axis=1)
    most = jnp.zeros((sizes.peers, 1), F32)
    for source in range(sizes.ch):
        marks = iota((sizes.peers, sizes.channels), 0) == owner[source]
        most = jnp.maximum(most, jnp.sum(jnp.where(marks, 1.0, 0.0), axis=1, keepdims=True))
    over_ref[...] = jnp.broadcast_to(jnp.max(most, axis=0, keepdims=True), (8, LANES)).astype(I32)

    earlier = jnp.zeros((sizes.own, 1), F32)
    for source in range(sizes.ch):
        mine = owner[source] == me
        where = jnp.where(mine, place[source], -1)
        marks = iota((sizes.own, sizes.channels), 0) == where
        counts, totals = running_counts(hot(marks), upper)
        slot = jnp.sum(counts, axis=0, keepdims=True).astype(I32)
        nth = jnp.sum(jnp.where(marks, counts + earlier, 0.0), axis=0, keepdims=True).astype(I32)
        earlier = earlier + totals
        row = jnp.where(mine, where * sizes.size + nth, -1)
        column = jnp.where(mine & (slot < sizes.cap - 1), slot, -1)
        to_row = hot(iota((256, sizes.channels), 0) == row)
        to_column = hot(iota((LANES, sizes.channels), 0) == column)
        at = slice(source * LANES, (source + 1) * LANES)
        back_ref[:, at] = dot_lanes(to_row, to_column).astype(BF16)

    modes = leap_ref.shape[0]
    terms = three_terms(param_ref[...])
    shape = (256, sizes.groups)
    wanted = sizes.group_here(lax.shift_right_logical(iota((256, 1), 0), bits(modes)), me, way)
    found = dot_lanes(hot(iota(shape, 1) == wanted), terms)
    found = three_sum(found, 1)
    mode = iota((256, 2 * modes), 0) & (modes - 1)
    lane = iota((256, 2 * modes), 1)
    rate = jnp.sum(jnp.where(lane == mode, found, 0.0), axis=1, keepdims=True)
    gain = jnp.sum(jnp.where(lane == mode + modes, found, 0.0), axis=1, keepdims=True)
    step = iota((256, sizes.run), 1).astype(F32)
    high, low = two_terms(gain * jnp.exp(-rate * step))
    table_ref[...] = jnp.concatenate([high, low], axis=1)
    shape = (sizes.groups, 256)
    wanted = sizes.group_here(lax.shift_right_logical(iota((1, 256), 1), bits(sizes.size)), me, way)
    found = three_sum(dot(terms, hot(iota(shape, 0) == wanted)), 0)
    leap_ref[...] = jnp.exp(found[:modes] * -float(sizes.run))


def three_terms(exact):
    high, rest = two_terms(exact)
    low, _ = two_terms(exact - high.astype(F32) - rest.astype(F32))
    return jnp.concatenate([high, rest, low], axis=0)


def three_sum(found, dim):
    high, rest, low = jnp.split(found, 3, axis=dim)
    return high + rest + low


def index(sizes, me, groups, dest, params):
    modes = params.shape[0] // 2
    return pl.pallas_call(
        functools.partial(index_kernel, sizes),
        in_specs=[pl.BlockSpec(memory_space=pltpu.SMEM)]
        + [pl.BlockSpec(memory_space=pltpu.VMEM)] * 3,
        out_shape=[
            jax.ShapeDtypeStruct((256, sizes.ch * LANES), BF16),
            jax.ShapeDtypeStruct((8, LANES), I32),
            jax.ShapeDtypeStruct((256, 2 * sizes.run), BF16),
            jax.ShapeDtypeStruct((modes, 256), F32),
        ],
        compiler_params=pltpu.CompilerParams(vmem_limit_bytes=VMEM_LIMIT),
        cost_estimate=pl.CostEstimate(flops=2 * 10**9, bytes_accessed=10**6, transcendentals=0),
        name="index_rows",
    )(me, groups, dest, params)


def local_kernel(
    sizes, me_ref, group_ref, param_ref, key_ref, value_ref, conv_ref, decay_ref, params, turned
):
    modes = param_ref.shape[0] // 2
    blocks = sizes.channels // LANES
    stacked = three_terms(param_ref[...])
    rows = 2 * modes
    first_lane = pl.multiple_of((me_ref[0] & (sizes.ch - 1)) * sizes.channels, LANES)
    groups = group_ref[:, pl.ds(first_lane, sizes.channels)]
    for start in range(0, sizes.channels, 256):
        chosen = hot(iota((sizes.groups, 256), 0) == groups[:, start : start + 256])
        found = three_sum(dot(stacked, chosen), 0)
        for half in range(2):
            block = start // LANES + half
            params[block * rows : (block + 1) * rows, :] = found[
                :, half * LANES : (half + 1) * LANES
            ]

    def turn(block, carry):
        at = pl.ds(pl.multiple_of(block * LANES, LANES), LANES)
        gated = (key_ref[at, :].astype(F32) * value_ref[at, :].astype(F32)).astype(BF16)
        turned[pl.ds(block, sizes.tokens, stride=blocks), :] = gated.astype(F32).T
        return carry

    lax.fori_loop(0, blocks, turn, 0)
    for first in range(0, blocks, 8):
        decays, gains = [], []
        for mode in range(modes):
            rate = params[pl.ds(first * rows + mode, 8, stride=rows), :]
            gains.append(params[pl.ds(first * rows + modes + mode, 8, stride=rows), :])
            decays.append(jnp.exp(-rate))
            decay_ref[mode * blocks + first : mode * blocks + first + 8, :] = decays[-1]
        for half in range(2):

            def step(token, states):
                at = (half * sizes.run + token) * blocks + first
                at = pl.ds(pl.multiple_of(at, 8), 8)
                value = turned[at, :]
                states = [a * s + c * value for a, c, s in zip(decays, gains, states)]
                conv_ref[at, :] = tree_sum(states)
                return states

            lax.fori_loop(0, sizes.run, step, [jnp.zeros((8, LANES), F32)] * modes)


def tree_sum(terms):
    while len(terms) > 1:
        terms = [
            terms[i] + terms[i + 1] if i + 1 < len(terms) else terms[i]
            for i in range(0, len(terms), 2)
        ]
    return terms[0]


def local(sizes, me, groups, params, key_proj, value_proj):
    modes = params.shape[0] // 2
    blocks = sizes.channels // LANES
    return pl.pallas_call(
        functools.partial(local_kernel, sizes),
        in_specs=[pl.BlockSpec(memory_space=pltpu.SMEM)]
        + [pl.BlockSpec(memory_space=pltpu.VMEM)] * 4,
        out_shape=[
            jax.ShapeDtypeStruct((sizes.tokens * blocks, LANES), F32),
            jax.ShapeDtypeStruct((modes * blocks, LANES), F32),
        ],
        scratch_shapes=[
            pltpu.VMEM(((blocks + 1) * 2 * modes, LANES), F32),
            pltpu.VMEM(((sizes.tokens + 1) * blocks, LANES), F32),
        ],
        compiler_params=pltpu.CompilerParams(vmem_limit_bytes=VMEM_LIMIT),
        cost_estimate=pl.CostEstimate(flops=4 * 10**9, bytes_accessed=3 * 10**6, transcendentals=0),
        name="local_runs",
    )(me, groups, params, key_proj, value_proj)


def owner_kernel(
    sizes,
    recv_ref,
    back_ref,
    table_ref,
    leap_ref,
    out_ref,
    merged,
    gated,
    weighted,
    states,
    sums,
    run_at,
):
    run, runs, own, size = sizes.run, sizes.runs, sizes.own, sizes.size
    rows = own * size
    weighted[runs : 2 * runs + 1] = jnp.zeros((runs + 1, rows, LANES), BF16)
    for source in range(sizes.ctx):
        tail = recv_ref[source * sizes.ch, sizes.cap - 16 : sizes.cap, :].astype(F32)
        run_at[2 * source] = tail[15, 0].astype(I32)
        run_at[2 * source + 1] = tail[15, LANES].astype(I32)
    lane = iota((rows, LANES), 1)
    nothing = jnp.zeros((sizes.rest, 2 * LANES), BF16)
    for source in range(sizes.ctx):
        block = []
        for peer in range(source * sizes.ch, (source + 1) * sizes.ch):
            block += [recv_ref[peer], nothing]
        found = dot(back_ref[...], jnp.concatenate(block, axis=0))
        found = found.astype(BF16)
        value = found[:, :LANES]
        turned = pltpu.roll(value, run, 1)
        merged[source, 0] = jnp.where(lane < run, value, turned)
        merged[source, 1] = jnp.where(lane < run, turned, value)
        merged[source, 2] = found[:, LANES:]
        merged[source, 3] = pltpu.roll(found[:, LANES:], run, 1)
    for source in range(sizes.ctx):
        first, second = run_at[2 * source], run_at[2 * source + 1]
        gated[first] = merged[source, 0]
        gated[second] = merged[source, 1]
        weighted[first + 1, :, :run] = merged[source, 2, :, :run]
        weighted[first, :, run:] = merged[source, 3, :, run:]
        weighted[second + 1, :, :run] = merged[source, 3, :, :run]
        weighted[second, :, run:] = merged[source, 2, :, run:]

    modes = states.shape[1]
    group_lane = lax.shift_right_logical(iota((modes, rows), 1), bits(size))
    carried = jnp.zeros((modes, rows), F32)
    leap = leap_ref[...]
    for at in range(runs):
        states[at] = carried
        if at + 1 < runs:
            ends = dot_lanes(table_ref[...], gated[at])
            total = ends[:modes]
            for group in range(1, own):
                piece = ends[group * modes : (group + 1) * modes]
                total = jnp.where(group_lane == group, piece, total)
            carried = carried * leap + total

    seq = run * runs

    def one_group(group, carry):
        at = pl.ds(pl.multiple_of(group * size, size), size)
        left = gated[:, at, :].reshape(runs * size, LANES).T[:run]
        right = jnp.concatenate(
            [
                weighted[1 + lag : 1 + lag + runs, at, :].reshape(runs * size, LANES)
                for lag in range(0, runs, 2)
            ],
            axis=1,
        )
        gram = jnp.concatenate([dot(left, right), jnp.zeros((run, LANES), F32)], axis=1)
        skewed = pltpu.roll(gram, seq + LANES - (run - 1), 1, stride=1, stride_axis=0)
        sums[pl.ds(group, 1), :] = jnp.sum(skewed, axis=0, keepdims=True)[:, :seq]
        return carry

    lax.fori_loop(0, own, one_group, 0, unroll=True)

    each, cap, rest = sizes.each, sizes.cap, sizes.rest
    wide = 2 * modes - 8
    few_lags = LANES // 2 - rest
    pairs = [
        jnp.concatenate([states[run_at[2 * target]], states[run_at[2 * target + 1]]], axis=0)
        for target in range(sizes.ctx)
    ]
    front = dot(jnp.concatenate(pairs, axis=0).astype(BF16), back_ref[...])
    out_lane = iota((8, LANES), 1)
    for target in range(sizes.ctx):
        lags = sums[:, target * LANES : (target + 1) * LANES]
        moves = [(cap, cap - rest), (LANES - few_lags - 2 * rest, LANES - 2 * few_lags - 2 * rest)]
        moved = [[pltpu.roll(lags, shift % LANES, 1) for shift in pair] for pair in moves]
        for chan in range(sizes.ch):
            at = slice(chan * LANES, (chan + 1) * LANES)
            mine = slice(chan * each, (chan + 1) * each)
            most, few = [jnp.concatenate([part[mine] for part in pair], axis=0) for pair in moved]
            head = front[target * 2 * modes : target * 2 * modes + wide, at]
            last = front[target * 2 * modes + wide : (target + 1) * 2 * modes, at]
            third = pltpu.roll(last, cap - rest, 1)
            beside = [
                pltpu.roll(last, cap, 1),
                jnp.where(out_lane < LANES - few_lags, third, few),
                most,
            ]
            out_ref[target * sizes.ch + chan] = jnp.concatenate(
                [
                    jnp.where(out_lane < cap, head[8 * row : 8 * row + 8], beside[row])
                    for row in range(3)
                ],
                axis=0,
            ).astype(BF16)


def owner(sizes, recv, back, table, leap):
    rows = sizes.own * sizes.size
    modes = leap.shape[0]
    return pl.pallas_call(
        functools.partial(owner_kernel, sizes),
        in_specs=[pl.BlockSpec(memory_space=pltpu.VMEM)] * 4,
        out_shape=jax.ShapeDtypeStruct((sizes.peers, 2 * modes - 8, LANES), BF16),
        scratch_shapes=[
            pltpu.VMEM((sizes.ctx, 4, rows, LANES), BF16),
            pltpu.VMEM((sizes.runs, rows, LANES), BF16),
            pltpu.VMEM((2 * sizes.runs + 1, rows, LANES), BF16),
            pltpu.VMEM((sizes.runs, modes, rows), F32),
            pltpu.VMEM((sizes.own, sizes.run * sizes.runs), F32),
            pltpu.SMEM((sizes.runs,), I32),
        ],
        compiler_params=pltpu.CompilerParams(vmem_limit_bytes=VMEM_LIMIT),
        name="owner_sums",
    )(recv, back, table, leap)


def finish_kernel(
    sizes,
    recv_ref,
    dest_ref,
    conv_ref,
    decay_ref,
    query_ref,
    out_hbm,
    grad_ref,
    found,
    total,
    out_ref,
    left,
):
    blocks = sizes.channels // LANES
    wide = recv_ref.shape[1]
    rows = wide + 8
    modes = rows // 2
    cap, rest = sizes.cap, sizes.rest
    halves = sizes.peers // 2
    both = recv_ref[...].reshape(halves, 2, wide, LANES)
    both = jnp.concatenate([both[:, 0], both[:, 1]], axis=2)
    front = both.reshape(halves * wide, 2 * LANES)
    second = both[:, :8].astype(F32).reshape(halves * 8, 2 * LANES).astype(BF16)
    third = both[:, 8:16].astype(F32).reshape(halves * 8, 2 * LANES).astype(BF16)

    def fetch(part):
        at = pl.ds(part * 256, 256)
        owner, slot = dest_ref[1:2, at], dest_ref[2:3, at]
        half, offset = lax.shift_right_logical(owner, 1), (owner & 1) * LANES
        in_second = jnp.where(slot < rest, slot + cap + offset, -1)
        in_third = jnp.where(slot >= rest, slot + cap - rest + offset, -1)
        most = dot(front, hot_at(2 * LANES, slot + offset))
        few = dot(second, hot_at(2 * LANES, in_second)) + dot(third, hot_at(2 * LANES, in_third))
        mine = [jnp.zeros((wide, 256), F32), jnp.zeros((8, 256), F32)]
        for peer in range(halves):
            mine[0] = mine[0] + jnp.where(half == peer, most[peer * wide : (peer + 1) * wide], 0.0)
            mine[1] = mine[1] + jnp.where(half == peer, few[peer * 8 : (peer + 1) * 8], 0.0)
        for side in range(2):
            start = (2 * part + side) * rows
            for piece, first in zip(mine, (0, wide)):
                found[pl.ds(start + first, piece.shape[0]), :] = piece[
                    :, side * LANES : (side + 1) * LANES
                ]

    def turn(block):
        at = pl.ds(block * LANES, LANES)
        conv = total[pl.ds(block, sizes.tokens, stride=blocks), :].astype(BF16).T
        out_ref[at, :] = (query_ref[at, :].astype(F32) * conv.astype(F32)).astype(BF16)

    copies = []
    for first in range(0, blocks, 8):
        for part in range(first // 2, first // 2 + 4):
            fetch(part)
        decays = [
            decay_ref[mode * blocks + first : mode * blocks + first + 8, :]
            for mode in range(modes)
        ]
        for half in range(2):
            states = [
                found[pl.ds(first * rows + half * modes + mode, 8, stride=rows), :]
                for mode in range(modes)
            ]

            def step(token, states):
                at = (half * sizes.run + token) * blocks + first
                at = pl.ds(pl.multiple_of(at, 8), 8)
                states = [a * s for a, s in zip(decays, states)]
                total[at, :] = conv_ref[at, :] + tree_sum(states)
                return states

            lax.fori_loop(0, sizes.run, step, states, unroll=True)
        for block in range(first, first + 8):
            turn(block)
        at = pl.ds(first * LANES, 8 * LANES)
        copies.append(
            pltpu.make_async_copy(out_ref.at[at], out_hbm.at[at], left.at[first // 8])
        )
        copies[-1].start()

    each, few_lags = sizes.each, LANES // 2 - rest
    shape = (sizes.peers * 8, LANES)
    upper = lax.shift_right_logical(iota(shape, 0) & 7, bits(each)) == 1
    lane = iota(shape, 1)
    placed = jnp.zeros(shape, F32)
    for rows_at, count, come, go in ((16, rest, cap, 0), (8, few_lags, LANES - few_lags, 2 * rest)):
        piece = recv_ref[:, rows_at : rows_at + 8, :].astype(F32).reshape(shape)
        for part in range(2):
            start = go + part * count
            moved = pltpu.roll(piece, (start - come) % LANES, 1)
            here = (upper == (part == 1)) & (lane >= start) & (lane < start + count)
            placed = jnp.where(here, moved, placed)
    come = iota((1, sizes.peers * 8), 1)
    seat = lax.shift_right_logical(come, 3) * each + (come & (each - 1))
    wanted = sizes.group_at(seat, way_of(dest_ref))
    chosen = hot(iota((sizes.block, sizes.peers * 8), 0) == wanted)
    grad_ref[...] = dot(chosen, placed.astype(BF16))
    for copy in copies:
        copy.wait()


def finish(sizes, recv, dest, conv, decay, query_proj):
    blocks = sizes.channels // LANES
    return pl.pallas_call(
        functools.partial(finish_kernel, sizes),
        in_specs=[pl.BlockSpec(memory_space=pltpu.VMEM)] * 5,
        out_specs=[
            pl.BlockSpec(memory_space=pltpu.HBM),
            pl.BlockSpec(memory_space=pltpu.VMEM),
        ],
        out_shape=[
            jax.ShapeDtypeStruct((sizes.channels, sizes.tokens), BF16),
            jax.ShapeDtypeStruct((sizes.block, LANES), F32),
        ],
        scratch_shapes=[
            pltpu.VMEM(((blocks + 1) * (recv.shape[1] + 8), LANES), F32),
            pltpu.VMEM(((sizes.tokens + 1) * blocks, LANES), F32),
            pltpu.VMEM(query_proj.shape, BF16),
            pltpu.SemaphoreType.DMA((blocks // 8,)),
        ],
        compiler_params=pltpu.CompilerParams(vmem_limit_bytes=VMEM_LIMIT),
        name="finish_rows",
    )(recv, dest, conv, decay, query_proj)


def exchange(blocks):
    return lax.all_to_all(blocks, ("ctx", "ch"), split_axis=0, concat_axis=0, tiled=True)


def owners_way(sizes, args):
    query_proj, key_proj, value_proj, cotangent, positions, group_of, decay_rates, residues = args
    me = (lax.axis_index("ctx") * sizes.ch + lax.axis_index("ch")).reshape(1).astype(I32)
    groups = group_of.reshape(1, -1)
    sent, dest = pack(sizes, positions, groups, key_proj, value_proj, cotangent, query_proj)
    recv = exchange(sent)

    gains = residues * jnp.sqrt(2.0 * decay_rates)
    params = jnp.concatenate([decay_rates, gains], axis=1).T
    conv, decay = local(sizes, me, groups, params, key_proj, value_proj)
    back, most, table, leap = index(sizes, me, groups, dest, params)

    def fast(recv, back, table, leap, dest, conv, decay, *args):
        returned = exchange(owner(sizes, recv, back, table, leap))
        return tuple(finish(sizes, returned, dest, conv, decay, args[0]))

    def slow(recv, back, table, leap, dest, conv, decay, *args):
        return general_way(*args)

    return lax.cond(
        most[0, 0] <= sizes.cap - 1,
        fast,
        slow,
        recv,
        back,
        table,
        leap,
        dest,
        conv,
        decay,
        *args,
    )


def shards(*args):
    sizes = Sizes(
        lax.axis_size("ctx"), lax.axis_size("ch"), *args[0].shape, args[6].shape[0]
    )
    if not sizes.fits:
        return general_way(*args)
    return owners_way(sizes, args)


def solution(mesh):
    placed = (
        P("ch", "ctx"),
        P("ch", "ctx"),
        P("ch", "ctx"),
        P("ch", "ctx"),
        P("ctx"),
        P(),
        P(),
        P(),
    )
    return jax.shard_map(
        shards,
        mesh=mesh,
        in_specs=placed,
        out_specs=(P("ch", "ctx"), P("ch", "ctx")),
        check_vma=False,
    )
```
